32 devices in a mesh: seq: 8 (over z, x), freq: 4 (over y, core).
Axes of the slice: x: 2, y: 2, z: 4, core: 2. Of those that a mesh axis runs over, the one named last changes fastest.
Arguments:
- tokens: bfloat16 [8, 3072, 768], P('seq', 'freq'), may hold values from -6 to 6
- freq_ids: int32 [8, 3072], P('seq', 'freq'), may hold values from 0 to 11, as said below
- clip_ids: int32 [8, 3072], P('seq'), may hold values from 0 to 7, as said below
- cotangent: bfloat16 [8, 3072, 768], P('seq', 'freq'), may hold values from -6 to 6
- ln1_gain: bfloat16 [768], P(('seq', 'freq')), may hold values from 0.25 to 1.75
- first_norm_bias: bfloat16 [768], P(('seq', 'freq')), may hold values from -1.75 to 1.75
- qkv_weight: bfloat16 [768, 2304], P(('seq', 'freq')), may hold values from -0.3125 to 0.3125
- q_bias: bfloat16 [768], P(('seq', 'freq')), may hold values from -3 to 3
- v_bias: bfloat16 [768], P(('seq', 'freq')), may hold values from -3 to 3
- out_weight: bfloat16 [768, 768], P(('seq', 'freq')), may hold values from -0.875 to 0.875
- out_bias: bfloat16 [768], P(('seq', 'freq')), may hold values from -1.75 to 1.75
- ln2_gain: bfloat16 [768], P(('seq', 'freq')), may hold values from 0.25 to 1.75
- ln2_bias: bfloat16 [768], P(('seq', 'freq')), may hold values from -1.75 to 1.75
- up_weight: bfloat16 [768, 3072], P(('seq', 'freq')), may hold values from -0.21875 to 0.21875
- up_bias: bfloat16 [3072], P(('seq', 'freq')), may hold values from -3 to 3
- down_weight: bfloat16 [3072, 768], P(('seq', 'freq')), may hold values from -0.21875 to 0.21875
- down_bias: bfloat16 [768], P(('seq', 'freq')), may hold values from -1.75 to 1.75
- freq_table: bfloat16 [768, 12], P(('seq', 'freq')), may hold values from -3 to 3
Outputs:
- mixed: bfloat16 [8, 3072, 768], P('seq', 'freq')
- input_grad: bfloat16 [8, 3072, 768], P('seq', 'freq')
- grad_ln1_gain: float32 [768], P(('seq', 'freq'))
- grad_ln1_bias: float32 [768], P(('seq', 'freq'))
- grad_qkv_weight: float32 [768, 2304], P(('seq', 'freq'))
- grad_q_bias: float32 [768], P(('seq', 'freq'))
- grad_v_bias: float32 [768], P(('seq', 'freq'))
- grad_out_weight: float32 [768, 768], P(('seq', 'freq'))
- grad_out_bias: float32 [768], P(('seq', 'freq'))
- grad_ln2_gain: float32 [768], P(('seq', 'freq'))
- grad_ln2_bias: float32 [768], P(('seq', 'freq'))
- grad_up_weight: float32 [768, 3072], P(('seq', 'freq'))
- grad_up_bias: float32 [3072], P(('seq', 'freq'))
- grad_down_weight: float32 [3072, 768], P(('seq', 'freq'))
- grad_down_bias: float32 [768], P(('seq', 'freq'))
- grad_freq_table: float32 [768, 12], P(('seq', 'freq'))
The draws below stay inside these ranges and needn't reach their ends.
Inputs may be any that keep to these rules, and one draw needn't show every extreme that they name: `clip_ids`: within each of the 4 aligned groups of 768 positions of a sequence, clip ids never fall and every clip 0 to 7 occurs. `freq_ids`: positions in the k-th aligned group of 768 positions of a sequence have frequency rows k * (3) to (k + 1) * 3 - 1.
All inputs are finite; a program needn't handle non-finite values.
Results may differ from the reference program's by a relative error of at most 0.015.
Values may be sent and summed in bfloat16 or wider, within the bound.
No kernel may reach another device: no remote copies, remote signals or barrier semaphores. Data moves between devices by JAX's collectives and lax.ppermute only.
A program may use at most 512 MiB of HBM per device.

```python
import math
import jax
import jax.numpy as jnp
from jax import lax

D = 768
HEADS = 12
HEAD_DIM = 64
FF = 3072
FREQS = 12
LEN = 3072
CLIPS = 8
SEQ_DEV = 1
SEQS = 8
GROUP_LEN = 768
N_SEQ = 8
N_FREQ = 4


def draw_clip_ids(key, part):
    key = jax.random.fold_in(key, 11)
    extras = jax.random.randint(key, (SEQS, N_FREQ, GROUP_LEN - CLIPS), 0, CLIPS)
    present = jnp.broadcast_to(jnp.arange(CLIPS, dtype=jnp.int32), (SEQS, N_FREQ, CLIPS))
    joined = jnp.sort(jnp.concatenate([present, extras.astype(jnp.int32)], axis=2), axis=2)
    return joined.reshape(SEQS, LEN).astype(jnp.int32)


def draw_freq_ids(key, part):
    key = jax.random.fold_in(key, 23)
    per_group = FREQS // N_FREQ
    inner_rows = jax.random.randint(key, (SEQS, N_FREQ, GROUP_LEN), 0, per_group).astype(jnp.int32)
    inner_rows = inner_rows.at[:, :, 0].set(per_group - 1)
    offsets = (jnp.arange(N_FREQ, dtype=jnp.int32) * per_group)[None, :, None]
    return (inner_rows + offsets).reshape(SEQS, LEN).astype(jnp.int32)


def shard_levels(key, dims, pieces, least, high):
    level = 1.0
    for position, blocks in pieces:
        steps = jax.random.uniform(jax.random.fold_in(jax.random.fold_in(key, 6), position), (blocks,), jnp.float32, least / len(pieces), high / len(pieces))
        level = level * jnp.repeat(jnp.exp(steps), dims[position] // blocks).reshape((-1,) + (1,) * (len(dims) - 1 - position))
    return level


def scatter_about(key, shape, deviation, limit, split=(), kind=jnp.bfloat16):
    drawn = jax.random.normal(key, shape, jnp.float32) * deviation
    if len(split) > 0:
        drawn = shard_levels(key, shape, split, -0.22, 0.18) * drawn
    return jnp.clip(drawn, min=-limit, max=limit).astype(kind)


def setup_inputs(seed: int = 0) -> dict:
    streams_of = jax.random.split(jax.random.key(seed), 19)
    tokens = scatter_about(streams_of[0], (SEQS, LEN, D), 1.0, 6.0, ((0, 8), (1, 4)))
    freq_ids = draw_freq_ids(jax.random.fold_in(streams_of[18], 71), 0)
    clip_ids = draw_clip_ids(jax.random.fold_in(streams_of[18], 71), 0)
    cotangent = scatter_about(streams_of[3], (SEQS, LEN, D), 1.0, 6.0, ((0, 8), (1, 4)))
    ln1_gain = jnp.clip(1.0 + 0.15 * jax.random.normal(streams_of[4], (D,), jnp.float32), 0.25, 1.75).astype(jnp.bfloat16)
    first_norm_bias = scatter_about(streams_of[5], (D,), 0.3, 1.75, ((0, 32),))
    qkv_weight = scatter_about(streams_of[6], (D, 3 * D), (D // 2) ** -0.5, 0.3125, ((0, 32),))
    q_bias = scatter_about(streams_of[7], (D,), 0.5, 3.0, ((0, 32),))
    v_bias = scatter_about(streams_of[8], (D,), 0.5, 3.0, ((0, 32),))
    out_weight = scatter_about(streams_of[9], (D, D), (D // 16) ** -0.5, 0.875, ((0, 32),))
    out_bias = scatter_about(streams_of[10], (D,), 0.3, 1.75, ((0, 32),))
    ln2_gain = jnp.clip(1.0 + 0.15 * jax.random.normal(streams_of[11], (D,), jnp.float32), 0.25, 1.75).astype(jnp.bfloat16)
    ln2_bias = scatter_about(streams_of[12], (D,), 0.3, 1.75, ((0, 32),))
    up_weight = scatter_about(streams_of[13], (D, FF), D ** -0.5, 0.21875, ((0, 32),))
    up_bias = scatter_about(streams_of[14], (FF,), 0.5, 3.0, ((0, 32),))
    down_weight = scatter_about(streams_of[15], (FF, D), (FF // 4) ** -0.5, 0.21875, ((0, 32),))
    down_bias = scatter_about(streams_of[16], (D,), 0.3, 1.75, ((0, 32),))
    freq_table = scatter_about(streams_of[17], (D, FREQS), 0.5, 3.0, ((0, 32),))
    return dict(tokens=tokens, freq_ids=freq_ids, clip_ids=clip_ids, cotangent=cotangent, ln1_gain=ln1_gain, first_norm_bias=first_norm_bias, qkv_weight=qkv_weight, q_bias=q_bias, v_bias=v_bias, out_weight=out_weight, out_bias=out_bias, ln2_gain=ln2_gain, ln2_bias=ln2_bias, up_weight=up_weight, up_bias=up_bias, down_weight=down_weight, down_bias=down_bias, freq_table=freq_table)


@jax.custom_vjp
def low(v):
    return lax.optimization_barrier(v.astype(jnp.bfloat16)).astype(jnp.float32)

@jax.custom_vjp
def low_back(v):
    return v

def low_keep(v):
    return (low(v), None)

def low_pass(kept, grad):
    return (grad,)

def back_keep(v):
    return (v, None)

def back_low(kept, grad):
    return (low(grad),)
low.defvjp(low_keep, low_pass)
low_back.defvjp(back_keep, back_low)
epsilon = 1e-06
masked_score = -1e+30

def layer_norm(values, gain_vec, shift_vec):
    center = values - lax.optimization_barrier(jnp.mean(values, axis=-1, keepdims=True))
    spread = lax.optimization_barrier(jnp.mean(center * center, axis=-1, keepdims=True))
    return center * lax.rsqrt(spread + epsilon) * gain_vec + shift_vec

def forward(inputs, params, freq_rows, clip_rows):
    ln1_gain, first_norm_bias, qkv_weight, q_bias, v_bias, out_weight, out_bias, ln2_gain, ln2_bias, up_weight, up_bias, down_weight, down_bias, freq_table = params
    highest_precision_flag = lax.Precision.HIGHEST
    batch = inputs.shape[0]
    onehot = (freq_rows[..., None] == jnp.arange(FREQS, dtype=jnp.int32)).astype(jnp.float32)
    hidden = inputs + jnp.einsum('blr,dr->bld', onehot, freq_table, precision=highest_precision_flag)
    normed = low(layer_norm(hidden, ln1_gain, first_norm_bias))
    projected = jnp.einsum('bld,de->ble', normed, qkv_weight, precision=highest_precision_flag)
    queries = low_back(low(projected[..., :D] + q_bias))
    keys_all = low_back(low(projected[..., D:2 * D]))
    values_all = low_back(low(projected[..., 2 * D:] + v_bias))
    query_heads = jnp.moveaxis(queries.reshape(batch, LEN, HEADS, HEAD_DIM), 2, 0)
    key_heads = jnp.moveaxis(keys_all.reshape(batch, LEN, HEADS, HEAD_DIM), 2, 0)
    value_heads = jnp.moveaxis(values_all.reshape(batch, LEN, HEADS, HEAD_DIM), 2, 0)
    same_clip = clip_rows[:, :, None] == clip_rows[:, None, :]

    def head_block(parts):
        single_query_block, single_key_block, single_value_block = parts
        unscaled_scores = jnp.einsum('rty,rvy->rtv', single_query_block, single_key_block, precision=highest_precision_flag)
        scaled = low_back(unscaled_scores * (1.0 / math.sqrt(HEAD_DIM)))
        scores = jnp.where(same_clip, scaled, masked_score)
        attention_probability_map = low(jax.nn.softmax(scores, axis=-1))
        return jnp.einsum('naj,njv->nav', attention_probability_map, single_value_block, precision=highest_precision_flag)
    context_heads = lax.map(jax.checkpoint(head_block), (query_heads, key_heads, value_heads))
    context = jnp.moveaxis(context_heads, 0, 2).reshape(batch, LEN, D)
    context = low_back(low(context))
    branch = low_back(jnp.einsum('bld,de->ble', context, out_weight, precision=highest_precision_flag))
    middle = hidden + branch + out_bias
    second = low(layer_norm(middle, ln2_gain, ln2_bias))
    upward = low_back(jnp.einsum('bld,df->blf', second, up_weight, precision=highest_precision_flag) + up_bias)
    activated = low(jax.nn.gelu(upward, approximate=False))
    lowered = jnp.einsum('blf,fd->bld', activated, down_weight, precision=highest_precision_flag)
    return middle + lowered + down_bias

def reference(tokens, freq_ids, clip_ids, cotangent, ln1_gain, first_norm_bias, qkv_weight, q_bias, v_bias, out_weight, out_bias, ln2_gain, ln2_bias, up_weight, up_bias, down_weight, down_bias, freq_table):
    params = tuple((entry.astype(jnp.float32) for entry in (ln1_gain, first_norm_bias, qkv_weight, q_bias, v_bias, out_weight, out_bias, ln2_gain, ln2_bias, up_weight, up_bias, down_weight, down_bias, freq_table)))
    token_groups = tokens.astype(jnp.float32).reshape(N_SEQ, SEQ_DEV, LEN, D)
    freq_groups = freq_ids.reshape(N_SEQ, SEQ_DEV, LEN)
    clip_groups = clip_ids.reshape(N_SEQ, SEQ_DEV, LEN)
    grad_groups = cotangent.astype(jnp.float32).reshape(N_SEQ, SEQ_DEV, LEN, D)

    def step(carry, batch_items):
        inputs, freq_rows, clip_rows, upstream = batch_items

        def apply(layer_in, layer_params):
            return forward(layer_in, layer_params, freq_rows, clip_rows)
        outputs, pull = jax.vjp(apply, inputs, params)
        grad_in, grad_params = pull(upstream)
        carry = jax.tree.map(jnp.add, carry, grad_params)
        return (carry, (outputs.astype(jnp.bfloat16), grad_in.astype(jnp.bfloat16)))
    zeros = tuple((jnp.zeros_like(entry) for entry in params))
    sums, (outputs, incoming_gradient_list) = lax.scan(step, zeros, (token_groups, freq_groups, clip_groups, grad_groups))
    mixed = outputs.reshape(SEQS, LEN, D)
    input_grad = incoming_gradient_list.reshape(SEQS, LEN, D)
    return (mixed, input_grad, sums[0], sums[1], sums[2], sums[3], sums[4], sums[5], sums[6], sums[7], sums[8], sums[9], sums[10], sums[11], sums[12], sums[13])
```

```python
import functools

import jax
import jax.numpy as jnp
import numpy as np
from jax import lax
from jax.experimental import pallas as pl
from jax.experimental.pallas import tpu as pltpu
from jax.sharding import PartitionSpec as P

HEADS = 12
HEAD_DIM = 64
FREQS = 12
CLIPS = 8
WIN = 128
CHIPS = 16
EPS = 1e-06
MASKED = -1e30
BOTH = ("seq", "freq")
F32 = jnp.float32
BF16 = jnp.bfloat16
VMEM_LIMIT = 60 * 1024 * 1024


def params(**kw):
    return pltpu.CompilerParams(vmem_limit_bytes=VMEM_LIMIT, **kw)


def whole():
    return pl.BlockSpec(memory_space=pltpu.VMEM)


def smem():
    return pl.BlockSpec(memory_space=pltpu.SMEM)


def hbm():
    return pl.BlockSpec(memory_space=pl.ANY)


def once(shape):
    return pl.BlockSpec(shape, lambda *_: (0,) * len(shape), pipeline_mode=pl.Buffered(1))


def mm(a, b):
    return jnp.dot(a, b, preferred_element_type=F32)


def mm_nt(a, b):
    return lax.dot_general(a, b, (((1,), (1,)), ((), ())), preferred_element_type=F32)


def mm_tn(a, b):
    return lax.dot_general(a, b, (((0,), (0,)), ((), ())), preferred_element_type=F32)


def norm_stats(values):
    center = values - jnp.mean(values, axis=-1, keepdims=True)
    spread = jnp.mean(center * center, axis=-1, keepdims=True)
    inv = lax.rsqrt(spread + EPS)
    return center * inv, inv


def norm_back(vhat, inv, dy, gain):
    gd = dy * gain
    return inv * (
        gd
        - jnp.mean(gd, axis=-1, keepdims=True)
        - vhat * jnp.mean(gd * vhat, axis=-1, keepdims=True)
    )


def row_sum(values):
    return jnp.sum(values, axis=0, keepdims=True)


def embed(tokens, ids, ptab):
    hot = (lax.broadcasted_iota(jnp.int32, (16, ids.shape[1]), 0) == ids).astype(BF16)
    return tokens.astype(F32) + mm_tn(hot, ptab[16:32, :].astype(BF16)), hot


def qkv_kernel(
    tab, t0, t1, t2, t3, ids, own, oth, normed, keys, values, queries, hidden, weight, ptab,
    pm, sems, *, rows
):
    step = pl.program_id(0)
    feature = weight.shape[0]
    block = feature // CHIPS
    seg = feature // 2
    core = tab[4, 0]

    def copies(cc):
        made = []
        for r in range(CHIPS):
            for half, ref in ((cc, own), (1 - cc, oth)):
                dst = pl.multiple_of(tab[0 if half == cc else 1, r] * block, 16)
                for n in range(3):
                    made.append(
                        pltpu.make_async_copy(
                            ref.at[pl.ds(r * block, block), pl.ds(n * seg, seg)],
                            weight.at[
                                pl.ds(dst, block), pl.ds(n * feature + half * seg, seg)
                            ],
                            sems.at[len(made)],
                        )
                    )
            made.append(
                pltpu.make_async_copy(
                    own.at[pl.ds(r * block, block), pl.ds(3 * seg, 128)],
                    pm.at[pl.ds(pl.multiple_of(tab[0, r] * block, 16), block), :],
                    sems.at[len(made)],
                )
            )
        return made

    @pl.when(step == 0)
    def _():
        for cc in (0, 1):

            @pl.when(core == cc)
            def _():
                made = copies(cc)
                for one in made:
                    one.start()
                for one in made:
                    one.wait()

        ptab[...] = pm[...].astype(F32).T[:32, :]

    per = keys.shape[0]
    tiles = t0.shape[0]
    steps = 768 // per
    del tiles

    def body(tok, own_rows):
        value, _ = embed(tok[...], ids[0], ptab)
        vhat, _ = norm_stats(value)
        low = (vhat * ptab[0:1, :] + ptab[1:2, :]).astype(BF16)
        normed[...] = low
        if own_rows:
            hidden[...] = value
            q = mm(low, weight[:, 0:feature]) + ptab[2:3, :]
            queries[...] = q.astype(BF16) * jnp.asarray(HEAD_DIM**-0.5, BF16)
        keys[...] = mm(low, weight[:, feature : 2 * feature]).astype(BF16)
        values[...] = (mm(low, weight[:, 2 * feature :]) + ptab[3:4, :]).astype(BF16)

    for piece, tok in enumerate((t0, t1, t2, t3)):

        @pl.when((step >= piece * steps) & (step < (piece + 1) * steps))
        def _():
            body(tok, piece == 0)


def qkv_call(tab, pieces, ids, own, oth):
    group, feature = pieces[0].shape
    per = 256
    steps = group // per
    total = 4 * steps

    def at(piece):
        return pl.BlockSpec(
            (per, feature), lambda i: (jnp.clip(i - piece * steps, 0, steps - 1), 0)
        )

    tile = pl.BlockSpec((per, feature), lambda i: (i, 0))
    first = pl.BlockSpec((per, feature), lambda i: (jnp.minimum(i, steps - 1), 0))
    return pl.pallas_call(
        functools.partial(qkv_kernel, rows=per),
        grid=(total,),
        in_specs=[smem()]
        + [at(p) for p in range(4)]
        + [pl.BlockSpec((1, 1, per), lambda i: (i, 0, 0)), hbm(), hbm()],
        out_specs=[tile, tile, tile, first, first, once((feature, 3 * feature)), once((32, feature))],
        out_shape=[
            jax.ShapeDtypeStruct((4 * group, feature), BF16),
            jax.ShapeDtypeStruct((4 * group, feature), BF16),
            jax.ShapeDtypeStruct((4 * group, feature), BF16),
            jax.ShapeDtypeStruct((group, feature), BF16),
            jax.ShapeDtypeStruct((group, feature), F32),
            jax.ShapeDtypeStruct((feature, 3 * feature), BF16),
            jax.ShapeDtypeStruct((32, feature), F32),
        ],
        scratch_shapes=[
            pltpu.VMEM((feature, 128), BF16),
            pltpu.SemaphoreType.DMA((7 * CHIPS,)),
        ],
        compiler_params=params(),
        cost_estimate=pl.CostEstimate(
            flops=2 * group * feature * feature * 9, bytes_accessed=30_000_000, transcendentals=0
        ),
        name="qkv",
    )(tab, *pieces, ids.reshape(total, 1, per), own, oth)


def window(starts, g, clip, n, group):
    first = starts[g * 16 + clip]
    last = starts[g * 16 + clip + 1]
    lead = (first // 16) * 16 + n * WIN
    base = pl.multiple_of(jnp.minimum(lead, group - WIN), 16)
    return base, jnp.maximum(first, lead) - base, last - base


def counts(starts, clip, groups):
    def need(g):
        first = (starts[g * 16 + clip] // 16) * 16
        return (starts[g * 16 + clip + 1] - first + WIN - 1) // WIN

    spans = [need(g) for g in groups]
    most = spans[0]
    for s in spans[1:]:
        most = jnp.maximum(most, s)
    return most


def lane_halves():
    lane = lax.broadcasted_iota(jnp.int32, (1, 128), 1)
    left = (lane < HEAD_DIM).astype(BF16)
    return left, 1 - left


def stack_heads(rows):
    left, right = lane_halves()
    return jnp.concatenate([rows * left, rows * right], axis=0)


def merge_heads(stacked):
    lane = lax.broadcasted_iota(jnp.int32, (WIN, 128), 1)
    return jnp.where(lane < HEAD_DIM, stacked[:WIN], stacked[WIN:])


def row_valid(lo, hi):
    row = lax.broadcasted_iota(jnp.int32, (WIN, 128), 0)
    return (row >= lo) & (row < hi)


def load_keys(starts, clip, n, group, *refs):
    tiles = [[] for _ in refs]
    spans = []
    for g in range(4):
        base, lo, hi = window(starts, g, clip, n, group)
        for t, ref in zip(tiles, refs):
            t.append(ref[pl.ds(pl.multiple_of(g * group + base, 16), WIN), :])
        spans.append((base, lo, hi))
    return [jnp.concatenate(t, axis=0) for t in tiles], spans


def key_bias_row(spans):
    lane = lax.broadcasted_iota(jnp.int32, (1, WIN), 1)
    return jnp.concatenate(
        [jnp.where((lane >= lo) & (lane < hi), 0.0, MASKED) for _, lo, hi in spans], axis=1
    )


def key_bias_col(spans):
    row = lax.broadcasted_iota(jnp.int32, (WIN, 2 * WIN), 0)
    return jnp.concatenate(
        [jnp.where((row >= lo) & (row < hi), 0.0, MASKED) for _, lo, hi in spans], axis=0
    )


def attn_kernel(starts, q, k, v, out, *, group):
    def one(clip):
        base, lo, hi = window(starts, 0, clip, 0, group)
        stacked = stack_heads(q[pl.ds(base, WIN), :])
        (kt, vt), spans = load_keys(starts, clip, 0, group, k, v)
        scores = mm_nt(stacked, kt) + key_bias_row(spans)
        peak = jnp.max(scores, axis=1, keepdims=True)
        e = jnp.exp(scores - peak)
        total = jnp.sum(e, axis=1, keepdims=True)
        o = mm(e.astype(BF16), vt) * (1.0 / total)
        spot = pl.ds(base, WIN)
        out[spot, :] = jnp.where(row_valid(lo, hi), merge_heads(o).astype(BF16), out[spot, :])

    def many(clip, rows, steps):
        @pl.loop(0, rows)
        def _(i):
            base, lo, hi = window(starts, 0, clip, i, group)
            stacked = stack_heads(q[pl.ds(base, WIN), :])

            def inner(j, carry):
                peak, total, acc = carry
                (kt, vt), spans = load_keys(starts, clip, j, group, k, v)
                scores = mm_nt(stacked, kt) + key_bias_row(spans)
                new = jnp.maximum(peak, jnp.max(scores, axis=1, keepdims=True))
                e = jnp.exp(scores - new)
                shrink = jnp.exp(peak - new)
                return (
                    new,
                    total * shrink + jnp.sum(e, axis=1, keepdims=True),
                    acc * shrink + mm(e.astype(BF16), vt),
                )

            start = (
                jnp.full((2 * WIN, 1), 2 * MASKED, F32),
                jnp.zeros((2 * WIN, 1), F32),
                jnp.zeros((2 * WIN, 128), F32),
            )
            _, total, acc = lax.fori_loop(0, steps, inner, start)
            o = merge_heads(acc * (1.0 / total)).astype(BF16)
            spot = pl.ds(base, WIN)
            out[spot, :] = jnp.where(row_valid(lo, hi), o, out[spot, :])

    most = counts(starts, 0, range(4))
    for clip in range(1, CLIPS):
        most = jnp.maximum(most, counts(starts, clip, range(4)))

    @pl.when(most <= 1)
    def _():
        for clip in range(CLIPS):
            one(clip)

    @pl.when(most > 1)
    def _():
        @pl.loop(0, CLIPS)
        def _(clip):
            many(clip, counts(starts, clip, [0]), counts(starts, clip, range(4)))


def attn_call(starts, queries, keys, values):
    group, feature = queries.shape
    return pl.pallas_call(
        functools.partial(attn_kernel, group=group),
        grid=(feature // 128,),
        in_specs=[
            smem(),
            pl.BlockSpec((group, 128), lambda i: (0, i)),
            pl.BlockSpec((4 * group, 128), lambda i: (0, i)),
            pl.BlockSpec((4 * group, 128), lambda i: (0, i)),
        ],
        out_specs=pl.BlockSpec((group, 128), lambda i: (0, i)),
        out_shape=jax.ShapeDtypeStruct((group, feature), BF16),
        compiler_params=params(),
        cost_estimate=pl.CostEstimate(
            flops=10_000_000_000, bytes_accessed=12_000_000, transcendentals=6_300_000
        ),
        name="attention",
    )(starts, queries, keys, values)


def attn_back_kernel(starts, q, k, v, go, dq, dk, dv, dk_acc, dv_acc, dq_acc, *, group):
    dk_acc[...] = jnp.zeros_like(dk_acc)
    dv_acc[...] = jnp.zeros_like(dv_acc)
    dq_acc[...] = jnp.zeros_like(dq_acc)
    scale = HEAD_DIM**-0.5

    def load_query(clip, i):
        base, lo, hi = window(starts, 0, clip, i, group)
        spot = pl.ds(base, WIN)
        keep = jnp.where(row_valid(lo, hi), go[spot, :], jnp.zeros((), BF16))
        return base, stack_heads(q[spot, :]), stack_heads(keep)

    def finish(spans, base, kt, stacked, back, prob, ds):
        ds = ds.astype(BF16)
        dvt = mm(prob.astype(BF16), back)
        dkt = mm(ds, stacked)
        for g, (kb, _, _) in enumerate(spans):
            spot = pl.ds(pl.multiple_of(g * group + kb, 16), WIN)
            dk_acc[spot, :] += dkt[g * WIN : (g + 1) * WIN]
            dv_acc[spot, :] += dvt[g * WIN : (g + 1) * WIN]
        spot = pl.ds(base, WIN)
        dq_acc[spot, :] += merge_heads(mm_tn(ds, kt))

    def one(clip):
        base, stacked, back = load_query(clip, 0)
        (kt, vt), spans = load_keys(starts, clip, 0, group, k, v)
        scores = mm_nt(kt, stacked) + key_bias_col(spans)
        peak = jnp.max(scores, axis=0, keepdims=True)
        e = jnp.exp(scores - peak)
        prob = e * (1.0 / jnp.sum(e, axis=0, keepdims=True))
        gp = mm_nt(vt, back)
        inner = jnp.sum(prob * gp, axis=0, keepdims=True)
        finish(spans, base, kt, stacked, back, prob, prob * (gp - inner))

    def many(clip, rows, steps):
        @pl.loop(0, rows)
        def _(i):
            base, stacked, back = load_query(clip, i)

            def totals(j, carry):
                peak, total, inner = carry
                (kt, vt), spans = load_keys(starts, clip, j, group, k, v)
                scores = mm_nt(kt, stacked) + key_bias_col(spans)
                new = jnp.maximum(peak, jnp.max(scores, axis=0, keepdims=True))
                e = jnp.exp(scores - new)
                shrink = jnp.exp(peak - new)
                gp = mm_nt(vt, back)
                return (
                    new,
                    total * shrink + jnp.sum(e, axis=0, keepdims=True),
                    inner * shrink + jnp.sum(e * gp, axis=0, keepdims=True),
                )

            zero = jnp.zeros((1, 2 * WIN), F32)
            peak, total, inner = lax.fori_loop(
                0, steps, totals, (jnp.full((1, 2 * WIN), 2 * MASKED, F32), zero, zero)
            )
            part = 1.0 / total
            inner = inner * part

            @pl.loop(0, steps)
            def _(j):
                (kt, vt), spans = load_keys(starts, clip, j, group, k, v)
                scores = mm_nt(kt, stacked) + key_bias_col(spans)
                prob = jnp.exp(scores - peak) * part
                gp = mm_nt(vt, back)
                finish(spans, base, kt, stacked, back, prob, prob * (gp - inner))

    most = counts(starts, 0, range(4))
    for clip in range(1, CLIPS):
        most = jnp.maximum(most, counts(starts, clip, range(4)))

    @pl.when(most <= 1)
    def _():
        for clip in range(CLIPS):
            one(clip)

    @pl.when(most > 1)
    def _():
        @pl.loop(0, CLIPS)
        def _(clip):
            many(clip, counts(starts, clip, [0]), counts(starts, clip, range(4)))

    dq[...] = (dq_acc[...] * scale).astype(BF16)
    dk[...] = dk_acc[...].astype(BF16)
    dv[...] = dv_acc[...].astype(BF16)


def attn_back_call(starts, queries, keys, values, grad_context):
    group, feature = queries.shape
    small = pl.BlockSpec((group, 128), lambda i: (0, i))
    large = pl.BlockSpec((4 * group, 128), lambda i: (0, i))
    return pl.pallas_call(
        functools.partial(attn_back_kernel, group=group),
        grid=(feature // 128,),
        in_specs=[smem(), small, large, large, small],
        out_specs=[small, large, large],
        out_shape=[
            jax.ShapeDtypeStruct((group, feature), BF16),
            jax.ShapeDtypeStruct((4 * group, feature), BF16),
            jax.ShapeDtypeStruct((4 * group, feature), BF16),
        ],
        scratch_shapes=[
            pltpu.VMEM((4 * group, 128), F32),
            pltpu.VMEM((4 * group, 128), F32),
            pltpu.VMEM((group, 128), F32),
        ],
        compiler_params=params(),
        cost_estimate=pl.CostEstimate(
            flops=20_000_000_000, bytes_accessed=24_000_000, transcendentals=6_300_000
        ),
        name="attention_back",
    )(starts, queries, keys, values, grad_context)


def phi_parts(u):
    x = jnp.abs(u) * (0.5**0.5)
    t = 1.0 / (1.0 + 0.3275911 * x)
    e = jnp.exp(-(x * x))
    poly = t * (
        0.254829592
        + t * (-0.284496736 + t * (1.421413741 + t * (-1.453152027 + t * 1.061405429)))
    )
    tail = 0.5 * poly * e
    return jnp.where(u < 0, tail, 1.0 - tail), e * 0.3989422804014327


def middle_kernel(
    tab, ctx, hidden, ups, ptab, up_bias, uo_own, uo_oth, dn_own, dn_oth,
    mixed, grad_mid, grad_ctx, g_uo_own, g_uo_oth, g_dn_own, g_dn_oth, small, g_up_bias,
    w_up, w_dn, w_out, mid, sec, sec_t, acc, gsec, act, gup, t_up, t_dn, in_sems, up_sems, dn_sems,
    *, chunks
):
    j = pl.program_id(0)
    group, feature = ctx.shape
    block = feature // CHIPS
    dblock = w_dn.shape[0] // CHIPS
    seg = feature // 2
    part = w_dn.shape[0] // chunks
    per_half = chunks // 2
    core = tab[4, 0]
    tile = 256
    tiles = group // tile

    def loads(cc):
        made = []

        def add(src, dst):
            made.append(pltpu.make_async_copy(src, dst, in_sems.at[len(made)]))

        for r in range(CHIPS):
            for half, ref, dref, row in ((cc, uo_own, dn_own, 0), (1 - cc, uo_oth, dn_oth, 1)):
                chip = tab[row, r]
                dst = pl.ds(pl.multiple_of(chip * block, 16), block)
                src = pl.ds(r * block, block)
                add(
                    ref.at[src, pl.ds(per_half * part, seg)],
                    w_out.at[dst, pl.ds(half * seg, seg)],
                )
                for n in range(per_half):
                    add(
                        ref.at[src, pl.ds(n * part, part)],
                        w_up.at[half * per_half + n, dst, :],
                    )
                add(
                    dref.at[pl.ds(r * dblock, dblock), :],
                    w_dn.at[
                        pl.ds(pl.multiple_of(chip * dblock, 16), dblock), pl.ds(half * seg, seg)
                    ],
                )
        return made

    def for_core(run):
        for cc in (0, 1):

            @pl.when(core == cc)
            def _():
                run(cc)

    @pl.when(j == 0)
    def _():
        def run(cc):
            made = loads(cc)
            for one in made:
                one.start()
            for one in made:
                one.wait()

        for_core(run)
        for t in range(tiles):
            rows = slice(t * tile, (t + 1) * tile)
            value = hidden[rows, :] + mm(ctx[rows, :], w_out[...]) + ptab[4:5, :]
            mid[rows, :] = value
            vhat, _ = norm_stats(value)
            low = (vhat * ptab[5:6, :] + ptab[6:7, :]).astype(BF16)
            sec[rows, :] = low
            sec_t[:, rows] = low.T
            acc[rows, :] = value + ptab[7:8, :]
            gsec[rows, :] = jnp.zeros((tile, feature), F32)

    slot = lax.rem(j, 2)

    def up_stores(jj, sl, cc):
        own = (jj // per_half) == cc
        made = []
        for r in range(CHIPS):
            made.append((r, own))
        return made

    def drain(sl):
        for r in range(CHIPS):
            pltpu.make_async_copy(
                t_up.at[sl, pl.ds(0, block), :],
                g_uo_own.at[pl.ds(0, block), pl.ds(0, part)],
                up_sems.at[sl, r],
            ).wait()
        for n in range(2 * (part // dblock)):
            pltpu.make_async_copy(
                t_dn.at[sl, pl.ds(0, dblock), pl.ds(0, seg)],
                g_dn_own.at[pl.ds(0, dblock), :],
                dn_sems.at[sl, n],
            ).wait()

    del up_stores

    upj = w_up[j]
    dnj = w_dn[pl.ds(pl.multiple_of(j * part, 128), part), :]
    bias = up_bias[pl.ds(j, 1), :]
    gub = jnp.zeros((1, part), F32)
    for t in range(tiles):
        rows = slice(t * tile, (t + 1) * tile)
        u = mm(sec[rows, :], upj) + bias
        dist, dens = phi_parts(u)
        a = (u * dist).astype(BF16)
        g = (mm_nt(ups[rows, :], dnj) * (dist + u * dens)).astype(BF16)
        act[rows, :] = a
        gup[rows, :] = g
        gub = gub + row_sum(g.astype(F32))
        acc[rows, :] += mm(a, dnj)
        gsec[rows, :] += mm_nt(g, upj)
    g_up_bias[pl.ds(j, 1), :] = gub

    @pl.when(j >= 2)
    def _():
        drain(slot)

    t_up[slot] = mm(sec_t[...], gup[...]).astype(BF16)
    t_dn[slot] = mm_tn(act[...], ups[...]).astype(BF16)

    def send(cc):
        col = pl.ds(pl.multiple_of(lax.rem(j, per_half) * part, 128), part)
        for is_own in (True, False):
            ref = g_uo_own if is_own else g_uo_oth

            @pl.when((j // per_half == cc) == is_own)
            def _():
                for r in range(CHIPS):
                    src = pl.ds(pl.multiple_of(tab[0 if is_own else 1, r] * block, 16), block)
                    pltpu.make_async_copy(
                        t_up.at[slot, src, :],
                        ref.at[pl.ds(r * block, block), col],
                        up_sems.at[slot, r],
                    ).start()

        n = 0
        count = part // dblock
        for half, ref, row in ((cc, g_dn_own, 2), (1 - cc, g_dn_oth, 3)):
            for i in range(count):
                place = tab[row, j * count + i]
                pltpu.make_async_copy(
                    t_dn.at[slot, pl.ds(i * dblock, dblock), pl.ds(half * seg, seg)],
                    ref.at[pl.ds(pl.multiple_of(place * dblock, 16), dblock), :],
                    dn_sems.at[slot, n],
                ).start()
                n += 1

    for_core(send)

    @pl.when(j == chunks - 1)
    def _():
        s_gain = jnp.zeros((1, feature), F32)
        s_shift = jnp.zeros((1, feature), F32)
        s_out = jnp.zeros((1, feature), F32)
        s_down = jnp.zeros((1, feature), F32)
        for t in range(tiles):
            rows = slice(t * tile, (t + 1) * tile)
            mixed[rows, :] = acc[rows, :].astype(BF16)
            vhat, inv = norm_stats(mid[rows, :])
            dy = gsec[rows, :]
            wide = ups[rows, :].astype(F32)
            gm = wide + norm_back(vhat, inv, dy, ptab[5:6, :])
            grad_mid[rows, :] = gm
            low = gm.astype(BF16)
            gup[rows, :] = low
            grad_ctx[rows, :] = mm_nt(low, w_out[...]).astype(BF16)
            s_gain = s_gain + row_sum(dy * vhat)
            s_shift = s_shift + row_sum(dy)
            s_out = s_out + row_sum(gm)
            s_down = s_down + row_sum(wide)
        zero = jnp.zeros((1, feature), F32)
        small[...] = jnp.concatenate(
            [zero, zero, zero, zero, s_out, s_gain, s_shift, s_down], axis=0
        )
        drain(1 - slot)
        act[...] = mm_tn(ctx[...], gup[...]).astype(BF16)

        def run(cc):
            made = []
            for half, ref, row in ((cc, g_uo_own, 0), (1 - cc, g_uo_oth, 1)):
                for r in range(CHIPS):
                    src = pl.ds(pl.multiple_of(tab[row, r] * block, 16), block)
                    made.append(
                        pltpu.make_async_copy(
                            act.at[src, pl.ds(half * seg, seg)],
                            ref.at[pl.ds(r * block, block), pl.ds(per_half * part, seg)],
                            in_sems.at[len(made)],
                        )
                    )
            for one in made:
                one.start()
            for one in made:
                one.wait()

        for_core(run)
        drain(slot)


def middle_call(tab, ctx, hidden, ups, ptab, up_bias, uo, dn):
    group, feature = ctx.shape
    ff = dn[0].shape[0]
    chunks = ff // feature
    part = ff // chunks
    half_uo = uo[0].shape[1]
    return pl.pallas_call(
        functools.partial(middle_kernel, chunks=chunks),
        grid=(chunks,),
        in_specs=[
            smem(),
            once((group, feature)),
            once((group, feature)),
            once((group, feature)),
            once((32, feature)),
            once((chunks, part)),
            hbm(), hbm(), hbm(), hbm(),
        ],
        out_specs=[
            once((group, feature)),
            once((group, feature)),
            once((group, feature)),
            hbm(), hbm(), hbm(), hbm(),
            once((8, feature)),
            once((chunks, part)),
        ],
        out_shape=[
            jax.ShapeDtypeStruct((group, feature), BF16),
            jax.ShapeDtypeStruct((group, feature), F32),
            jax.ShapeDtypeStruct((group, feature), BF16),
            jax.ShapeDtypeStruct((feature, half_uo), BF16),
            jax.ShapeDtypeStruct((feature, half_uo), BF16),
            jax.ShapeDtypeStruct((ff, feature // 2), BF16),
            jax.ShapeDtypeStruct((ff, feature // 2), BF16),
            jax.ShapeDtypeStruct((8, feature), F32),
            jax.ShapeDtypeStruct((chunks, part), F32),
        ],
        scratch_shapes=[
            pltpu.VMEM((chunks, feature, part), BF16),
            pltpu.VMEM((ff, feature), BF16),
            pltpu.VMEM((feature, feature), BF16),
            pltpu.VMEM((group, feature), F32),
            pltpu.VMEM((group, feature), BF16),
            pltpu.VMEM((feature, group), BF16),
            pltpu.VMEM((group, feature), F32),
            pltpu.VMEM((group, feature), F32),
            pltpu.VMEM((group, part), BF16),
            pltpu.VMEM((group, part), BF16),
            pltpu.VMEM((2, feature, part), BF16),
            pltpu.VMEM((2, part, feature), BF16),
            pltpu.SemaphoreType.DMA((2 * CHIPS * (2 + chunks // 2),)),
            pltpu.SemaphoreType.DMA((2, CHIPS)),
            pltpu.SemaphoreType.DMA((2, 2 * (part * CHIPS // ff))),
        ],
        compiler_params=params(),
        cost_estimate=pl.CostEstimate(
            flops=2 * group * feature * (3 * feature + 6 * ff),
            bytes_accessed=34_000_000,
            transcendentals=2 * group * ff,
        ),
        name="middle",
    )(tab, ctx, hidden, ups, ptab, up_bias, *uo, *dn)


def qkv_weight_kernel(tab, normed, dq, dk, dv, own, oth, norm_t, tmp, sems):
    total, feature = normed.shape
    group = dq.shape[0]
    block = feature // CHIPS
    seg = feature // 2
    core = tab[4, 0]
    tile = 256
    for t in range(total // tile):
        rows = slice(t * tile, (t + 1) * tile)
        norm_t[:, rows] = normed[rows, :].T

    def stores(cc, n):
        made = []
        for half, ref, row in ((cc, own, 0), (1 - cc, oth, 1)):
            for r in range(CHIPS):
                src = pl.ds(pl.multiple_of(tab[row, r] * block, 16), block)
                made.append(
                    pltpu.make_async_copy(
                        tmp.at[n, src, pl.ds(half * seg, seg)],
                        ref.at[pl.ds(r * block, block), pl.ds(n * seg, seg)],
                        sems.at[n, len(made)],
                    )
                )
        return made

    def on_core(run):
        for cc in (0, 1):

            @pl.when(core == cc)
            def _():
                run(cc)

    def start(n):
        def run(cc):
            for one in stores(cc, n):
                one.start()

        on_core(run)

    cut = 256
    for c0 in range(0, feature, cut):
        cols = slice(c0, c0 + cut)
        tmp[1, :, cols] = mm(norm_t[...], dk[:, cols]).astype(BF16)
    start(1)
    for c0 in range(0, feature, cut):
        cols = slice(c0, c0 + cut)
        tmp[2, :, cols] = mm(norm_t[...], dv[:, cols]).astype(BF16)
    start(2)
    tmp[0] = mm(norm_t[:, :group], dq[...]).astype(BF16)
    start(0)

    def finish(cc):
        for n in range(3):
            for one in stores(cc, n):
                one.wait()

    on_core(finish)


def qkv_weight_call(tab, normed, dq, dk, dv):
    total, feature = normed.shape
    half = 3 * feature // 2
    return pl.pallas_call(
        qkv_weight_kernel,
        in_specs=[smem()] + [whole()] * 4,
        out_specs=[hbm(), hbm()],
        out_shape=[jax.ShapeDtypeStruct((feature, half), BF16)] * 2,
        scratch_shapes=[
            pltpu.VMEM((feature, total), BF16),
            pltpu.VMEM((3, feature, feature), BF16),
            pltpu.SemaphoreType.DMA((3, 2 * CHIPS)),
        ],
        compiler_params=params(),
        cost_estimate=pl.CostEstimate(
            flops=2 * dq.shape[0] * feature * feature * 9,
            bytes_accessed=20_000_000,
            transcendentals=0,
        ),
        name="qkv_weight",
    )(tab, normed, dq, dk, dv)


def qkv_back_kernel(
    tab, t0, t1, t2, t3, ids, dq, dk, dv, gm, weight, ptab, given, out, own, sums, rel, sem
):
    step = pl.program_id(0)
    feature = weight.shape[0]
    steps = 768 // out.shape[0]
    block = feature // CHIPS
    core = tab[4, 0]

    @pl.when(step == 0)
    def _():
        sums[...] = jnp.zeros_like(sums)
        sums[4:12, :] = given[4:12, :]

    def body(tok, own_rows):
        value, hot = embed(tok[...], ids[0], ptab)
        vhat, inv = norm_stats(value)
        dy = mm_nt(dk[...], weight[:, feature : 2 * feature]) + mm_nt(
            dv[...], weight[:, 2 * feature :]
        )
        if own_rows:
            dy = dy + mm_nt(dq[...], weight[:, 0:feature])
            sums[2:3, :] += row_sum(dq[...].astype(F32))
        grad = norm_back(vhat, inv, dy, ptab[0:1, :])
        out[...] = grad.astype(BF16)
        sums[0:1, :] += row_sum(dy * vhat)
        sums[1:2, :] += row_sum(dy)
        sums[3:4, :] += row_sum(dv[...].astype(F32))
        if own_rows:
            grad = grad + gm[...]
        high = grad.astype(BF16)
        rest = (grad - high.astype(F32)).astype(BF16)
        sums[16:32, :] += mm(hot, high) + mm(hot, rest)

    for piece, tok in enumerate((t0, t1, t2, t3)):

        @pl.when((step >= piece * steps) & (step < (piece + 1) * steps))
        def _():
            body(tok, piece == 0)

    @pl.when(step == 4 * steps - 1)
    def _():
        turned = jnp.concatenate([sums[...], jnp.zeros((96, feature), F32)], axis=0).T
        rel[...] = turned.astype(BF16)
        made = []
        for side in range(2):
            for r in range(CHIPS):
                src = pl.ds(pl.multiple_of(tab[side, r] * block, 16), block)
                made.append(
                    pltpu.make_async_copy(
                        rel.at[src, :], own.at[side, pl.ds(r * block, block), :], sem.at[side, r]
                    )
                )
        for one in made:
            one.start()
        for one in made:
            one.wait()

    del core


def qkv_back_call(tab, pieces, ids, dq, dk, dv, gm, weight, ptab, given):
    group, feature = dq.shape
    per = 256
    steps = group // per
    total = 4 * steps

    def at(piece):
        return pl.BlockSpec(
            (per, feature), lambda i: (jnp.clip(i - piece * steps, 0, steps - 1), 0)
        )

    tile = pl.BlockSpec((per, feature), lambda i: (i, 0))
    first = pl.BlockSpec((per, feature), lambda i: (jnp.minimum(i, steps - 1), 0))
    return pl.pallas_call(
        qkv_back_kernel,
        grid=(total,),
        in_specs=[smem()]
        + [at(p) for p in range(4)]
        + [
            pl.BlockSpec((1, 1, per), lambda i: (i, 0, 0)),
            first,
            tile,
            tile,
            first,
            once((feature, 3 * feature)),
            once((32, feature)),
            once((16, feature)),
        ],
        out_specs=[tile, hbm()],
        out_shape=[
            jax.ShapeDtypeStruct((4 * group, feature), BF16),
            jax.ShapeDtypeStruct((2, feature, 128), BF16),
        ],
        scratch_shapes=[
            pltpu.VMEM((32, feature), F32),
            pltpu.VMEM((feature, 128), BF16),
            pltpu.SemaphoreType.DMA((2, CHIPS)),
        ],
        compiler_params=params(),
        cost_estimate=pl.CostEstimate(
            flops=2 * group * feature * feature * 9, bytes_accessed=30_000_000, transcendentals=0
        ),
        name="qkv_back",
    )(tab, *pieces, ids.reshape(total, 1, per), dq, dk, dv, gm, weight, ptab, given)


class Hops:
    def __init__(self, n_seq, n_freq):
        self.n_seq, self.n_freq = n_seq, n_freq
        self.swaps = n_seq == 8 and n_freq == 4
        self.core = lax.axis_index("freq") % 2
        chip = lax.axis_index("seq") * 2 + lax.axis_index("freq") // 2
        ident = np.arange(CHIPS)
        if self.swaps:
            bits = ((4, 8, 2, 1), (4, 8, 1, 2))
            masks = np.zeros((2, CHIPS), np.int32)
            for c in (0, 1):
                for r in range(CHIPS):
                    for b in range(4):
                        if r >> b & 1:
                            masks[c, r] ^= bits[c][b]
            inverse = np.argsort(masks, axis=1).astype(np.int32)
            one, two = jnp.asarray(masks[0]), jnp.asarray(masks[1])
            mine = jnp.where(self.core == 0, one, two) ^ chip
            theirs = jnp.where(self.core == 0, two, one) ^ chip

            def places(order):
                rows = (order[:, None] == jnp.arange(CHIPS)[None, :]).astype(jnp.int32)
                return jnp.sum(rows * jnp.arange(CHIPS, dtype=jnp.int32)[:, None], axis=0)

            del inverse
            rows = [mine, theirs, places(mine), places(theirs)]
        else:
            rows = [jnp.asarray(ident, jnp.int32)] * 4
        rows = [r.astype(jnp.int32) for r in rows]
        rows += [jnp.full((CHIPS,), self.core, jnp.int32)] + [rows[0]] * 3
        self.table = jnp.stack(rows)

    def swap(self, values, move):
        pairs = []
        for s in range(self.n_seq):
            for f in range(self.n_freq):
                ds, df = move(f % 2)
                pairs.append((s * self.n_freq + f, (s ^ ds) * self.n_freq + (f ^ df)))
        return lax.ppermute(values, BOTH, pairs)

    def swap_core(self, values):
        return self.swap(values, lambda c: (0, 1))

    def swap_y(self, values):
        return self.swap(values, lambda c: (0, 2))

    STEPS = (
        lambda c: (2, 0),
        lambda c: (4, 0),
        lambda c: (1, 0) if c == 0 else (0, 2),
        lambda c: (0, 2) if c == 0 else (1, 0),
    )

    def gather(self, shard):
        rows, cols = shard.shape
        half = cols // 2
        if not self.swaps:
            full = lax.all_gather(shard, BOTH, axis=0, tiled=True)
            return (
                lax.dynamic_slice_in_dim(full, self.core * half, half, 1),
                lax.dynamic_slice_in_dim(full, (1 - self.core) * half, half, 1),
            )
        left, right = shard[:, :half], shard[:, half:]
        first = self.core == 0
        mine = jnp.where(first, left, right)
        got = self.swap_core(jnp.where(first, right, left))
        held = jnp.concatenate(
            [jnp.where(first, mine, got), jnp.where(first, got, mine)], axis=0
        )
        for move in self.STEPS:
            held = jnp.concatenate([held, self.swap(held, move)], axis=0)
        return held, self.swap_core(held)

    def scatter(self, own, other):
        rows, half = own.shape
        shard = rows // (self.n_seq * self.n_freq)
        first = self.core == 0
        if not self.swaps:
            left = jnp.where(first, own, other)
            right = jnp.where(first, other, own)
            full = jnp.concatenate([left, right], axis=1).astype(F32)
            return lax.psum_scatter(full, BOTH, scatter_dimension=0, tiled=True)

        def add(a, b):
            return (a.astype(F32) + b.astype(F32)).astype(BF16)

        got = self.swap_core(other)
        for n, move in enumerate(self.STEPS[::-1]):
            cut = own.shape[0] // 2
            send = add(own[cut:], got[cut:])
            own = add(own[:cut], got[:cut])
            got = self.swap(send, move)
        whole_rows = own.astype(F32) + got.astype(F32)
        upper, lower = whole_rows[:shard], whole_rows[shard:]
        mine = jnp.where(first, upper, lower)
        got = self.swap_core(jnp.where(first, lower, upper).astype(BF16)).astype(F32)
        return jnp.concatenate(
            [jnp.where(first, mine, got), jnp.where(first, got, mine)], axis=1
        )


def local(
    tokens,
    freq_ids,
    clip_ids,
    cotangent,
    ln1_gain,
    first_norm_bias,
    qkv_weight,
    q_bias,
    v_bias,
    out_weight,
    out_bias,
    ln2_gain,
    ln2_bias,
    up_weight,
    up_bias,
    down_weight,
    down_bias,
    freq_table,
    *,
    n_seq,
    n_freq,
):
    _, group, feature = tokens.shape
    rd = qkv_weight.shape[0]
    n_dev = n_seq * n_freq
    seg = feature // 2
    ff = up_weight.shape[1]
    hops = Hops(n_seq, n_freq)
    tab = hops.table

    tok = tokens.reshape(group, feature)
    ids = freq_ids.reshape(1, group)
    tok_y, ids_y = hops.swap_y(tok), hops.swap_y(ids)
    tok_c, ids_c = hops.swap_core(tok), hops.swap_core(ids)
    tok_yc, ids_yc = hops.swap_core(tok_y), hops.swap_core(ids_y)
    pieces = (tok, tok_y, tok_c, tok_yc)
    all_ids = jnp.concatenate([ids, ids_y, ids_c, ids_yc], axis=0)

    vectors = [ln1_gain, first_norm_bias, q_bias, v_bias, out_bias, ln2_gain, ln2_bias, down_bias]
    small = jnp.concatenate(
        [vec[:, None] for vec in vectors]
        + [up_bias.reshape(4, rd).T, jnp.zeros((rd, 4), BF16), freq_table]
        + [jnp.zeros((rd, 100), BF16)],
        axis=1,
    )

    def halves(*arrays):
        left = [a[:, : a.shape[1] // 2] for a in arrays]
        right = [a[:, a.shape[1] // 2 :] for a in arrays]
        return left, right

    left, right = halves(
        qkv_weight[:, :feature], qkv_weight[:, feature : 2 * feature], qkv_weight[:, 2 * feature :]
    )
    qkv_pair = hops.gather(jnp.concatenate(left + [small] + right + [small], axis=1))
    left, right = halves(up_weight, out_weight)
    uo_pair = hops.gather(jnp.concatenate(left + right, axis=1))
    dn_pair = hops.gather(down_weight)

    place = lax.axis_index("freq")
    order = jnp.stack([place, place ^ 2, place ^ 1, place ^ 3])
    below = clip_ids.reshape(n_freq, group)[:, None, :] < jnp.arange(16, dtype=jnp.int32)[None, :, None]
    first_rows = jnp.sum(below.astype(jnp.int32), axis=2)
    pick = (order[:, None] == jnp.arange(n_freq)[None, :]).astype(jnp.int32)
    starts = jnp.sum(pick[:, :, None] * first_rows[None, :, :], axis=1).reshape(4 * 16)

    normed, keys, values, queries, hidden, w_qkv, ptab = qkv_call(tab, pieces, all_ids, *qkv_pair)
    context = attn_call(starts, queries, keys, values)
    up_rows = ptab[8:12].reshape(4, n_dev, rd).transpose(1, 0, 2).reshape(ff // feature, feature)
    upstream = cotangent.reshape(group, feature)
    mixed, grad_mid, grad_ctx, g_uo_own, g_uo_oth, g_dn_own, g_dn_oth, sums, g_up_bias = middle_call(
        tab, context, hidden, upstream, ptab, up_rows, uo_pair, dn_pair
    )
    g_dn = hops.scatter(g_dn_own, g_dn_oth)
    g_uo = hops.scatter(g_uo_own, g_uo_oth)
    dq, dk, dv = attn_back_call(starts, queries, keys, values, grad_ctx)
    g_qkv = hops.scatter(*qkv_weight_call(tab, normed, dq, dk, dv))
    given = jnp.concatenate(
        [
            sums,
            g_up_bias.reshape(n_dev, 4, rd).transpose(1, 0, 2).reshape(4, feature),
            jnp.zeros((4, feature), F32),
        ],
        axis=0,
    )
    back, g_small = qkv_back_call(
        tab, pieces, all_ids, dq, dk, dv, grad_mid, w_qkv, ptab, given
    )
    vecs = hops.scatter(g_small[0], g_small[1])

    near = hops.swap_core(back[2 * group :])
    far = (back[group : 2 * group].astype(F32) + near[group:].astype(F32)).astype(BF16)
    far = hops.swap_y(far)
    input_grad = grad_mid + back[:group].astype(F32) + near[:group].astype(F32) + far.astype(F32)

    vecs = vecs[:, :128]
    n_up = ff // 2
    grad_qkv = jnp.concatenate(
        [g_qkv[:, n * seg + h * 3 * seg : (n + 1) * seg + h * 3 * seg] for n in range(3) for h in (0, 1)],
        axis=1,
    )
    grad_up = jnp.concatenate([g_uo[:, :n_up], g_uo[:, n_up + seg : 2 * n_up + seg]], axis=1)
    grad_out = jnp.concatenate([g_uo[:, n_up : n_up + seg], g_uo[:, 2 * n_up + seg :]], axis=1)
    return (
        mixed.reshape(tokens.shape),
        input_grad.astype(BF16).reshape(tokens.shape),
        vecs[:, 0],
        vecs[:, 1],
        grad_qkv,
        vecs[:, 2],
        vecs[:, 3],
        grad_out,
        vecs[:, 4],
        vecs[:, 5],
        vecs[:, 6],
        grad_up,
        vecs[:, 8:12].T.reshape(4 * rd),
        g_dn,
        vecs[:, 7],
        vecs[:, 16 : 16 + FREQS],
    )


def solution(mesh):
    rows = P(BOTH)
    mat = P(BOTH, None)
    act = P("seq", "freq", None)
    in_specs = (
        act, P("seq", "freq"), P("seq", None), act,
        rows, rows, mat, rows, rows, mat, rows, rows, rows, mat, rows, mat, rows, mat,
    )
    out_specs = (
        act, act, rows, rows, mat, rows, rows, mat, rows, rows, rows, mat, rows, mat, rows, mat,
    )
    body = functools.partial(local, n_seq=mesh.shape["seq"], n_freq=mesh.shape["freq"])
    return jax.shard_map(body, mesh=mesh, in_specs=in_specs, out_specs=out_specs, check_vma=False)
```

```python
import functools

import jax
import jax.numpy as jnp
import numpy as np
from jax import lax
from jax.experimental import pallas as pl
from jax.experimental.pallas import tpu as pltpu
from jax.sharding import PartitionSpec as P

HEADS = 12
HEAD_DIM = 64
FREQS = 12
CLIPS = 8
WIN = 128
LARGE = 160
CHIPS = 16
EPS = 1e-06
MASKED = -1e30
BOTH = ("seq", "freq")
F32 = jnp.float32
BF16 = jnp.bfloat16
VMEM_LIMIT = 60 * 1024 * 1024


def params(**kw):
    return pltpu.CompilerParams(vmem_limit_bytes=VMEM_LIMIT, **kw)


def whole():
    return pl.BlockSpec(memory_space=pltpu.VMEM)


def smem():
    return pl.BlockSpec(memory_space=pltpu.SMEM)


def hbm():
    return pl.BlockSpec(memory_space=pl.ANY)


def once(shape):
    return pl.BlockSpec(shape, lambda *_: (0,) * len(shape), pipeline_mode=pl.Buffered(1))


def mm(a, b):
    return jnp.dot(a, b, preferred_element_type=F32)


def mm_nt(a, b):
    return lax.dot_general(a, b, (((1,), (1,)), ((), ())), preferred_element_type=F32)


def mm_tn(a, b):
    return lax.dot_general(a, b, (((0,), (0,)), ((), ())), preferred_element_type=F32)


def norm_stats(values):
    center = values - jnp.mean(values, axis=-1, keepdims=True)
    spread = jnp.mean(center * center, axis=-1, keepdims=True)
    inv = lax.rsqrt(spread + EPS)
    return center * inv, inv


def norm_back(vhat, inv, dy, gain):
    gd = dy * gain
    return inv * (
        gd
        - jnp.mean(gd, axis=-1, keepdims=True)
        - vhat * jnp.mean(gd * vhat, axis=-1, keepdims=True)
    )


def row_sum(values):
    return jnp.sum(values, axis=0, keepdims=True)


def embed(tokens, ids, n, ptab):
    count = tokens.shape[0]
    row = lax.broadcasted_iota(jnp.int32, (16, count), 0)
    mine = jnp.sum(
        jnp.where(row == n, ids[:, :count].astype(F32), 0.0), axis=0, keepdims=True
    ).astype(jnp.int32)
    hot = (row == mine).astype(BF16)
    return tokens.astype(F32) + mm_tn(hot, ptab[16:32, :].astype(BF16)), hot


def qkv_kernel(
    tab, t0, t1, t2, t3, i0, i1, i2, i3, own, oth,
    normed, keys, values, queries, hidden, weight, ptab, pm, sems,
    *, group
):
    step = pl.program_id(0)
    feature = weight.shape[0]
    block = feature // CHIPS
    seg = feature // 2
    core = tab[4, 0]

    def copies(cc):
        made = []
        for r in range(CHIPS):
            for half, ref in ((cc, own), (1 - cc, oth)):
                dst = pl.multiple_of(tab[0 if half == cc else 1, r] * block, 16)
                for n in range(3):
                    made.append(
                        pltpu.make_async_copy(
                            ref.at[pl.ds(r * block, block), pl.ds(n * seg, seg)],
                            weight.at[
                                pl.ds(dst, block), pl.ds(n * feature + half * seg, seg)
                            ],
                            sems.at[len(made)],
                        )
                    )
            made.append(
                pltpu.make_async_copy(
                    own.at[pl.ds(r * block, block), pl.ds(3 * seg, 128)],
                    pm.at[pl.ds(pl.multiple_of(tab[0, r] * block, 16), block), :],
                    sems.at[len(made)],
                )
            )
        return made

    @pl.when(step == 0)
    def _():
        for cc in (0, 1):

            @pl.when(core == cc)
            def _():
                made = copies(cc)
                for one in made:
                    one.start()
                for one in made:
                    one.wait()

        ptab[...] = pm[...].astype(F32).T[:32, :]

    steps = group // keys.shape[0]

    def body(tok, ids, own_rows):
        value, _ = embed(tok[...], ids[...], lax.rem(step, steps), ptab)
        vhat, _ = norm_stats(value)
        low = (vhat * ptab[0:1, :] + ptab[1:2, :]).astype(BF16)
        normed[...] = low
        if own_rows:
            hidden[...] = value
            q = mm(low, weight[:, 0:feature]) + ptab[2:3, :]
            queries[...] = q.astype(BF16) * jnp.asarray(HEAD_DIM**-0.5, BF16)
        keys[...] = mm(low, weight[:, feature : 2 * feature]).astype(BF16)
        values[...] = (mm(low, weight[:, 2 * feature :]) + ptab[3:4, :]).astype(BF16)

    for piece, (tok, ids) in enumerate(((t0, i0), (t1, i1), (t2, i2), (t3, i3))):

        @pl.when((step >= piece * steps) & (step < (piece + 1) * steps))
        def _():
            body(tok, ids, piece == 0)


def piece_specs(group, feature, per):
    steps = group // per

    def at(piece):
        return pl.BlockSpec(
            (per, feature), lambda i: (jnp.clip(i - piece * steps, 0, steps - 1), 0)
        )

    ids = pl.BlockSpec((16, feature), lambda i: (group // 16, 0))
    return [at(p) for p in range(4)] + [ids] * 4


def qkv_call(tab, pieces, own, oth):
    feature = pieces[0].shape[1]
    group = pieces[0].shape[0] - 16
    per = 256
    steps = group // per
    tile = pl.BlockSpec((per, feature), lambda i: (i, 0))
    first = pl.BlockSpec((per, feature), lambda i: (jnp.minimum(i, steps - 1), 0))
    return pl.pallas_call(
        functools.partial(qkv_kernel, group=group),
        grid=(4 * steps,),
        in_specs=[smem()] + piece_specs(group, feature, per) + [hbm(), hbm()],
        out_specs=[tile, tile, tile, first, first, once((feature, 3 * feature)), once((32, feature))],
        out_shape=[
            jax.ShapeDtypeStruct((4 * group, feature), BF16),
            jax.ShapeDtypeStruct((4 * group, feature), BF16),
            jax.ShapeDtypeStruct((4 * group, feature), BF16),
            jax.ShapeDtypeStruct((group, feature), BF16),
            jax.ShapeDtypeStruct((group, feature), F32),
            jax.ShapeDtypeStruct((feature, 3 * feature), BF16),
            jax.ShapeDtypeStruct((32, feature), F32),
        ],
        scratch_shapes=[
            pltpu.VMEM((feature, 128), BF16),
            pltpu.SemaphoreType.DMA((7 * CHIPS,)),
        ],
        compiler_params=params(),
        cost_estimate=pl.CostEstimate(
            flops=2 * group * feature * feature * 9, bytes_accessed=30_000_000, transcendentals=0
        ),
        name="qkv",
    )(tab, *pieces, *pieces, own, oth)


def window(starts, g, clip, n, group, win=WIN):
    first = starts[g * 16 + clip]
    last = starts[g * 16 + clip + 1]
    lead = (first // 16) * 16 + n * win
    base = pl.multiple_of(jnp.minimum(lead, group - win), 16)
    return base, jnp.maximum(first, lead) - base, last - base


def counts(starts, clip, groups, win=WIN):
    def need(g):
        first = (starts[g * 16 + clip] // 16) * 16
        return (starts[g * 16 + clip + 1] - first + win - 1) // win

    spans = [need(g) for g in groups]
    most = spans[0]
    for s in spans[1:]:
        most = jnp.maximum(most, s)
    return most


def each_clip(starts, one, many):
    together = 4

    @pl.loop(0, CLIPS // together)
    def _(n):
        clips = [n * together + i for i in range(together)]

        def most(win):
            steps = [counts(starts, clip, range(4), win) for clip in clips]
            top = steps[0]
            for step in steps[1:]:
                top = jnp.maximum(top, step)
            return top

        fits, fits_large = most(WIN) <= 1, most(LARGE) <= 1

        @pl.when(fits)
        def _():
            for clip in clips:
                one(clip, WIN)

        @pl.when(jnp.logical_not(fits) & fits_large)
        def _():
            for clip in clips:
                one(clip, LARGE)

        @pl.when(jnp.logical_not(fits_large))
        def _():
            @pl.loop(0, together)
            def _(i):
                clip = n * together + i
                many(clip, counts(starts, clip, [0]), counts(starts, clip, range(4)))


def lane_halves():
    lane = lax.broadcasted_iota(jnp.int32, (1, 128), 1)
    left = (lane < HEAD_DIM).astype(BF16)
    return left, 1 - left


def stack_heads(rows):
    left, right = lane_halves()
    return jnp.concatenate([rows * left, rows * right], axis=0)


def merge_heads(stacked):
    win = stacked.shape[0] // 2
    lane = lax.broadcasted_iota(jnp.int32, (win, 128), 1)
    return jnp.where(lane < HEAD_DIM, stacked[:win], stacked[win:])


def row_valid(lo, hi, win=WIN):
    row = lax.broadcasted_iota(jnp.int32, (win, 128), 0)
    return (row >= lo) & (row < hi)


def load_keys(starts, clip, n, group, *refs, win=WIN):
    tiles = [[] for _ in refs]
    spans = []
    for g in range(4):
        base, lo, hi = window(starts, g, clip, n, group, win)
        for t, ref in zip(tiles, refs):
            t.append(ref[pl.ds(pl.multiple_of(g * group + base, 16), win), :])
        spans.append((base, lo, hi))
    return [jnp.concatenate(t, axis=0) for t in tiles], spans


def key_bias_row(spans, win=WIN):
    lane = lax.broadcasted_iota(jnp.int32, (1, 4 * win), 1)
    valid = [
        (lane >= lo + g * win) & (lane < jnp.minimum(hi, win) + g * win)
        for g, (_, lo, hi) in enumerate(spans)
    ]
    return jnp.where(valid[0] | valid[1] | valid[2] | valid[3], 0.0, MASKED)


def key_bias_col(spans, win=WIN):
    row = lax.broadcasted_iota(jnp.int32, (win, 2 * win), 0)
    return jnp.concatenate(
        [jnp.where((row >= lo) & (row < hi), 0.0, MASKED) for _, lo, hi in spans], axis=0
    )


def attn_kernel(starts, q, k, v, *rest, group):
    out = rest[-1]

    def one(clip, win):
        base, lo, hi = window(starts, 0, clip, 0, group, win)
        stacked = stack_heads(q[pl.ds(base, win), :])
        (kt, vt), spans = load_keys(starts, clip, 0, group, k, v, win=win)
        scores = mm_nt(stacked, kt) + key_bias_row(spans, win)
        peak = jnp.max(scores, axis=1, keepdims=True)
        e = jnp.exp(scores - peak)
        total = jnp.sum(e, axis=1, keepdims=True)
        o = mm(e.astype(BF16), vt) * (1.0 / total)
        spot = pl.ds(base, win)
        out[spot, :] = jnp.where(row_valid(lo, hi, win), merge_heads(o).astype(BF16), out[spot, :])

    def many(clip, rows, steps):
        @pl.loop(0, rows)
        def _(i):
            base, lo, hi = window(starts, 0, clip, i, group)
            stacked = stack_heads(q[pl.ds(base, WIN), :])

            def inner(j, carry):
                peak, total, acc = carry
                (kt, vt), spans = load_keys(starts, clip, j, group, k, v)
                scores = mm_nt(stacked, kt) + key_bias_row(spans)
                new = jnp.maximum(peak, jnp.max(scores, axis=1, keepdims=True))
                e = jnp.exp(scores - new)
                shrink = jnp.exp(peak - new)
                return (
                    new,
                    total * shrink + jnp.sum(e, axis=1, keepdims=True),
                    acc * shrink + mm(e.astype(BF16), vt),
                )

            start = (
                jnp.full((2 * WIN, 1), 2 * MASKED, F32),
                jnp.zeros((2 * WIN, 1), F32),
                jnp.zeros((2 * WIN, 128), F32),
            )
            _, total, acc = lax.fori_loop(0, steps, inner, start)
            o = merge_heads(acc * (1.0 / total)).astype(BF16)
            spot = pl.ds(base, WIN)
            out[spot, :] = jnp.where(row_valid(lo, hi), o, out[spot, :])

    each_clip(starts, one, many)


def attn_call(starts, queries, keys, values, part, before=None):
    group, feature = queries.shape
    pairs = feature // 384
    small = pl.BlockSpec((group, 128), lambda i: (0, i + part * pairs))
    large = pl.BlockSpec((4 * group, 128), lambda i: (0, i + part * pairs))
    more = [] if before is None else [before]
    return pl.pallas_call(
        functools.partial(attn_kernel, group=group),
        grid=(pairs,),
        in_specs=[smem(), small, large, large] + [hbm()] * len(more),
        out_specs=small,
        out_shape=jax.ShapeDtypeStruct((group, feature), BF16),
        input_output_aliases={4: 0} if more else {},
        compiler_params=params(),
        cost_estimate=pl.CostEstimate(
            flops=10_000_000_000, bytes_accessed=12_000_000, transcendentals=6_300_000
        ),
        name="attention",
    )(starts, queries, keys, values, *more)


def attn_back_kernel(starts, q, k, v, go, *rest, group):
    dq, dk, dv, dk_acc, dv_acc, dq_acc = rest[-6:]
    dk_acc[...] = jnp.zeros_like(dk_acc)
    dv_acc[...] = jnp.zeros_like(dv_acc)
    dq_acc[...] = jnp.zeros_like(dq_acc)
    scale = HEAD_DIM**-0.5

    def load_query(clip, i, win=WIN):
        base, lo, hi = window(starts, 0, clip, i, group, win)
        spot = pl.ds(base, win)
        keep = jnp.where(row_valid(lo, hi, win), go[spot, :], jnp.zeros((), BF16))
        return base, stack_heads(q[spot, :]), stack_heads(keep)

    def finish(spans, base, kt, stacked, back, prob, ds, win=WIN):
        ds = ds.astype(BF16)
        dvt = mm(prob.astype(BF16), back)
        dkt = mm(ds, stacked)
        for g, (kb, _, _) in enumerate(spans):
            spot = pl.ds(pl.multiple_of(g * group + kb, 16), win)
            dk_acc[spot, :] += dkt[g * win : (g + 1) * win]
            dv_acc[spot, :] += dvt[g * win : (g + 1) * win]
        spot = pl.ds(base, win)
        dq_acc[spot, :] += merge_heads(mm_tn(ds, kt))

    def one(clip, win):
        base, stacked, back = load_query(clip, 0, win)
        (kt, vt), spans = load_keys(starts, clip, 0, group, k, v, win=win)
        scores = mm_nt(kt, stacked) + key_bias_col(spans, win)
        peak = jnp.max(scores, axis=0, keepdims=True)
        e = jnp.exp(scores - peak)
        prob = e * (1.0 / jnp.sum(e, axis=0, keepdims=True))
        gp = mm_nt(vt, back)
        inner = jnp.sum(prob * gp, axis=0, keepdims=True)
        finish(spans, base, kt, stacked, back, prob, prob * (gp - inner), win)

    def many(clip, rows, steps):
        @pl.loop(0, rows)
        def _(i):
            base, stacked, back = load_query(clip, i)

            def totals(j, carry):
                peak, total, inner = carry
                (kt, vt), spans = load_keys(starts, clip, j, group, k, v)
                scores = mm_nt(kt, stacked) + key_bias_col(spans)
                new = jnp.maximum(peak, jnp.max(scores, axis=0, keepdims=True))
                e = jnp.exp(scores - new)
                shrink = jnp.exp(peak - new)
                gp = mm_nt(vt, back)
                return (
                    new,
                    total * shrink + jnp.sum(e, axis=0, keepdims=True),
                    inner * shrink + jnp.sum(e * gp, axis=0, keepdims=True),
                )

            zero = jnp.zeros((1, 2 * WIN), F32)
            peak, total, inner = lax.fori_loop(
                0, steps, totals, (jnp.full((1, 2 * WIN), 2 * MASKED, F32), zero, zero)
            )
            part = 1.0 / total
            inner = inner * part

            @pl.loop(0, steps)
            def _(j):
                (kt, vt), spans = load_keys(starts, clip, j, group, k, v)
                scores = mm_nt(kt, stacked) + key_bias_col(spans)
                prob = jnp.exp(scores - peak) * part
                gp = mm_nt(vt, back)
                finish(spans, base, kt, stacked, back, prob, prob * (gp - inner))

    each_clip(starts, one, many)

    dq[...] = (dq_acc[...] * scale).astype(BF16)
    dk[...] = dk_acc[...].astype(BF16)
    dv[...] = dv_acc[...].astype(BF16)


def attn_back_call(starts, queries, keys, values, grad_context, part, before=()):
    group, feature = queries.shape
    pairs = feature // 384
    small = pl.BlockSpec((group, 128), lambda i: (0, i + part * pairs))
    large = pl.BlockSpec((4 * group, 128), lambda i: (0, i + part * pairs))
    return pl.pallas_call(
        functools.partial(attn_back_kernel, group=group),
        grid=(pairs,),
        in_specs=[smem(), small, large, large, small] + [hbm()] * len(before),
        out_specs=[small, large, large],
        out_shape=[
            jax.ShapeDtypeStruct((group, feature), BF16),
            jax.ShapeDtypeStruct((4 * group, feature), BF16),
            jax.ShapeDtypeStruct((4 * group, feature), BF16),
        ],
        input_output_aliases={5 + n: n for n in range(len(before))},
        scratch_shapes=[
            pltpu.VMEM((4 * group, 128), F32),
            pltpu.VMEM((4 * group, 128), F32),
            pltpu.VMEM((group, 128), F32),
        ],
        compiler_params=params(),
        cost_estimate=pl.CostEstimate(
            flops=20_000_000_000, bytes_accessed=24_000_000, transcendentals=6_300_000
        ),
        name="attention_back",
    )(starts, queries, keys, values, grad_context, *before)


def phi_parts(u):
    x = jnp.abs(u) * (0.5**0.5)
    t = 1.0 / (1.0 + 0.3275911 * x)
    e = jnp.exp(-(x * x))
    poly = t * (
        0.254829592
        + t * (-0.284496736 + t * (1.421413741 + t * (-1.453152027 + t * 1.061405429)))
    )
    tail = 0.5 * poly * e
    return jnp.where(u < 0, tail, 1.0 - tail), e * 0.3989422804014327


def middle_kernel(
    tab, ctx, hidden, ups, ptab, up_bias, u_own, u_oth, d_own, d_oth,
    mixed, grad_mid, grad_ctx, gu_own, gu_oth, gd_own, gd_oth, small, g_up_bias,
    w_up, w_dn, w_out, mid, sec, sec_t, acc, gsec, act, gup, t_up, t_dn, in_sems, up_sems, dn_sems,
    *, chunks
):
    j = pl.program_id(0)
    group, feature = ctx.shape
    block = feature // CHIPS
    dblock = w_dn.shape[0] // CHIPS
    seg = feature // 2
    part = w_dn.shape[0] // chunks
    per_half = chunks // 2
    core = tab[4, 0]
    tile = 256
    tiles = group // tile

    def loads(cc):
        made = []

        def add(src, dst):
            made.append(pltpu.make_async_copy(src, dst, in_sems.at[len(made)]))

        for r in range(CHIPS):
            for half, ref, dref, row in ((cc, u_own, d_own, 0), (1 - cc, u_oth, d_oth, 1)):
                chip = tab[row, r]
                dst = pl.ds(pl.multiple_of(chip * block, 16), block)
                src = pl.ds(r * block, block)
                add(
                    ref.at[src, pl.ds(per_half * part, seg)],
                    w_out.at[dst, pl.ds(half * seg, seg)],
                )
                for n in range(per_half):
                    add(
                        ref.at[src, pl.ds(n * part, part)],
                        w_up.at[half * per_half + n, dst, :],
                    )
                for n in range(dblock // block):
                    row0 = pl.multiple_of(chip * dblock + n * block, 16)
                    add(
                        dref.at[src, pl.ds(n * seg, seg)],
                        w_dn.at[pl.ds(row0, block), pl.ds(half * seg, seg)],
                    )
        return made

    def for_core(run):
        for cc in (0, 1):

            @pl.when(core == cc)
            def _():
                run(cc)

    @pl.when(j == 0)
    def _():
        def run(cc):
            made = loads(cc)
            for one in made:
                one.start()
            for one in made:
                one.wait()

        for_core(run)
        for t in range(tiles):
            rows = slice(t * tile, (t + 1) * tile)
            value = hidden[rows, :] + mm(ctx[rows, :], w_out[...]) + ptab[4:5, :]
            mid[rows, :] = value
            vhat, _ = norm_stats(value)
            low = (vhat * ptab[5:6, :] + ptab[6:7, :]).astype(BF16)
            sec[rows, :] = low
            sec_t[:, rows] = low.T
            acc[rows, :] = value + ptab[7:8, :]
            gsec[rows, :] = jnp.zeros((tile, feature), F32)

    slot = lax.rem(j, 2)

    def drain(sl):
        for r in range(CHIPS):
            pltpu.make_async_copy(
                t_up.at[sl, pl.ds(0, block), :],
                gu_own.at[pl.ds(0, block), pl.ds(0, part)],
                up_sems.at[sl, r],
            ).wait()
        for n in range(2 * (part // block)):
            pltpu.make_async_copy(
                t_dn.at[sl, pl.ds(0, block), pl.ds(0, seg)],
                gd_own.at[pl.ds(0, block), pl.ds(0, seg)],
                dn_sems.at[sl, n],
            ).wait()

    upj = w_up[j]
    dnj = w_dn[pl.ds(pl.multiple_of(j * part, 128), part), :]
    bias = up_bias[pl.ds(j, 1), :]
    gub = jnp.zeros((1, part), F32)
    for t in range(tiles):
        rows = slice(t * tile, (t + 1) * tile)
        u = mm(sec[rows, :], upj) + bias
        dist, dens = phi_parts(u)
        a = (u * dist).astype(BF16)
        g = (mm_nt(ups[rows, :], dnj) * (dist + u * dens)).astype(BF16)
        act[rows, :] = a
        gup[rows, :] = g
        gub = gub + row_sum(g.astype(F32))
        acc[rows, :] += mm(a, dnj)
        gsec[rows, :] += mm_nt(g, upj)
    g_up_bias[pl.ds(j, 1), :] = gub

    @pl.when(j >= 2)
    def _():
        drain(slot)

    t_up[slot] = mm(sec_t[...], gup[...]).astype(BF16)
    t_dn[slot] = mm_tn(act[...], ups[...]).astype(BF16)

    def send(cc):
        col = pl.ds(pl.multiple_of(lax.rem(j, per_half) * part, 128), part)
        for is_own in (True, False):
            ref = gu_own if is_own else gu_oth

            @pl.when((j // per_half == cc) == is_own)
            def _():
                for r in range(CHIPS):
                    src = pl.ds(pl.multiple_of(tab[0 if is_own else 1, r] * block, 16), block)
                    pltpu.make_async_copy(
                        t_up.at[slot, src, :],
                        ref.at[pl.ds(r * block, block), col],
                        up_sems.at[slot, r],
                    ).start()

        n = 0
        count = part // dblock
        for half, ref, row in ((cc, gd_own, 2), (1 - cc, gd_oth, 3)):
            for i in range(count):
                place = pl.multiple_of(tab[row, j * count + i] * block, 16)
                for m in range(dblock // block):
                    pltpu.make_async_copy(
                        t_dn.at[
                            slot, pl.ds(i * dblock + m * block, block), pl.ds(half * seg, seg)
                        ],
                        ref.at[pl.ds(place, block), pl.ds(m * seg, seg)],
                        dn_sems.at[slot, n],
                    ).start()
                    n += 1

    for_core(send)

    @pl.when(j == chunks - 1)
    def _():
        s_gain = jnp.zeros((1, feature), F32)
        s_shift = jnp.zeros((1, feature), F32)
        s_out = jnp.zeros((1, feature), F32)
        s_down = jnp.zeros((1, feature), F32)
        for t in range(tiles):
            rows = slice(t * tile, (t + 1) * tile)
            mixed[rows, :] = acc[rows, :].astype(BF16)
            vhat, inv = norm_stats(mid[rows, :])
            dy = gsec[rows, :]
            wide = ups[rows, :].astype(F32)
            gm = wide + norm_back(vhat, inv, dy, ptab[5:6, :])
            grad_mid[rows, :] = gm
            low = gm.astype(BF16)
            gup[rows, :] = low
            grad_ctx[rows, :] = mm_nt(low, w_out[...]).astype(BF16)
            s_gain = s_gain + row_sum(dy * vhat)
            s_shift = s_shift + row_sum(dy)
            s_out = s_out + row_sum(gm)
            s_down = s_down + row_sum(wide)
        zero = jnp.zeros((1, feature), F32)
        small[...] = jnp.concatenate(
            [zero, zero, zero, zero, s_out, s_gain, s_shift, s_down], axis=0
        )
        drain(1 - slot)
        act[...] = mm_tn(ctx[...], gup[...]).astype(BF16)

        def run(cc):
            made = []
            for half, ref, row in ((cc, gu_own, 0), (1 - cc, gu_oth, 1)):
                for r in range(CHIPS):
                    src = pl.ds(pl.multiple_of(tab[row, r] * block, 16), block)
                    made.append(
                        pltpu.make_async_copy(
                            act.at[src, pl.ds(half * seg, seg)],
                            ref.at[pl.ds(r * block, block), pl.ds(per_half * part, seg)],
                            in_sems.at[len(made)],
                        )
                    )
            for one in made:
                one.start()
            for one in made:
                one.wait()

        for_core(run)
        drain(slot)


def middle_call(tab, ctx, hidden, ups, ptab, up_bias, up_pair, down_pair, ff):
    group, feature = hidden.shape
    chunks = ff // feature
    part = ff // chunks
    return pl.pallas_call(
        functools.partial(middle_kernel, chunks=chunks),
        grid=(chunks,),
        in_specs=[
            smem(),
            once((group, feature)),
            once((group, feature)),
            once((group, feature)),
            once((32, feature)),
            once((chunks, part)),
            hbm(), hbm(), hbm(), hbm(),
        ],
        out_specs=[
            once((group, feature)),
            once((group, feature)),
            once((group, feature)),
            hbm(), hbm(), hbm(), hbm(),
            once((8, feature)),
            once((chunks, part)),
        ],
        out_shape=[
            jax.ShapeDtypeStruct((group, feature), BF16),
            jax.ShapeDtypeStruct((group, feature), F32),
            jax.ShapeDtypeStruct((group, feature), BF16),
            jax.ShapeDtypeStruct(up_pair[0].shape, BF16),
            jax.ShapeDtypeStruct(up_pair[0].shape, BF16),
            jax.ShapeDtypeStruct(down_pair[0].shape, BF16),
            jax.ShapeDtypeStruct(down_pair[0].shape, BF16),
            jax.ShapeDtypeStruct((8, feature), F32),
            jax.ShapeDtypeStruct((chunks, part), F32),
        ],
        scratch_shapes=[
            pltpu.VMEM((chunks, feature, part), BF16),
            pltpu.VMEM((ff, feature), BF16),
            pltpu.VMEM((feature, feature), BF16),
            pltpu.VMEM((group, feature), F32),
            pltpu.VMEM((group, feature), BF16),
            pltpu.VMEM((feature, group), BF16),
            pltpu.VMEM((group, feature), F32),
            pltpu.VMEM((group, feature), F32),
            pltpu.VMEM((group, part), BF16),
            pltpu.VMEM((group, part), BF16),
            pltpu.VMEM((2, feature, part), BF16),
            pltpu.VMEM((2, part, feature), BF16),
            pltpu.SemaphoreType.DMA((2 * CHIPS * (1 + chunks // 2 + ff // feature),)),
            pltpu.SemaphoreType.DMA((2, CHIPS)),
            pltpu.SemaphoreType.DMA((2, 2 * CHIPS)),
        ],
        compiler_params=params(),
        cost_estimate=pl.CostEstimate(
            flops=2 * group * feature * (3 * feature + 6 * ff),
            bytes_accessed=34_000_000,
            transcendentals=2 * group * ff,
        ),
        name="middle",
    )(tab, ctx, hidden, ups, ptab, up_bias, *up_pair, *down_pair)


def qkv_weight_kernel(tab, normed, dq, dk, dv, own, oth, norm_t, tmp, sems):
    total, feature = normed.shape
    group = dq.shape[0]
    block = feature // CHIPS
    seg = feature // 2
    core = tab[4, 0]
    tile = 256
    for t in range(total // tile):
        rows = slice(t * tile, (t + 1) * tile)
        norm_t[:, rows] = normed[rows, :].T

    def stores(cc, n):
        made = []
        for half, ref, row in ((cc, own, 0), (1 - cc, oth, 1)):
            for r in range(CHIPS):
                src = pl.ds(pl.multiple_of(tab[row, r] * block, 16), block)
                made.append(
                    pltpu.make_async_copy(
                        tmp.at[n, src, pl.ds(half * seg, seg)],
                        ref.at[pl.ds(r * block, block), pl.ds(n * seg, seg)],
                        sems.at[n, len(made)],
                    )
                )
        return made

    def on_core(run):
        for cc in (0, 1):

            @pl.when(core == cc)
            def _():
                run(cc)

    def start(n):
        def run(cc):
            for one in stores(cc, n):
                one.start()

        on_core(run)

    cut = 256
    for c0 in range(0, feature, cut):
        cols = slice(c0, c0 + cut)
        tmp[1, :, cols] = mm(norm_t[...], dk[:, cols]).astype(BF16)
    start(1)
    for c0 in range(0, feature, cut):
        cols = slice(c0, c0 + cut)
        tmp[2, :, cols] = mm(norm_t[...], dv[:, cols]).astype(BF16)
    start(2)
    tmp[0] = mm(norm_t[:, :group], dq[...]).astype(BF16)
    start(0)

    def finish(cc):
        for n in range(3):
            for one in stores(cc, n):
                one.wait()

    on_core(finish)


def qkv_weight_call(tab, normed, dq, dk, dv):
    total, feature = normed.shape
    half = 3 * feature // 2
    return pl.pallas_call(
        qkv_weight_kernel,
        in_specs=[smem()] + [whole()] * 4,
        out_specs=[hbm(), hbm()],
        out_shape=[jax.ShapeDtypeStruct((feature, half), BF16)] * 2,
        scratch_shapes=[
            pltpu.VMEM((feature, total), BF16),
            pltpu.VMEM((3, feature, feature), BF16),
            pltpu.SemaphoreType.DMA((3, 2 * CHIPS)),
        ],
        compiler_params=params(),
        cost_estimate=pl.CostEstimate(
            flops=2 * dq.shape[0] * feature * feature * 9,
            bytes_accessed=20_000_000,
            transcendentals=0,
        ),
        name="qkv_weight",
    )(tab, normed, dq, dk, dv)


def qkv_back_kernel(*refs, group, own_rows):
    tab, refs = refs[0], refs[1:]
    n_pieces = 2 if own_rows else 1
    toks, idss, refs = refs[:n_pieces], refs[n_pieces : 2 * n_pieces], refs[2 * n_pieces :]
    dk, dv, weight, ptab, given = refs[:5]
    refs = refs[5:]
    if own_rows:
        dq, gm, out, sums, small, moved, sems = refs
    else:
        out, sums = refs
    step = pl.program_id(0)
    feature = weight.shape[0]
    steps = group // out.shape[0]

    @pl.when(step == 0)
    def _():
        sums[...] = given[...]

    def body(tok, ids, own):
        value, hot = embed(tok[...], ids[...], lax.rem(step, steps), ptab)
        vhat, inv = norm_stats(value)
        dy = mm_nt(dk[...], weight[:, feature : 2 * feature]) + mm_nt(
            dv[...], weight[:, 2 * feature :]
        )
        if own:
            dy = dy + mm_nt(dq[...], weight[:, 0:feature])
            sums[2:3, :] += row_sum(dq[...].astype(F32))
        grad = norm_back(vhat, inv, dy, ptab[0:1, :])
        out[...] = grad.astype(BF16)
        sums[0:1, :] += row_sum(dy * vhat)
        sums[1:2, :] += row_sum(dy)
        sums[3:4, :] += row_sum(dv[...].astype(F32))
        if own:
            grad = grad + gm[...]
        high = grad.astype(BF16)
        rest = (grad - high.astype(F32)).astype(BF16)
        sums[16:32, :] += mm(hot, high) + mm(hot, rest)

    if own_rows:

        @pl.when(step < steps)
        def _():
            body(toks[0], idss[0], True)

        @pl.when(step >= steps)
        def _():
            body(toks[1], idss[1], False)

    else:
        body(toks[0], idss[0], False)

    if own_rows:

        @pl.when(step == 2 * steps - 1)
        def _():
            turned = jnp.concatenate([sums[...], jnp.zeros((96, feature), F32)], axis=0).T
            moved[...] = turned.astype(BF16)
            block = feature // CHIPS
            made = []
            for side in range(2):
                for r in range(CHIPS):
                    src = pl.ds(pl.multiple_of(tab[side, r] * block, 16), block)
                    made.append(
                        pltpu.make_async_copy(
                            moved.at[src, :],
                            small.at[side, pl.ds(r * block, block), :],
                            sems.at[side, r],
                        )
                    )
            for one in made:
                one.start()
            for one in made:
                one.wait()


def qkv_back_call(tab, pair, first_piece, dk, dv, weight, ptab, given, own=()):
    feature = dk.shape[1]
    group = pair[0].shape[0] - 16
    per = 256
    steps = group // per
    skip = first_piece * steps
    count = len(pair)

    def at(piece):
        return pl.BlockSpec(
            (per, feature), lambda i: (jnp.clip(i - piece * steps, 0, steps - 1), 0)
        )

    ids = pl.BlockSpec((16, feature), lambda i: (group // 16, 0))
    tile = pl.BlockSpec((per, feature), lambda i: (i, 0))
    later = pl.BlockSpec((per, feature), lambda i: (i + skip, 0))
    first = pl.BlockSpec((per, feature), lambda i: (jnp.minimum(i, steps - 1), 0))
    return pl.pallas_call(
        functools.partial(qkv_back_kernel, group=group, own_rows=bool(own)),
        grid=(count * steps,),
        in_specs=[smem()]
        + [at(n) for n in range(count)]
        + [ids] * count
        + [later, later]
        + [once((feature, 3 * feature)), once((32, feature)), once((32, feature))]
        + [first] * len(own),
        out_specs=[tile, once((32, feature))] + [hbm()] * bool(own),
        out_shape=[
            jax.ShapeDtypeStruct((count * group, feature), BF16),
            jax.ShapeDtypeStruct((32, feature), F32),
            jax.ShapeDtypeStruct((2, feature, 128), BF16),
        ][: 2 + bool(own)],
        scratch_shapes=[pltpu.VMEM((feature, 128), BF16), pltpu.SemaphoreType.DMA((2, CHIPS))][
            : 2 * bool(own)
        ],
        compiler_params=params(),
        cost_estimate=pl.CostEstimate(
            flops=group * feature * feature * 9, bytes_accessed=15_000_000, transcendentals=0
        ),
        name="qkv_back",
    )(tab, *pair, *pair, dk, dv, weight, ptab, given, *own)


def payload_kernel(tab, *refs, rd, times):
    vecs, (up_bias, table, qkv, up, out, down, mine, other, lines) = refs[:8], refs[8:]
    feature = down.shape[1]
    seg = feature // 2
    ff = up.shape[1]
    core = tab[4, 0]
    lines[...] = jnp.zeros_like(lines)
    for n, vec in enumerate(vecs):
        lines[n : n + 1, 0:rd] = vec[...].astype(F32)
    for n in range(4):
        lines[8 + n : 9 + n, 0:rd] = up_bias[:, n * rd : (n + 1) * rd].astype(F32)

    def places(rows, first):
        row = lax.broadcasted_iota(jnp.int32, (rows, 128), 0)
        return (lax.broadcasted_iota(jnp.int32, (rows, 128), 1) == row + first).astype(BF16)

    small = mm_tn(lines[...].astype(BF16), places(16, 0))[:rd] + mm(table[...], places(FREQS, 16))
    small = small.astype(BF16)
    wide = down[...].astype(F32)

    def fill(ref, h):
        at = 0

        def put(value):
            nonlocal at
            ref[:, at : at + value.shape[1]] = value
            at += value.shape[1]

        for n in range(3):
            put(qkv[:, n * feature + h * seg : n * feature + (h + 1) * seg])
        put(small)
        put(up[:, h * (ff // 2) : (h + 1) * (ff // 2)])
        put(out[:, h * seg : (h + 1) * seg])
        for n in range(times):
            put(wide[n * rd : (n + 1) * rd, h * seg : (h + 1) * seg].astype(BF16))

    for cc in (0, 1):

        @pl.when(core == cc)
        def _():
            fill(mine, cc)
            fill(other, 1 - cc)


def payload_call(tab, vecs, up_bias, table, qkv, up, out, down):
    rd, times = qkv.shape[0], down.shape[0] // qkv.shape[0]
    half = (qkv.shape[1] + up.shape[1] + out.shape[1] + times * down.shape[1]) // 2 + 128
    return pl.pallas_call(
        functools.partial(payload_kernel, rd=rd, times=times),
        in_specs=[smem()] + [whole()] * (len(vecs) + 6),
        out_specs=[whole(), whole()],
        out_shape=[jax.ShapeDtypeStruct((rd, half), BF16)] * 2,
        scratch_shapes=[pltpu.VMEM((16, 128), F32)],
        compiler_params=params(),
        name="payload",
    )(tab, *[v.reshape(1, -1) for v in vecs], up_bias.reshape(1, -1), table, qkv, up, out, down)


def pair_kernel(tab, mine, got, for_q, for_u, for_d, *, widths):
    rd = mine.shape[0]
    n_q, n_u, times, seg = widths
    core = tab[4, 0]

    def fill(top, low):
        for ref, start, width in ((for_q, 0, n_q), (for_u, n_q, n_u)):
            cols = slice(start, start + width)
            ref[...] = jnp.concatenate(
                [top[:, cols].astype(F32), low[:, cols].astype(F32)], axis=0
            ).astype(BF16)
        for block in range(times):
            part = top if block < times // 2 else low
            start = n_q + n_u + (block % (times // 2)) * 2 * seg
            rows = [part[:, start + i * seg : start + (i + 1) * seg].astype(F32) for i in (0, 1)]
            for_d[:, block * seg : (block + 1) * seg] = jnp.concatenate(rows, axis=0).astype(BF16)

    for cc in (0, 1):

        @pl.when(core == cc)
        def _():
            fill(*((mine, got) if cc == 0 else (got, mine)))


def pair_call(tab, mine, got, widths):
    rd = mine.shape[0]
    n_q, n_u, times, seg = widths
    return pl.pallas_call(
        functools.partial(pair_kernel, widths=widths),
        in_specs=[smem(), whole(), whole()],
        out_specs=[whole()] * 3,
        out_shape=[jax.ShapeDtypeStruct((2 * rd, n), BF16) for n in (n_q, n_u, times * seg)],
        compiler_params=params(),
        name="pair",
    )(tab, mine, got)


def tail_rows_kernel(tokens, ids, out):
    group, feature = tokens.shape
    out[0:group, :] = tokens[...]
    rows = [ids[:, n * 256 : (n + 1) * 256].astype(F32) for n in range(group // 256)]
    rows = jnp.concatenate(rows + [jnp.zeros((16 - len(rows), 256), F32)], axis=0).astype(BF16)
    out[group : group + 16, :] = jnp.concatenate(
        [rows, jnp.zeros((16, feature - 256), BF16)], axis=1
    )


def tail_rows_call(tokens, ids):
    group, feature = tokens.shape
    return pl.pallas_call(
        tail_rows_kernel,
        in_specs=[whole(), whole()],
        out_specs=whole(),
        out_shape=jax.ShapeDtypeStruct((group + 16, feature), BF16),
        compiler_params=params(),
        name="tail_rows",
    )(tokens, ids)


class Hops:
    def __init__(self, n_seq, n_freq):
        self.n_seq, self.n_freq = n_seq, n_freq
        self.swaps = n_seq == 8 and n_freq == 4
        self.core = lax.axis_index("freq") % 2
        self.first = self.core == 0
        chip = lax.axis_index("seq") * 2 + lax.axis_index("freq") // 2
        if self.swaps:
            bits = ((4, 8, 2, 1), (4, 8, 1, 2))
            masks = np.zeros((2, CHIPS), np.int32)
            for c in (0, 1):
                for r in range(CHIPS):
                    for b in range(4):
                        if r >> b & 1:
                            masks[c, r] ^= bits[c][b]
            one, two = jnp.asarray(masks[0]), jnp.asarray(masks[1])
            mine = jnp.where(self.first, one, two) ^ chip
            theirs = jnp.where(self.first, two, one) ^ chip

            def places(order):
                rows = (order[:, None] == jnp.arange(CHIPS)[None, :]).astype(jnp.int32)
                return jnp.sum(rows * jnp.arange(CHIPS, dtype=jnp.int32)[:, None], axis=0)

            rows = [mine, theirs, places(mine), places(theirs)]
        else:
            rows = [jnp.arange(CHIPS, dtype=jnp.int32)] * 4
        rows = [r.astype(jnp.int32) for r in rows]
        rows += [jnp.full((CHIPS,), self.core, jnp.int32)] + [rows[0]] * 3
        self.table = jnp.stack(rows)

    def swap(self, values, move):
        pairs = []
        for s in range(self.n_seq):
            for f in range(self.n_freq):
                ds, df = move(f % 2)
                pairs.append((s * self.n_freq + f, (s ^ ds) * self.n_freq + (f ^ df)))
        return lax.ppermute(values, BOTH, pairs)

    def swap_core(self, values):
        return self.swap(values, lambda c: (0, 1))

    def swap_y(self, values):
        return self.swap(values, lambda c: (0, 2))

    def swap_z(self, values, n):
        return self.swap(values, lambda c: (2 * n, 0))

    def swap_xy(self, values, n):
        return self.swap(values, lambda c: (1, 0) if c == n else (0, 2))

    def sides(self, mine, other):
        return jnp.where(self.first, mine, other), jnp.where(self.first, other, mine)

    def own_other(self, left, right):
        return jnp.where(self.first, left, right), jnp.where(self.first, right, left)

    def gather(self, held):
        held = yield jnp.concatenate([held] + [self.swap_z(held, n) for n in (1, 2, 3)], axis=0)
        held = yield jnp.concatenate([held, self.swap_xy(held, 0)], axis=0)
        held = yield jnp.concatenate([held, self.swap_xy(held, 1)], axis=0)
        yield held, self.swap_core(held)

    def scatter(self, own, other):
        own, got = yield own, self.swap_core(other)
        add = self.add
        for n in (1, 0):
            cut = own.shape[0] // 2
            send = add(own[cut:], got[cut:])
            own = add(own[:cut], got[:cut])
            own, got = yield own, self.swap_xy(send, n)
        yield from self.last_sums((own, got))

    @staticmethod
    def add(a, b):
        return (a.astype(F32) + b.astype(F32)).astype(BF16)

    def last_sums(self, pair):
        own, got = pair
        add = self.add
        cut = own.shape[0] // 4
        sends = [add(own[n * cut : (n + 1) * cut], got[n * cut : (n + 1) * cut]) for n in (1, 2, 3)]
        own = own[:cut].astype(F32) + got[:cut].astype(F32)
        own, got = yield own, [self.swap_z(send, n) for n, send in zip((1, 2, 3), sends)]
        yield own + sum(g.astype(F32) for g in got)


class Chain:
    def __init__(self, steps, count):
        self.steps, self.left, self.at = steps, count, None

    def step(self, times=1):
        for _ in range(times):
            self.at = next(self.steps) if self.at is None else self.steps.send(self.at)
            self.left -= 1
        return self.at

    def end(self):
        return self.step(self.left)


class Still:
    def __init__(self, value):
        self.at = value

    def step(self, times=1):
        return self.at

    end = step


def after(values, *chains):
    values, held = lax.optimization_barrier((values, tuple(c.at for c in chains)))
    for c, h in zip(chains, held):
        c.at = h
    return values


def col_halves(*arrays):
    left = [a[:, : a.shape[1] // 2] for a in arrays]
    right = [a[:, a.shape[1] // 2 :] for a in arrays]
    return left, right


def side_rows(down, count):
    rows, cols = down.shape
    return down.reshape(count, rows // count, cols).transpose(1, 0, 2).reshape(rows // count, -1)


def under_rows(wide, count):
    rows, cols = wide.shape
    return wide.reshape(rows, count, cols // count).transpose(1, 0, 2).reshape(rows * count, -1)


def local(
    tokens,
    freq_ids,
    clip_ids,
    cotangent,
    ln1_gain,
    first_norm_bias,
    qkv_weight,
    q_bias,
    v_bias,
    out_weight,
    out_bias,
    ln2_gain,
    ln2_bias,
    up_weight,
    up_bias,
    down_weight,
    down_bias,
    freq_table,
    *,
    n_seq,
    n_freq,
):
    _, group, feature = tokens.shape
    rd = qkv_weight.shape[0]
    n_dev = n_seq * n_freq
    seg = feature // 2
    ff = up_weight.shape[1]
    times = ff // feature
    hops = Hops(n_seq, n_freq)
    tab = hops.table

    tok = tail_rows_call(tokens.reshape(group, feature), freq_ids.reshape(1, group))
    vectors = [ln1_gain, first_norm_bias, q_bias, v_bias, out_bias, ln2_gain, ln2_bias, down_bias]
    wide_q = 3 * seg + 128
    n_up = ff // 2
    n_uo = n_up + seg
    n_all = wide_q + n_uo
    tok_c, tok_y = hops.swap_core(tok), hops.swap_y(tok)
    if hops.swaps:
        mine, other = payload_call(
            tab, vectors, up_bias, freq_table, qkv_weight, up_weight, out_weight, down_weight
        )
        held = pair_call(tab, mine, hops.swap_core(other), (wide_q, n_uo, times, seg))
        weights, ups, downs = [Chain(hops.gather(h), 4) for h in held]
    else:

        def full(x):
            return lax.all_gather(x, BOTH, axis=0, tiled=True)

        lines = jnp.concatenate(vectors + [up_bias]).reshape(12, rd)
        small = jnp.concatenate(
            [lines, jnp.zeros((4, rd), BF16), freq_table.T, jnp.zeros((100, rd), BF16)], axis=0
        ).T
        f_qkv, f_small, f_up = full(qkv_weight), full(small), full(up_weight)
        f_out, f_down = full(out_weight), full(down_weight)
        q_full = [f_qkv[:, n * feature : (n + 1) * feature] for n in range(3)]
        down_side = f_down.reshape(CHIPS, times, -1, feature).transpose(0, 2, 1, 3)
        down_side = down_side.reshape(feature, times, 2, seg)
        sides_q, sides_u, sides_d = [], [], []
        for h in (0, 1):
            sides_q.append(jnp.concatenate(col_halves(*q_full)[h] + [f_small], axis=1))
            sides_u.append(jnp.concatenate(col_halves(f_up, f_out)[h], axis=1))
            sides_d.append(down_side[:, :, h].reshape(feature, times * seg))
        weights, ups, downs = [
            Still(hops.own_other(*sides)) for sides in (sides_q, sides_u, sides_d)
        ]

    weights.step()
    tok_c = after(tok_c, weights)
    ups.step()
    weights.step()
    tok_y = after(tok_y, weights)
    weights.step()
    tok_yc = hops.swap_core(tok_y)
    tok_c = after(tok_c, weights, ups)
    downs.step()
    weights.end()
    pieces = (tok, tok_c, tok_y, tok_yc)

    place = lax.axis_index("freq")
    order = jnp.stack([place, place ^ 1, place ^ 2, place ^ 3])
    below = clip_ids.reshape(n_freq, group)[:, None, :] < jnp.arange(16, dtype=jnp.int32)[None, :, None]
    first_rows = jnp.sum(below.astype(jnp.int32), axis=2)
    pick = (order[:, None] == jnp.arange(n_freq)[None, :]).astype(jnp.int32)
    starts = jnp.sum(pick[:, :, None] * first_rows[None, :, :], axis=1).reshape(4 * 16)

    ups.step()
    normed, keys, values, queries, hidden, w_qkv, ptab = qkv_call(tab, pieces, *weights.at)
    queries, keys, values = after((queries, keys, values), ups, downs)
    ups.step()
    downs.step()
    context = attn_call(starts, queries, keys, values, 0)
    queries, context = after((queries, context), downs)
    downs.step()
    context = attn_call(starts, queries, keys, values, 1, context)
    queries, context = after((queries, context), ups, downs)
    ups.step()
    downs.step()
    context = attn_call(starts, queries, keys, values, 2, context)
    up_rows = ptab[8:12].reshape(4, n_dev, rd).transpose(1, 0, 2).reshape(times, feature)
    upstream = cotangent.reshape(group, feature)
    mixed, grad_mid, grad_ctx, *sent, sums, g_up_bias = middle_call(
        tab, context, hidden, upstream, ptab, up_rows, ups.at, downs.at, ff
    )

    def summing(own, oth):
        return Chain(hops.scatter(own, oth), 5) if hops.swaps else Still((own, oth))

    g_u, g_d = summing(*sent[:2]), summing(*sent[2:])
    g_u.step()
    g_d.step()
    grads = attn_back_call(starts, queries, keys, values, grad_ctx, 0)
    grads, queries = after((grads, queries), g_u, g_d)
    g_u.step()
    grads = attn_back_call(starts, queries, keys, values, grad_ctx, 1, grads)
    grads, queries = after((grads, queries), g_u)
    g_u.step()
    g_d.step()
    grads = attn_back_call(starts, queries, keys, values, grad_ctx, 2, grads)
    dq, dk, dv = after(grads, g_u, g_d)
    g_u.step()
    g_d.step()
    g_q = qkv_weight_call(tab, normed, dq, dk, dv)
    g_q, dk, dv = after((g_q, dk, dv), g_u, g_d)
    g_q = summing(*g_q)
    g_q.step()
    g_d.step()
    given = jnp.concatenate(
        [
            sums,
            g_up_bias.reshape(n_dev, 4, rd).transpose(1, 0, 2).reshape(4, feature),
            jnp.zeros((20, feature), F32),
        ],
        axis=0,
    )
    back_yc, given = qkv_back_call(tab, (tok_yc,), 3, dk, dv, w_qkv, ptab, given)
    far = hops.swap_core(back_yc)
    dk, dv = after((dk, dv), g_q)
    g_q.step()
    back_y, given = qkv_back_call(tab, (tok_y,), 2, dk, dv, w_qkv, ptab, given)
    far, dk, dv, back_y = after((far, dk, dv, back_y), g_d)
    far = hops.swap_y((back_y.astype(F32) + far.astype(F32)).astype(BF16))
    back, _, g_small = qkv_back_call(
        tab, (tok, tok_c), 0, dk, dv, w_qkv, ptab, given, (dq, grad_mid)
    )
    back, g_small = after((back, g_small), g_q)
    g_s = summing(g_small[0], g_small[1])
    near = hops.swap_core(back[group:])
    g_s.step(3)
    g_q.step()
    if hops.swaps:
        g_q = Chain(hops.last_sums([jnp.concatenate(p, axis=1) for p in zip(g_q.at, g_s.at)]), 2)
    else:
        g_q = Still(tuple(jnp.concatenate(p, axis=1) for p in zip(g_q.at, g_s.at)))
    g_q.step()
    far, near = after((far, near), g_q)
    input_grad = grad_mid + back[:group].astype(F32) + near.astype(F32) + far.astype(F32)
    g_q, g_u, g_d = g_q.end(), g_u.end(), g_d.end()

    if hops.swaps:

        def rows_of(k):
            down = g_d[:, k * (times // 2) * seg : (k + 1) * (times // 2) * seg]
            part = slice(k * rd, (k + 1) * rd)
            return jnp.concatenate(
                [g_q[part], g_u[part], down[:rd], down[rd:]], axis=1
            )

        mine, other = hops.own_other(rows_of(0), rows_of(1))
        got = hops.swap_core(other.astype(BF16)).astype(F32)
        left, right = hops.sides(mine, got)
        down = [
            under_rows(
                jnp.concatenate([x[:, n_all : n_all + 2 * seg], x[:, n_all + 2 * seg :]], axis=0), 2
            )
            for x in (left, right)
        ]
        grad_down = jnp.concatenate(down, axis=1)
    else:

        def scattered(x):
            return lax.psum_scatter(x, BOTH, scatter_dimension=0, tiled=True)

        left, right = [
            jnp.concatenate(parts, axis=1).astype(F32)
            for parts in zip(*[hops.sides(*g) for g in (g_q, g_u, g_d)])
        ]
        down = [
            x[:, n_all:].reshape(CHIPS, -1, times, seg).transpose(0, 2, 1, 3).reshape(ff, seg)
            for x in (left, right)
        ]
        grad_down = scattered(jnp.concatenate(down, axis=1))
        left, right = scattered(left[:, :n_all]), scattered(right[:, :n_all])

    vecs = left[:, 3 * seg : 3 * seg + 128]
    grad_qkv = jnp.concatenate(
        [x[:, n * seg : (n + 1) * seg] for n in range(3) for x in (left, right)], axis=1
    )
    grad_up = jnp.concatenate([x[:, wide_q : wide_q + n_up] for x in (left, right)], axis=1)
    grad_out = jnp.concatenate([x[:, wide_q + n_up : n_all] for x in (left, right)], axis=1)
    return (
        mixed.reshape(tokens.shape),
        input_grad.astype(BF16).reshape(tokens.shape),
        vecs[:, 0],
        vecs[:, 1],
        grad_qkv,
        vecs[:, 2],
        vecs[:, 3],
        grad_out,
        vecs[:, 4],
        vecs[:, 5],
        vecs[:, 6],
        grad_up,
        vecs[:, 8:12].T.reshape(4 * rd),
        grad_down,
        vecs[:, 7],
        vecs[:, 16 : 16 + FREQS],
    )


def solution(mesh):
    rows = P(BOTH)
    mat = P(BOTH, None)
    act = P("seq", "freq", None)
    in_specs = (
        act, P("seq", "freq"), P("seq", None), act,
        rows, rows, mat, rows, rows, mat, rows, rows, rows, mat, rows, mat, rows, mat,
    )
    out_specs = (
        act, act, rows, rows, mat, rows, rows, mat, rows, rows, rows, mat, rows, mat, rows, mat,
    )
    body = functools.partial(local, n_seq=mesh.shape["seq"], n_freq=mesh.shape["freq"])
    return jax.shard_map(body, mesh=mesh, in_specs=in_specs, out_specs=out_specs, check_vma=False)
```

```python
import functools

import jax
import jax.numpy as jnp
import numpy as np
from jax import lax
from jax.experimental import pallas as pl
from jax.experimental.pallas import tpu as pltpu
from jax.sharding import PartitionSpec as P

HEADS = 12
HEAD_DIM = 64
FREQS = 12
CLIPS = 8
WIN = 128
LARGE = 160
CHIPS = 16
EPS = 1e-06
MASKED = -1e30
BOTH = ("seq", "freq")
F32 = jnp.float32
BF16 = jnp.bfloat16
VMEM_LIMIT = 60 * 1024 * 1024


def params(**kw):
    return pltpu.CompilerParams(vmem_limit_bytes=VMEM_LIMIT, **kw)


def whole():
    return pl.BlockSpec(memory_space=pltpu.VMEM)


def smem():
    return pl.BlockSpec(memory_space=pltpu.SMEM)


def hbm():
    return pl.BlockSpec(memory_space=pl.ANY)


def once(shape):
    return pl.BlockSpec(shape, lambda *_: (0,) * len(shape), pipeline_mode=pl.Buffered(1))


def mm(a, b):
    return jnp.dot(a, b, preferred_element_type=F32)


def mm_nt(a, b):
    return lax.dot_general(a, b, (((1,), (1,)), ((), ())), preferred_element_type=F32)


def mm_tn(a, b):
    return lax.dot_general(a, b, (((0,), (0,)), ((), ())), preferred_element_type=F32)


def norm_stats(values):
    center = values - jnp.mean(values, axis=-1, keepdims=True)
    spread = jnp.mean(center * center, axis=-1, keepdims=True)
    inv = lax.rsqrt(spread + EPS)
    return center * inv, inv


def norm_back(vhat, inv, dy, gain):
    gd = dy * gain
    return inv * (
        gd
        - jnp.mean(gd, axis=-1, keepdims=True)
        - vhat * jnp.mean(gd * vhat, axis=-1, keepdims=True)
    )


def row_sum(values):
    return jnp.sum(values, axis=0, keepdims=True)


def embed(tokens, ids, n, ptab):
    count = tokens.shape[0]
    each = count // 128
    pick = lax.broadcasted_iota(jnp.int32, (16, 128), 0)
    wide = ids[:, :128].astype(F32)
    mine = jnp.concatenate(
        [
            jnp.sum(jnp.where(pick == n * each + i, wide, 0.0), axis=0, keepdims=True)
            for i in range(each)
        ],
        axis=1,
    ).astype(jnp.int32)
    row = lax.broadcasted_iota(jnp.int32, (16, count), 0)
    hot = (row == mine).astype(BF16)
    return tokens.astype(F32) + mm_tn(hot, ptab[16:32, :].astype(BF16)), hot


def qkv_kernel(
    tab, t0, t1, t2, t3, i0, i1, i2, i3, own, oth,
    normed, keys, values, queries, hidden, weight, ptab, pm, low0, low1, sems, pm_sems
):
    step = pl.program_id(0)
    feature = weight.shape[0]
    block = feature // CHIPS
    seg = feature // 2
    core = tab[4, 0]
    per = t0.shape[0]

    def copies(cc, vectors):
        made, first = [], []
        for r in range(CHIPS):
            for half, ref in ((cc, own), (1 - cc, oth)):
                dst = pl.multiple_of(tab[0 if half == cc else 1, r] * block, 16)
                for n in range(0 if vectors else 3):
                    made.append(
                        pltpu.make_async_copy(
                            ref.at[pl.ds(r * block, block), pl.ds(n * seg, seg)],
                            weight.at[
                                pl.ds(dst, block), pl.ds(n * feature + half * seg, seg)
                            ],
                            sems.at[len(made)],
                        )
                    )
            if vectors:
                first.append(
                    pltpu.make_async_copy(
                        own.at[pl.ds(r * block, block), pl.ds(3 * seg, 128)],
                        pm.at[pl.ds(pl.multiple_of(tab[0, r] * block, 16), block), :],
                        pm_sems.at[len(first)],
                    )
                )
        return first if vectors else made

    def on_core(run):
        for cc in (0, 1):

            @pl.when(core == cc)
            def _():
                run(cc)

    def prepare(low):
        tile = jnp.minimum(step, pl.num_programs(0) - 2)
        for piece, (tok, ids) in enumerate(((t0, i0), (t1, i1), (t2, i2), (t3, i3))):
            value, _ = embed(tok[...], ids[...], tile, ptab)
            vhat, _ = norm_stats(value)
            line = (vhat * ptab[0:1, :] + ptab[1:2, :]).astype(BF16)
            normed[piece] = line
            low[piece * per : (piece + 1) * per, :] = line
            if piece == 0:
                hidden[...] = value

    def multiply(low):
        q = mm(low[0:per, :], weight[:, 0:feature]) + ptab[2:3, :]
        queries[...] = q.astype(BF16) * jnp.asarray(HEAD_DIM**-0.5, BF16)
        k = mm(low[...], weight[:, feature : 2 * feature]).astype(BF16)
        v = (mm(low[...], weight[:, 2 * feature :]) + ptab[3:4, :]).astype(BF16)
        for piece in range(4):
            rows = slice(piece * per, (piece + 1) * per)
            keys[piece] = k[rows]
            values[piece] = v[rows]

    @pl.when(step == 0)
    def _():
        def begin(cc):
            first = copies(cc, True)
            for one in first + copies(cc, False):
                one.start()
            for one in first:
                one.wait()

        on_core(begin)
        ptab[...] = pm[...].astype(F32).T[:32, :]
        prepare(low0)

        def finish(cc):
            for one in copies(cc, False):
                one.wait()

        on_core(finish)

    for parity, (before, now) in enumerate(((low1, low0), (low0, low1))):

        @pl.when((step > 0) & (lax.rem(step, 2) == parity))
        def _():
            multiply(before)
            prepare(now)


def qkv_call(tab, pieces, own, oth):
    feature = pieces[0].shape[1]
    group = pieces[0].shape[0] - 16
    per = 128
    steps = group // per
    tok = pl.BlockSpec((per, feature), lambda i: (jnp.minimum(i, steps - 1), 0))
    ids = pl.BlockSpec((16, feature), lambda i: (group // 16, 0))
    now = pl.BlockSpec((4, per, feature), lambda i: (0, jnp.minimum(i, steps - 1), 0))
    before = pl.BlockSpec((4, per, feature), lambda i: (0, jnp.maximum(i - 1, 0), 0))
    out = pl.pallas_call(
        qkv_kernel,
        grid=(steps + 1,),
        in_specs=[smem()] + [tok] * 4 + [ids] * 4 + [hbm(), hbm()],
        out_specs=[
            now,
            before,
            before,
            pl.BlockSpec((per, feature), lambda i: (jnp.maximum(i - 1, 0), 0)),
            tok,
            once((feature, 3 * feature)),
            once((32, feature)),
        ],
        out_shape=[
            jax.ShapeDtypeStruct((4, group, feature), BF16),
            jax.ShapeDtypeStruct((4, group, feature), BF16),
            jax.ShapeDtypeStruct((4, group, feature), BF16),
            jax.ShapeDtypeStruct((group, feature), BF16),
            jax.ShapeDtypeStruct((group, feature), F32),
            jax.ShapeDtypeStruct((feature, 3 * feature), BF16),
            jax.ShapeDtypeStruct((32, feature), F32),
        ],
        scratch_shapes=[
            pltpu.VMEM((feature, 128), BF16),
            pltpu.VMEM((4 * per, feature), BF16),
            pltpu.VMEM((4 * per, feature), BF16),
            pltpu.SemaphoreType.DMA((6 * CHIPS,)),
            pltpu.SemaphoreType.DMA((CHIPS,)),
        ],
        compiler_params=params(),
        cost_estimate=pl.CostEstimate(
            flops=2 * group * feature * feature * 9, bytes_accessed=30_000_000, transcendentals=0
        ),
        name="qkv",
    )(tab, *pieces, *pieces, own, oth)
    return [x.reshape(4 * group, feature) for x in out[:3]] + list(out[3:])


def window(starts, g, clip, n, group, win=WIN):
    first = starts[g * 16 + clip]
    last = starts[g * 16 + clip + 1]
    lead = (first // 16) * 16 + n * win
    base = pl.multiple_of(jnp.minimum(lead, group - win), 16)
    return base, jnp.maximum(first, lead) - base, last - base


def counts(starts, clip, groups, win=WIN):
    def need(g):
        first = (starts[g * 16 + clip] // 16) * 16
        return (starts[g * 16 + clip + 1] - first + win - 1) // win

    spans = [need(g) for g in groups]
    most = spans[0]
    for s in spans[1:]:
        most = jnp.maximum(most, s)
    return most


def each_clip(starts, one, many):
    together = 4
    for start in range(0, CLIPS, together):
        clips = range(start, start + together)

        def most(win):
            steps = [counts(starts, clip, range(4), win) for clip in clips]
            return functools.reduce(jnp.maximum, steps)

        fits, fits_large = most(WIN) <= 1, most(LARGE) <= 1

        @pl.when(fits)
        def _():
            for clip in clips:
                one(clip, WIN)

        @pl.when(jnp.logical_not(fits) & fits_large)
        def _():
            for clip in clips:
                one(clip, LARGE)

        @pl.when(jnp.logical_not(fits_large))
        def _():
            @pl.loop(0, together)
            def _(i):
                clip = start + i
                many(clip, counts(starts, clip, [0]), counts(starts, clip, range(4)))


def lane_halves():
    lane = lax.broadcasted_iota(jnp.int32, (1, 128), 1)
    left = (lane < HEAD_DIM).astype(BF16)
    return left, 1 - left


def stack_heads(rows):
    left, right = lane_halves()
    return jnp.concatenate([rows * left, rows * right], axis=0)


def merge_heads(stacked):
    win = stacked.shape[0] // 2
    lane = lax.broadcasted_iota(jnp.int32, (win, 128), 1)
    return jnp.where(lane < HEAD_DIM, stacked[:win], stacked[win:])


def row_valid(lo, hi, win=WIN):
    row = lax.broadcasted_iota(jnp.int32, (win, 128), 0)
    return (row >= lo) & (row < hi)


def load_keys(starts, clip, n, group, *refs, win=WIN):
    tiles = [[] for _ in refs]
    spans = []
    for g in range(4):
        base, lo, hi = window(starts, g, clip, n, group, win)
        for t, ref in zip(tiles, refs):
            t.append(ref[pl.ds(pl.multiple_of(g * group + base, 16), win), :])
        spans.append((base, lo, hi))
    return [jnp.concatenate(t, axis=0) for t in tiles], spans


def key_bias_row(spans, win=WIN):
    lane = lax.broadcasted_iota(jnp.int32, (1, 4 * win), 1)
    valid = [
        (lane >= lo + g * win) & (lane < jnp.minimum(hi, win) + g * win)
        for g, (_, lo, hi) in enumerate(spans)
    ]
    return jnp.where(valid[0] | valid[1] | valid[2] | valid[3], 0.0, MASKED)


def key_bias_col(spans, win=WIN):
    row = lax.broadcasted_iota(jnp.int32, (win, 2 * win), 0)
    return jnp.concatenate(
        [jnp.where((row >= lo) & (row < hi), 0.0, MASKED) for _, lo, hi in spans], axis=0
    )


def attn_kernel(starts, q, k, v, *rest, group):
    out, logs = rest[-2:]

    def one(clip, win):
        base, lo, hi = window(starts, 0, clip, 0, group, win)
        stacked = stack_heads(q[pl.ds(base, win), :])
        (kt, vt), spans = load_keys(starts, clip, 0, group, k, v, win=win)
        scores = mm_nt(stacked, kt) + key_bias_row(spans, win)
        peak = jnp.max(scores, axis=1, keepdims=True)
        e = jnp.exp(scores - peak).astype(BF16)
        o = mm(e, jnp.concatenate([vt, jnp.ones((4 * win, 128), BF16)], axis=1))
        total = o[:, 128:]
        logs[0, clip : clip + 1, 0 : 2 * win] = (peak + jnp.log(total)).T[:1]
        o = o[:, :128] * (1.0 / total)
        spot = pl.ds(base, win)
        out[spot, :] = jnp.where(row_valid(lo, hi, win), merge_heads(o).astype(BF16), out[spot, :])

    def many(clip, rows, steps):
        @pl.loop(0, rows)
        def _(i):
            base, lo, hi = window(starts, 0, clip, i, group)
            stacked = stack_heads(q[pl.ds(base, WIN), :])

            def inner(j, carry):
                peak, total, acc = carry
                (kt, vt), spans = load_keys(starts, clip, j, group, k, v)
                scores = mm_nt(stacked, kt) + key_bias_row(spans)
                new = jnp.maximum(peak, jnp.max(scores, axis=1, keepdims=True))
                e = jnp.exp(scores - new)
                shrink = jnp.exp(peak - new)
                return (
                    new,
                    total * shrink + jnp.sum(e, axis=1, keepdims=True),
                    acc * shrink + mm(e.astype(BF16), vt),
                )

            start = (
                jnp.full((2 * WIN, 1), 2 * MASKED, F32),
                jnp.zeros((2 * WIN, 1), F32),
                jnp.zeros((2 * WIN, 128), F32),
            )
            _, total, acc = lax.fori_loop(0, steps, inner, start)
            o = merge_heads(acc * (1.0 / total)).astype(BF16)
            spot = pl.ds(base, WIN)
            out[spot, :] = jnp.where(row_valid(lo, hi), o, out[spot, :])

    each_clip(starts, one, many)


def attn_call(starts, queries, keys, values, part, before=()):
    group, feature = queries.shape
    pairs = feature // 384
    small = pl.BlockSpec((group, 128), lambda i: (0, i + part * pairs))
    large = pl.BlockSpec((4 * group, 128), lambda i: (0, i + part * pairs))
    logs = pl.BlockSpec((1, CLIPS, 384), lambda i: (i + part * pairs, 0, 0))
    return pl.pallas_call(
        functools.partial(attn_kernel, group=group),
        grid=(pairs,),
        in_specs=[smem(), small, large, large] + [hbm()] * len(before),
        out_specs=[small, logs],
        out_shape=[
            jax.ShapeDtypeStruct((group, feature), BF16),
            jax.ShapeDtypeStruct((feature // 128, CLIPS, 384), F32),
        ],
        input_output_aliases={4 + n: n for n in range(len(before))},
        compiler_params=params(),
        cost_estimate=pl.CostEstimate(
            flops=10_000_000_000, bytes_accessed=12_000_000, transcendentals=6_300_000
        ),
        name="attention",
    )(starts, queries, keys, values, *before)


def attn_back_kernel(starts, q, k, v, go, ctx, logs, *rest, group):
    dq, dk, dv, dk_acc, dv_acc, dq_acc = rest[-6:]
    dk_acc[...] = jnp.zeros_like(dk_acc)
    dv_acc[...] = jnp.zeros_like(dv_acc)
    dq_acc[...] = jnp.zeros_like(dq_acc)
    scale = HEAD_DIM**-0.5

    def load_query(clip, i, win=WIN):
        base, lo, hi = window(starts, 0, clip, i, group, win)
        spot = pl.ds(base, win)
        keep = jnp.where(row_valid(lo, hi, win), go[spot, :], jnp.zeros((), BF16))
        return base, stack_heads(q[spot, :]), stack_heads(keep)

    def finish(spans, base, kt, stacked, back, prob, ds, win=WIN):
        ds = ds.astype(BF16)
        dvt = mm(prob.astype(BF16), back)
        dkt = mm(ds, stacked)
        for g, (kb, _, _) in enumerate(spans):
            spot = pl.ds(pl.multiple_of(g * group + kb, 16), win)
            dk_acc[spot, :] += dkt[g * win : (g + 1) * win]
            dv_acc[spot, :] += dvt[g * win : (g + 1) * win]
        spot = pl.ds(base, win)
        dq_acc[spot, :] += merge_heads(mm_tn(ds, kt))

    def one(clip, win):
        base, stacked, back = load_query(clip, 0, win)
        (kt, vt), spans = load_keys(starts, clip, 0, group, k, v, win=win)
        prob = jnp.exp(
            mm_nt(kt, stacked)
            + key_bias_col(spans, win)
            - logs[0, clip : clip + 1, 0 : 2 * win]
        )
        gp = mm_nt(vt, back)
        spot = pl.ds(base, win)
        both = (stack_heads(ctx[spot, :]).astype(F32) * back.astype(F32)).astype(BF16)
        inner = mm_nt(jnp.ones((8, 128), BF16), both)[:1]
        finish(spans, base, kt, stacked, back, prob, prob * (gp - inner), win)

    def many(clip, rows, steps):
        @pl.loop(0, rows)
        def _(i):
            base, stacked, back = load_query(clip, i)

            def totals(j, carry):
                peak, total, inner = carry
                (kt, vt), spans = load_keys(starts, clip, j, group, k, v)
                scores = mm_nt(kt, stacked) + key_bias_col(spans)
                new = jnp.maximum(peak, jnp.max(scores, axis=0, keepdims=True))
                e = jnp.exp(scores - new)
                shrink = jnp.exp(peak - new)
                gp = mm_nt(vt, back)
                return (
                    new,
                    total * shrink + jnp.sum(e, axis=0, keepdims=True),
                    inner * shrink + jnp.sum(e * gp, axis=0, keepdims=True),
                )

            zero = jnp.zeros((1, 2 * WIN), F32)
            peak, total, inner = lax.fori_loop(
                0, steps, totals, (jnp.full((1, 2 * WIN), 2 * MASKED, F32), zero, zero)
            )
            part = 1.0 / total
            inner = inner * part

            @pl.loop(0, steps)
            def _(j):
                (kt, vt), spans = load_keys(starts, clip, j, group, k, v)
                scores = mm_nt(kt, stacked) + key_bias_col(spans)
                prob = jnp.exp(scores - peak) * part
                gp = mm_nt(vt, back)
                finish(spans, base, kt, stacked, back, prob, prob * (gp - inner))

    each_clip(starts, one, many)

    dq[...] = (dq_acc[...] * scale).astype(BF16)
    dk[...] = dk_acc[...].astype(BF16)
    dv[...] = dv_acc[...].astype(BF16)


def attn_back_call(starts, queries, keys, values, grad_context, context, logs, part, before=()):
    group, feature = queries.shape
    pairs = feature // 384
    small = pl.BlockSpec((group, 128), lambda i: (0, i + part * pairs))
    large = pl.BlockSpec((4 * group, 128), lambda i: (0, i + part * pairs))
    return pl.pallas_call(
        functools.partial(attn_back_kernel, group=group),
        grid=(pairs,),
        in_specs=[smem(), small, large, large, small, small]
        + [pl.BlockSpec((1, CLIPS, 384), lambda i: (i + part * pairs, 0, 0))]
        + [hbm()] * len(before),
        out_specs=[small, large, large],
        out_shape=[
            jax.ShapeDtypeStruct((group, feature), BF16),
            jax.ShapeDtypeStruct((4 * group, feature), BF16),
            jax.ShapeDtypeStruct((4 * group, feature), BF16),
        ],
        input_output_aliases={7 + n: n for n in range(len(before))},
        scratch_shapes=[
            pltpu.VMEM((4 * group, 128), F32),
            pltpu.VMEM((4 * group, 128), F32),
            pltpu.VMEM((group, 128), F32),
        ],
        compiler_params=params(),
        cost_estimate=pl.CostEstimate(
            flops=20_000_000_000, bytes_accessed=24_000_000, transcendentals=6_300_000
        ),
        name="attention_back",
    )(starts, queries, keys, values, grad_context, context, logs, *before)


def phi_parts(u):
    x = jnp.abs(u) * (0.5**0.5)
    t = 1.0 / (1.0 + 0.3275911 * x)
    e = jnp.exp(-(x * x))
    poly = t * (
        0.254829592
        + t * (-0.284496736 + t * (1.421413741 + t * (-1.453152027 + t * 1.061405429)))
    )
    tail = 0.5 * poly * e
    return jnp.where(u < 0, tail, 1.0 - tail), e * 0.3989422804014327


def middle_kernel(
    tab, ctx, hidden, ups, ptab, up_bias, u_own, u_oth, d_own, d_oth,
    mixed, grad_mid, grad_ctx, gu_own, gu_oth, gd_own, gd_oth, small, g_up_bias,
    w_up, w_dn, w_out, mid, sec, sec_t, acc, gsec, act, gup, t_up, t_dn, in_sems, up_sems, dn_sems,
    *, chunks
):
    j = pl.program_id(0)
    group, feature = ctx.shape
    block = feature // CHIPS
    dblock = w_dn.shape[0] // CHIPS
    seg = feature // 2
    part = w_dn.shape[0] // chunks
    per_half = chunks // 2
    core = tab[4, 0]
    tile = 256
    tiles = group // tile

    def loads(cc, part_of):
        made = []
        count = 0

        def add(src, dst, kind):
            nonlocal count
            if kind == part_of:
                made.append(pltpu.make_async_copy(src, dst, in_sems.at[count]))
            count += 1

        for r in range(CHIPS):
            for half, ref, dref, row in ((cc, u_own, d_own, 0), (1 - cc, u_oth, d_oth, 1)):
                chip = tab[row, r]
                dst = pl.ds(pl.multiple_of(chip * block, 16), block)
                src = pl.ds(r * block, block)
                add(
                    ref.at[src, pl.ds(per_half * part, seg)],
                    w_out.at[dst, pl.ds(half * seg, seg)],
                    0,
                )
                for n in range(per_half):
                    add(
                        ref.at[src, pl.ds(n * part, part)],
                        w_up.at[half * per_half + n, dst, :],
                        1,
                    )
                for n in range(dblock // block):
                    row0 = pl.multiple_of(chip * dblock + n * block, 16)
                    add(
                        dref.at[src, pl.ds(n * seg, seg)],
                        w_dn.at[pl.ds(row0, block), pl.ds(half * seg, seg)],
                        1,
                    )
        return made

    def for_core(run):
        for cc in (0, 1):

            @pl.when(core == cc)
            def _():
                run(cc)

    @pl.when(j == 0)
    def _():
        def run(cc):
            first = loads(cc, 0)
            for one in first + loads(cc, 1):
                one.start()
            for one in first:
                one.wait()

        for_core(run)
        for t in range(tiles):
            rows = slice(t * tile, (t + 1) * tile)
            value = hidden[rows, :] + mm(ctx[rows, :], w_out[...]) + ptab[4:5, :]
            mid[rows, :] = value
            vhat, _ = norm_stats(value)
            low = (vhat * ptab[5:6, :] + ptab[6:7, :]).astype(BF16)
            sec[rows, :] = low
            sec_t[:, rows] = low.T
            acc[rows, :] = value + ptab[7:8, :]
            gsec[rows, :] = jnp.zeros((tile, feature), F32)

        def rest(cc):
            for one in loads(cc, 1):
                one.wait()

        for_core(rest)

    slot = lax.rem(j, 2)

    def drain(sl):
        for r in range(CHIPS):
            pltpu.make_async_copy(
                t_up.at[sl, pl.ds(0, block), :],
                gu_own.at[pl.ds(0, block), pl.ds(0, part)],
                up_sems.at[sl, r],
            ).wait()
        for n in range(2 * (part // block)):
            pltpu.make_async_copy(
                t_dn.at[sl, pl.ds(0, block), pl.ds(0, seg)],
                gd_own.at[pl.ds(0, block), pl.ds(0, seg)],
                dn_sems.at[sl, n],
            ).wait()

    upj = w_up[j]
    dnj = w_dn[pl.ds(pl.multiple_of(j * part, 128), part), :]
    bias = up_bias[pl.ds(j, 1), :]
    gub = jnp.zeros((1, part), F32)
    for t in range(tiles):
        rows = slice(t * tile, (t + 1) * tile)
        u = mm(sec[rows, :], upj) + bias
        dist, dens = phi_parts(u)
        a = (u * dist).astype(BF16)
        g = (mm_nt(ups[rows, :], dnj) * (dist + u * dens)).astype(BF16)
        act[rows, :] = a
        gup[rows, :] = g
        gub = gub + row_sum(g.astype(F32))
        acc[rows, :] += mm(a, dnj)
        gsec[rows, :] += mm_nt(g, upj)
    g_up_bias[pl.ds(j, 1), :] = gub

    @pl.when(j >= 2)
    def _():
        drain(slot)

    t_up[slot] = mm(sec_t[...], gup[...]).astype(BF16)
    t_dn[slot] = mm_tn(act[...], ups[...]).astype(BF16)

    def send(cc):
        col = pl.ds(pl.multiple_of(lax.rem(j, per_half) * part, 128), part)
        for is_own in (True, False):
            ref = gu_own if is_own else gu_oth

            @pl.when((j // per_half == cc) == is_own)
            def _():
                for r in range(CHIPS):
                    src = pl.ds(pl.multiple_of(tab[0 if is_own else 1, r] * block, 16), block)
                    pltpu.make_async_copy(
                        t_up.at[slot, src, :],
                        ref.at[pl.ds(r * block, block), col],
                        up_sems.at[slot, r],
                    ).start()

        n = 0
        count = part // dblock
        for half, ref, row in ((cc, gd_own, 2), (1 - cc, gd_oth, 3)):
            for i in range(count):
                place = pl.multiple_of(tab[row, j * count + i] * block, 16)
                for m in range(dblock // block):
                    pltpu.make_async_copy(
                        t_dn.at[
                            slot, pl.ds(i * dblock + m * block, block), pl.ds(half * seg, seg)
                        ],
                        ref.at[pl.ds(place, block), pl.ds(m * seg, seg)],
                        dn_sems.at[slot, n],
                    ).start()
                    n += 1

    for_core(send)

    @pl.when(j == chunks - 1)
    def _():
        s_gain = jnp.zeros((1, feature), F32)
        s_shift = jnp.zeros((1, feature), F32)
        s_out = jnp.zeros((1, feature), F32)
        s_down = jnp.zeros((1, feature), F32)
        for t in range(tiles):
            rows = slice(t * tile, (t + 1) * tile)
            mixed[rows, :] = acc[rows, :].astype(BF16)
            vhat, inv = norm_stats(mid[rows, :])
            dy = gsec[rows, :]
            wide = ups[rows, :].astype(F32)
            gm = wide + norm_back(vhat, inv, dy, ptab[5:6, :])
            grad_mid[rows, :] = gm
            low = gm.astype(BF16)
            gup[rows, :] = low
            grad_ctx[rows, :] = mm_nt(low, w_out[...]).astype(BF16)
            s_gain = s_gain + row_sum(dy * vhat)
            s_shift = s_shift + row_sum(dy)
            s_out = s_out + row_sum(gm)
            s_down = s_down + row_sum(wide)
        zero = jnp.zeros((1, feature), F32)
        small[...] = jnp.concatenate(
            [zero, zero, zero, zero, s_out, s_gain, s_shift, s_down], axis=0
        )
        drain(1 - slot)
        act[...] = mm_tn(ctx[...], gup[...]).astype(BF16)

        def run(cc):
            made = []
            for half, ref, row in ((cc, gu_own, 0), (1 - cc, gu_oth, 1)):
                for r in range(CHIPS):
                    src = pl.ds(pl.multiple_of(tab[row, r] * block, 16), block)
                    made.append(
                        pltpu.make_async_copy(
                            act.at[src, pl.ds(half * seg, seg)],
                            ref.at[pl.ds(r * block, block), pl.ds(per_half * part, seg)],
                            in_sems.at[len(made)],
                        )
                    )
            for one in made:
                one.start()
            for one in made:
                one.wait()

        for_core(run)
        drain(slot)


def middle_call(tab, ctx, hidden, ups, ptab, up_bias, up_pair, down_pair, ff):
    group, feature = hidden.shape
    chunks = ff // feature
    part = ff // chunks
    return pl.pallas_call(
        functools.partial(middle_kernel, chunks=chunks),
        grid=(chunks,),
        in_specs=[
            smem(),
            once((group, feature)),
            once((group, feature)),
            once((group, feature)),
            once((32, feature)),
            once((chunks, part)),
            hbm(), hbm(), hbm(), hbm(),
        ],
        out_specs=[
            once((group, feature)),
            once((group, feature)),
            once((group, feature)),
            hbm(), hbm(), hbm(), hbm(),
            once((8, feature)),
            once((chunks, part)),
        ],
        out_shape=[
            jax.ShapeDtypeStruct((group, feature), BF16),
            jax.ShapeDtypeStruct((group, feature), F32),
            jax.ShapeDtypeStruct((group, feature), BF16),
            jax.ShapeDtypeStruct(up_pair[0].shape, BF16),
            jax.ShapeDtypeStruct(up_pair[0].shape, BF16),
            jax.ShapeDtypeStruct(down_pair[0].shape, BF16),
            jax.ShapeDtypeStruct(down_pair[0].shape, BF16),
            jax.ShapeDtypeStruct((8, feature), F32),
            jax.ShapeDtypeStruct((chunks, part), F32),
        ],
        scratch_shapes=[
            pltpu.VMEM((chunks, feature, part), BF16),
            pltpu.VMEM((ff, feature), BF16),
            pltpu.VMEM((feature, feature), BF16),
            pltpu.VMEM((group, feature), F32),
            pltpu.VMEM((group, feature), BF16),
            pltpu.VMEM((feature, group), BF16),
            pltpu.VMEM((group, feature), F32),
            pltpu.VMEM((group, feature), F32),
            pltpu.VMEM((group, part), BF16),
            pltpu.VMEM((group, part), BF16),
            pltpu.VMEM((2, feature, part), BF16),
            pltpu.VMEM((2, part, feature), BF16),
            pltpu.SemaphoreType.DMA((2 * CHIPS * (1 + chunks // 2 + ff // feature),)),
            pltpu.SemaphoreType.DMA((2, CHIPS)),
            pltpu.SemaphoreType.DMA((2, 2 * CHIPS)),
        ],
        compiler_params=params(),
        cost_estimate=pl.CostEstimate(
            flops=2 * group * feature * (3 * feature + 6 * ff),
            bytes_accessed=34_000_000,
            transcendentals=2 * group * ff,
        ),
        name="middle",
    )(tab, ctx, hidden, ups, ptab, up_bias, *up_pair, *down_pair)


def qkv_weight_kernel(tab, normed, dq, dk, dv, own, oth, norm_t, tmp, sems, *, blocks):
    step = pl.program_id(0)
    total, feature = normed.shape
    group = dq.shape[0]
    block = feature // CHIPS
    seg = feature // 2
    core = tab[4, 0]

    def stores(cc, n):
        made = []
        for half, ref, row in ((cc, own, 0), (1 - cc, oth, 1)):
            for r in range(CHIPS):
                src = pl.ds(pl.multiple_of(tab[row, r] * block, 16), block)
                made.append(
                    pltpu.make_async_copy(
                        tmp.at[n, src, pl.ds(half * seg, seg)],
                        ref.at[pl.ds(r * block, block), pl.ds(n * seg, seg)],
                        sems.at[n, len(made)],
                    )
                )
        return made

    def on_core(run):
        for cc in (0, 1):

            @pl.when(core == cc)
            def _():
                run(cc)

    def start(n):
        def run(cc):
            for one in stores(cc, n):
                one.start()

        on_core(run)

    @pl.when(step == 0)
    def _():
        tile = 256
        for t in range(total // tile):
            rows = slice(t * tile, (t + 1) * tile)
            norm_t[:, rows] = normed[rows, :].T
        tmp[0] = mm(norm_t[:, :group], dq[...]).astype(BF16)
        start(0)

    cut = feature // blocks
    for n, ref in ((1, dk), (2, dv)):
        for i in range(blocks):

            @pl.when(step == 1 + (n - 1) * blocks + i)
            def _():
                tmp[n, :, i * cut : (i + 1) * cut] = mm(norm_t[...], ref[...]).astype(BF16)
                if i == blocks - 1:
                    start(n)

    @pl.when(step == 2 * blocks)
    def _():
        def finish(cc):
            for n in range(3):
                for one in stores(cc, n):
                    one.wait()

        on_core(finish)


def qkv_weight_call(tab, normed, dq, dk, dv):
    total, feature = normed.shape
    half = 3 * feature // 2
    blocks = 3
    cut = feature // blocks
    return pl.pallas_call(
        functools.partial(qkv_weight_kernel, blocks=blocks),
        grid=(1 + 2 * blocks,),
        in_specs=[
            smem(),
            once(normed.shape),
            once(dq.shape),
            pl.BlockSpec((total, cut), lambda i: (0, jnp.clip(i - 1, 0, blocks - 1))),
            pl.BlockSpec((total, cut), lambda i: (0, jnp.clip(i - 1 - blocks, 0, blocks - 1))),
        ],
        out_specs=[hbm(), hbm()],
        out_shape=[jax.ShapeDtypeStruct((feature, half), BF16)] * 2,
        scratch_shapes=[
            pltpu.VMEM((feature, total), BF16),
            pltpu.VMEM((3, feature, feature), BF16),
            pltpu.SemaphoreType.DMA((3, 2 * CHIPS)),
        ],
        compiler_params=params(),
        cost_estimate=pl.CostEstimate(
            flops=2 * dq.shape[0] * feature * feature * 9,
            bytes_accessed=20_000_000,
            transcendentals=0,
        ),
        name="qkv_weight",
    )(tab, normed, dq, dk, dv)


def qkv_back_kernel(*refs, group, own_rows):
    tab, refs = refs[0], refs[1:]
    n_pieces = 2 if own_rows else 1
    toks, idss, refs = refs[:n_pieces], refs[n_pieces : 2 * n_pieces], refs[2 * n_pieces :]
    dk, dv, weight, ptab, given = refs[:5]
    refs = refs[5:]
    if own_rows:
        dq, gm, out, sums, small, moved, sems = refs
    else:
        out, sums = refs
    step = pl.program_id(0)
    feature = weight.shape[0]
    steps = group // out.shape[0]

    @pl.when(step == 0)
    def _():
        sums[...] = given[...]

    def body(tok, ids, own):
        value, hot = embed(tok[...], ids[...], lax.rem(step, steps), ptab)
        vhat, inv = norm_stats(value)
        dy = mm_nt(dk[...], weight[:, feature : 2 * feature]) + mm_nt(
            dv[...], weight[:, 2 * feature :]
        )
        if own:
            dy = dy + mm_nt(dq[...], weight[:, 0:feature])
            sums[2:3, :] += row_sum(dq[...].astype(F32))
        grad = norm_back(vhat, inv, dy, ptab[0:1, :])
        out[...] = grad.astype(BF16)
        sums[0:1, :] += row_sum(dy * vhat)
        sums[1:2, :] += row_sum(dy)
        sums[3:4, :] += row_sum(dv[...].astype(F32))
        if own:
            grad = grad + gm[...]
        high = grad.astype(BF16)
        rest = (grad - high.astype(F32)).astype(BF16)
        sums[16:32, :] += mm(hot, high) + mm(hot, rest)

    if own_rows:

        @pl.when(step < steps)
        def _():
            body(toks[0], idss[0], True)

        @pl.when(step >= steps)
        def _():
            body(toks[1], idss[1], False)

    else:
        body(toks[0], idss[0], False)

    if own_rows:

        @pl.when(step == 2 * steps - 1)
        def _():
            turned = jnp.concatenate([sums[...], jnp.zeros((96, feature), F32)], axis=0).T
            moved[...] = turned.astype(BF16)
            block = feature // CHIPS
            made = []
            for side in range(2):
                for r in range(CHIPS):
                    src = pl.ds(pl.multiple_of(tab[side, r] * block, 16), block)
                    made.append(
                        pltpu.make_async_copy(
                            moved.at[src, :],
                            small.at[side, pl.ds(r * block, block), :],
                            sems.at[side, r],
                        )
                    )
            for one in made:
                one.start()
            for one in made:
                one.wait()


def qkv_back_call(tab, pair, first_piece, dk, dv, weight, ptab, given, own=()):
    feature = dk.shape[1]
    group = pair[0].shape[0] - 16
    per = 256
    steps = group // per
    skip = first_piece * steps
    count = len(pair)

    def at(piece):
        return pl.BlockSpec(
            (per, feature), lambda i: (jnp.clip(i - piece * steps, 0, steps - 1), 0)
        )

    ids = pl.BlockSpec((16, feature), lambda i: (group // 16, 0))
    tile = pl.BlockSpec((per, feature), lambda i: (i, 0))
    later = pl.BlockSpec((per, feature), lambda i: (i + skip, 0))
    first = pl.BlockSpec((per, feature), lambda i: (jnp.minimum(i, steps - 1), 0))
    return pl.pallas_call(
        functools.partial(qkv_back_kernel, group=group, own_rows=bool(own)),
        grid=(count * steps,),
        in_specs=[smem()]
        + [at(n) for n in range(count)]
        + [ids] * count
        + [later, later]
        + [once((feature, 3 * feature)), once((32, feature)), once((32, feature))]
        + [first] * len(own),
        out_specs=[tile, once((32, feature))] + [hbm()] * bool(own),
        out_shape=[
            jax.ShapeDtypeStruct((count * group, feature), BF16),
            jax.ShapeDtypeStruct((32, feature), F32),
            jax.ShapeDtypeStruct((2, feature, 128), BF16),
        ][: 2 + bool(own)],
        scratch_shapes=[pltpu.VMEM((feature, 128), BF16), pltpu.SemaphoreType.DMA((2, CHIPS))][
            : 2 * bool(own)
        ],
        compiler_params=params(),
        cost_estimate=pl.CostEstimate(
            flops=group * feature * feature * 9, bytes_accessed=15_000_000, transcendentals=0
        ),
        name="qkv_back",
    )(tab, *pair, *pair, dk, dv, weight, ptab, given, *own)


def payload_kernel(tab, *refs, rd, times):
    vecs, (up_bias, table, qkv, up, out, down, mine, other, lines) = refs[:8], refs[8:]
    feature = down.shape[1]
    seg = feature // 2
    ff = up.shape[1]
    core = tab[4, 0]
    lines[...] = jnp.zeros_like(lines)
    for n, vec in enumerate(vecs):
        lines[n : n + 1, 0:rd] = vec[...].astype(F32)
    for n in range(4):
        lines[8 + n : 9 + n, 0:rd] = up_bias[:, n * rd : (n + 1) * rd].astype(F32)

    def places(rows, first):
        row = lax.broadcasted_iota(jnp.int32, (rows, 128), 0)
        return (lax.broadcasted_iota(jnp.int32, (rows, 128), 1) == row + first).astype(BF16)

    small = mm_tn(lines[...].astype(BF16), places(16, 0))[:rd] + mm(table[...], places(FREQS, 16))
    small = small.astype(BF16)
    wide = down[...].astype(F32)

    def fill(ref, h):
        at = 0

        def put(value):
            nonlocal at
            ref[:, at : at + value.shape[1]] = value
            at += value.shape[1]

        for n in range(3):
            put(qkv[:, n * feature + h * seg : n * feature + (h + 1) * seg])
        put(small)
        put(up[:, h * (ff // 2) : (h + 1) * (ff // 2)])
        put(out[:, h * seg : (h + 1) * seg])
        for n in range(times):
            put(wide[n * rd : (n + 1) * rd, h * seg : (h + 1) * seg].astype(BF16))

    for cc in (0, 1):

        @pl.when(core == cc)
        def _():
            fill(mine, cc)
            fill(other, 1 - cc)


def payload_call(tab, vecs, up_bias, table, qkv, up, out, down):
    rd, times = qkv.shape[0], down.shape[0] // qkv.shape[0]
    half = (qkv.shape[1] + up.shape[1] + out.shape[1] + times * down.shape[1]) // 2 + 128
    return pl.pallas_call(
        functools.partial(payload_kernel, rd=rd, times=times),
        in_specs=[smem()] + [whole()] * (len(vecs) + 6),
        out_specs=[whole(), whole()],
        out_shape=[jax.ShapeDtypeStruct((rd, half), BF16)] * 2,
        scratch_shapes=[pltpu.VMEM((16, 128), F32)],
        compiler_params=params(),
        name="payload",
    )(tab, *[v.reshape(1, -1) for v in vecs], up_bias.reshape(1, -1), table, qkv, up, out, down)


def pair_kernel(tab, mine, got, for_q, for_u, for_d, *, widths):
    rd = mine.shape[0]
    n_q, n_u, times, seg = widths
    core = tab[4, 0]

    def fill(top, low):
        for ref, start, width in ((for_q, 0, n_q), (for_u, n_q, n_u)):
            cols = slice(start, start + width)
            ref[...] = jnp.concatenate(
                [top[:, cols].astype(F32), low[:, cols].astype(F32)], axis=0
            ).astype(BF16)
        for block in range(times):
            part = top if block < times // 2 else low
            start = n_q + n_u + (block % (times // 2)) * 2 * seg
            rows = [part[:, start + i * seg : start + (i + 1) * seg].astype(F32) for i in (0, 1)]
            for_d[:, block * seg : (block + 1) * seg] = jnp.concatenate(rows, axis=0).astype(BF16)

    for cc in (0, 1):

        @pl.when(core == cc)
        def _():
            fill(*((mine, got) if cc == 0 else (got, mine)))


def pair_call(tab, mine, got, widths):
    rd = mine.shape[0]
    n_q, n_u, times, seg = widths
    return pl.pallas_call(
        functools.partial(pair_kernel, widths=widths),
        in_specs=[smem(), whole(), whole()],
        out_specs=[whole()] * 3,
        out_shape=[jax.ShapeDtypeStruct((2 * rd, n), BF16) for n in (n_q, n_u, times * seg)],
        compiler_params=params(),
        name="pair",
    )(tab, mine, got)


def tail_rows_kernel(tokens, ids, out):
    group, feature = tokens.shape
    out[0:group, :] = tokens[...]
    rows = [ids[:, n * 128 : (n + 1) * 128].astype(F32) for n in range(group // 128)]
    rows = jnp.concatenate(rows + [jnp.zeros((16 - len(rows), 128), F32)], axis=0).astype(BF16)
    out[group : group + 16, :] = jnp.concatenate(
        [rows, jnp.zeros((16, feature - 128), BF16)], axis=1
    )


def tail_rows_call(tokens, ids):
    group, feature = tokens.shape
    return pl.pallas_call(
        tail_rows_kernel,
        in_specs=[whole(), whole()],
        out_specs=whole(),
        out_shape=jax.ShapeDtypeStruct((group + 16, feature), BF16),
        compiler_params=params(),
        name="tail_rows",
    )(tokens, ids)


class Hops:
    def __init__(self, n_seq, n_freq):
        self.n_seq, self.n_freq = n_seq, n_freq
        self.swaps = n_seq == 8 and n_freq == 4
        self.core = lax.axis_index("freq") % 2
        self.first = self.core == 0
        chip = lax.axis_index("seq") * 2 + lax.axis_index("freq") // 2
        if self.swaps:
            bits = ((4, 8, 2, 1), (4, 8, 1, 2))
            masks = np.zeros((2, CHIPS), np.int32)
            for c in (0, 1):
                for r in range(CHIPS):
                    for b in range(4):
                        if r >> b & 1:
                            masks[c, r] ^= bits[c][b]
            one, two = jnp.asarray(masks[0]), jnp.asarray(masks[1])
            mine = jnp.where(self.first, one, two) ^ chip
            theirs = jnp.where(self.first, two, one) ^ chip

            def places(order):
                rows = (order[:, None] == jnp.arange(CHIPS)[None, :]).astype(jnp.int32)
                return jnp.sum(rows * jnp.arange(CHIPS, dtype=jnp.int32)[:, None], axis=0)

            rows = [mine, theirs, places(mine), places(theirs)]
        else:
            rows = [jnp.arange(CHIPS, dtype=jnp.int32)] * 4
        rows = [r.astype(jnp.int32) for r in rows]
        rows += [jnp.full((CHIPS,), self.core, jnp.int32)] + [rows[0]] * 3
        self.table = jnp.stack(rows)

    def swap(self, values, move):
        pairs = []
        for s in range(self.n_seq):
            for f in range(self.n_freq):
                ds, df = move(f % 2)
                pairs.append((s * self.n_freq + f, (s ^ ds) * self.n_freq + (f ^ df)))
        return lax.ppermute(values, BOTH, pairs)

    def swap_core(self, values):
        return self.swap(values, lambda c: (0, 1))

    def swap_y(self, values):
        return self.swap(values, lambda c: (0, 2))

    def swap_z(self, values, n):
        return self.swap(values, lambda c: (2 * n, 0))

    def swap_xy(self, values, n):
        return self.swap(values, lambda c: (1, 0) if c == n else (0, 2))

    def sides(self, mine, other):
        return jnp.where(self.first, mine, other), jnp.where(self.first, other, mine)

    def own_other(self, left, right):
        return jnp.where(self.first, left, right), jnp.where(self.first, right, left)

    def gather(self, held):
        parts = yield [held] + [self.swap_z(held, n) for n in (1, 2, 3)]
        for n in (0, 1):
            held = jnp.concatenate(parts, axis=0)
            parts = yield held, self.swap_xy(held, n)
        held = jnp.concatenate(parts, axis=0)
        yield held, self.swap_core(held)

    def scatter(self, own, other):
        own, got = yield own, self.swap_core(other)
        add = self.add
        for n in (1, 0):
            cut = own.shape[0] // 2
            send = add(own[cut:], got[cut:])
            own = add(own[:cut], got[:cut])
            own, got = yield own, self.swap_xy(send, n)
        yield from self.last_sums((own, got))

    @staticmethod
    def add(a, b):
        return (a.astype(F32) + b.astype(F32)).astype(BF16)

    def last_sums(self, pair):
        own, got = pair
        add = self.add
        cut = own.shape[0] // 4
        sends = [add(own[n * cut : (n + 1) * cut], got[n * cut : (n + 1) * cut]) for n in (1, 2, 3)]
        own = own[:cut].astype(F32) + got[:cut].astype(F32)
        own, got = yield own, [self.swap_z(send, n) for n, send in zip((1, 2, 3), sends)]
        yield own + sum(g.astype(F32) for g in got)


class Chain:
    def __init__(self, steps, count):
        self.steps, self.left, self.at = steps, count, None

    def step(self, times=1):
        for _ in range(times):
            self.at = next(self.steps) if self.at is None else self.steps.send(self.at)
            self.left -= 1
        return self.at

    def end(self):
        return self.step(self.left)


class Still:
    def __init__(self, value):
        self.at = value

    def step(self, times=1):
        return self.at

    end = step


def after(values, *chains):
    values, held = lax.optimization_barrier((values, tuple(c.at for c in chains)))
    for c, h in zip(chains, held):
        c.at = h
    return values


def col_halves(*arrays):
    left = [a[:, : a.shape[1] // 2] for a in arrays]
    right = [a[:, a.shape[1] // 2 :] for a in arrays]
    return left, right


def side_rows(down, count):
    rows, cols = down.shape
    return down.reshape(count, rows // count, cols).transpose(1, 0, 2).reshape(rows // count, -1)


def under_rows(wide, count):
    rows, cols = wide.shape
    return wide.reshape(rows, count, cols // count).transpose(1, 0, 2).reshape(rows * count, -1)


def local(
    tokens,
    freq_ids,
    clip_ids,
    cotangent,
    ln1_gain,
    first_norm_bias,
    qkv_weight,
    q_bias,
    v_bias,
    out_weight,
    out_bias,
    ln2_gain,
    ln2_bias,
    up_weight,
    up_bias,
    down_weight,
    down_bias,
    freq_table,
    *,
    n_seq,
    n_freq,
):
    _, group, feature = tokens.shape
    rd = qkv_weight.shape[0]
    n_dev = n_seq * n_freq
    seg = feature // 2
    ff = up_weight.shape[1]
    times = ff // feature
    hops = Hops(n_seq, n_freq)
    tab = hops.table

    tok = tail_rows_call(tokens.reshape(group, feature), freq_ids.reshape(1, group))
    vectors = [ln1_gain, first_norm_bias, q_bias, v_bias, out_bias, ln2_gain, ln2_bias, down_bias]
    wide_q = 3 * seg + 128
    n_up = ff // 2
    n_uo = n_up + seg
    n_all = wide_q + n_uo
    tok_c, tok_y = hops.swap_core(tok), hops.swap_y(tok)
    if hops.swaps:
        mine, other = payload_call(
            tab, vectors, up_bias, freq_table, qkv_weight, up_weight, out_weight, down_weight
        )
        held = pair_call(tab, mine, hops.swap_core(other), (wide_q, n_uo, times, seg))
        weights, ups, downs = [Chain(hops.gather(h), 4) for h in held]
    else:

        def full(x):
            return lax.all_gather(x, BOTH, axis=0, tiled=True)

        lines = jnp.concatenate(vectors + [up_bias]).reshape(12, rd)
        small = jnp.concatenate(
            [lines, jnp.zeros((4, rd), BF16), freq_table.T, jnp.zeros((100, rd), BF16)], axis=0
        ).T
        f_qkv, f_small, f_up = full(qkv_weight), full(small), full(up_weight)
        f_out, f_down = full(out_weight), full(down_weight)
        q_full = [f_qkv[:, n * feature : (n + 1) * feature] for n in range(3)]
        down_side = f_down.reshape(CHIPS, times, -1, feature).transpose(0, 2, 1, 3)
        down_side = down_side.reshape(feature, times, 2, seg)
        sides_q, sides_u, sides_d = [], [], []
        for h in (0, 1):
            sides_q.append(jnp.concatenate(col_halves(*q_full)[h] + [f_small], axis=1))
            sides_u.append(jnp.concatenate(col_halves(f_up, f_out)[h], axis=1))
            sides_d.append(down_side[:, :, h].reshape(feature, times * seg))
        weights, ups, downs = [
            Still(hops.own_other(*sides)) for sides in (sides_q, sides_u, sides_d)
        ]

    weights.step()
    tok_c = after(tok_c, weights)
    ups.step()
    weights.step()
    tok_y = after(tok_y, weights)
    weights.step()
    tok_yc = hops.swap_core(tok_y)
    tok_c = after(tok_c, weights, ups)
    ups.step()
    downs.step()
    weights.end()
    pieces = (tok, tok_c, tok_y, tok_yc)

    place = lax.axis_index("freq")
    order = jnp.stack([place, place ^ 1, place ^ 2, place ^ 3])
    below = clip_ids.reshape(n_freq, group)[:, None, :] < jnp.arange(16, dtype=jnp.int32)[None, :, None]
    first_rows = jnp.sum(below.astype(jnp.int32), axis=2)
    pick = (order[:, None] == jnp.arange(n_freq)[None, :]).astype(jnp.int32)
    starts = jnp.sum(pick[:, :, None] * first_rows[None, :, :], axis=1).reshape(4 * 16)

    normed, keys, values, queries, hidden, w_qkv, ptab = qkv_call(tab, pieces, *weights.at)
    queries, keys, values = after((queries, keys, values), ups, downs)
    ups.step()
    downs.step()
    context = attn_call(starts, queries, keys, values, 0)
    queries, context = after((queries, context), downs)
    downs.step()
    context = attn_call(starts, queries, keys, values, 1, context)
    queries, context = after((queries, context), ups, downs)
    ups.step()
    downs.step()
    context = attn_call(starts, queries, keys, values, 2, context)
    up_rows = ptab[8:12].reshape(4, n_dev, rd).transpose(1, 0, 2).reshape(times, feature)
    upstream = cotangent.reshape(group, feature)
    context, logs = context
    mixed, grad_mid, grad_ctx, *sent, sums, g_up_bias = middle_call(
        tab, context, hidden, upstream, ptab, up_rows, ups.at, downs.at, ff
    )

    def summing(own, oth):
        return Chain(hops.scatter(own, oth), 5) if hops.swaps else Still((own, oth))

    g_u, g_d = summing(*sent[:2]), summing(*sent[2:])
    g_u.step()
    g_d.step()
    grads = attn_back_call(starts, queries, keys, values, grad_ctx, context, logs, 0)
    grads, queries = after((grads, queries), g_u, g_d)
    g_u.step()
    grads = attn_back_call(starts, queries, keys, values, grad_ctx, context, logs, 1, grads)
    grads, queries = after((grads, queries), g_u, g_d)
    g_d.step()
    grads = attn_back_call(starts, queries, keys, values, grad_ctx, context, logs, 2, grads)
    dq, dk, dv = after(grads, g_u, g_d)
    g_u.step()
    g_d.step()
    g_q = qkv_weight_call(tab, normed, dq, dk, dv)
    g_q, dk, dv = after((g_q, dk, dv), g_u, g_d)
    g_q = summing(*g_q)
    g_q.step()
    g_u.step()
    given = jnp.concatenate(
        [
            sums,
            g_up_bias.reshape(n_dev, 4, rd).transpose(1, 0, 2).reshape(4, feature),
            jnp.zeros((20, feature), F32),
        ],
        axis=0,
    )
    back_yc, given = qkv_back_call(tab, (tok_yc,), 3, dk, dv, w_qkv, ptab, given)
    far = hops.swap_core(back_yc)
    dk, dv = after((dk, dv), g_q)
    g_q.step()
    back_y, given = qkv_back_call(tab, (tok_y,), 2, dk, dv, w_qkv, ptab, given)
    far, dk, dv, back_y = after((far, dk, dv, back_y), g_u, g_d)
    g_d.step()
    far = hops.swap_y((back_y.astype(F32) + far.astype(F32)).astype(BF16))
    back, _, g_small = qkv_back_call(
        tab, (tok, tok_c), 0, dk, dv, w_qkv, ptab, given, (dq, grad_mid)
    )
    back, g_small = after((back, g_small), g_q)
    g_s = summing(g_small[0], g_small[1])
    near = hops.swap_core(back[group:])
    g_s.step(3)
    g_q.step()
    if hops.swaps:
        g_q = Chain(hops.last_sums([jnp.concatenate(p, axis=1) for p in zip(g_q.at, g_s.at)]), 2)
    else:
        g_q = Still(tuple(jnp.concatenate(p, axis=1) for p in zip(g_q.at, g_s.at)))
    g_q.step()
    far, near = after((far, near), g_q)
    input_grad = grad_mid + back[:group].astype(F32) + near.astype(F32) + far.astype(F32)
    g_q, g_u, g_d = g_q.end(), g_u.end(), g_d.end()

    if hops.swaps:

        def rows_of(k):
            down = g_d[:, k * (times // 2) * seg : (k + 1) * (times // 2) * seg]
            part = slice(k * rd, (k + 1) * rd)
            return jnp.concatenate(
                [g_q[part], g_u[part], down[:rd], down[rd:]], axis=1
            )

        mine, other = hops.own_other(rows_of(0), rows_of(1))
        got = hops.swap_core(other.astype(BF16)).astype(F32)
        left, right = hops.sides(mine, got)
        down = [
            under_rows(
                jnp.concatenate([x[:, n_all : n_all + 2 * seg], x[:, n_all + 2 * seg :]], axis=0), 2
            )
            for x in (left, right)
        ]
        grad_down = jnp.concatenate(down, axis=1)
    else:

        def scattered(x):
            return lax.psum_scatter(x, BOTH, scatter_dimension=0, tiled=True)

        left, right = [
            jnp.concatenate(parts, axis=1).astype(F32)
            for parts in zip(*[hops.sides(*g) for g in (g_q, g_u, g_d)])
        ]
        down = [
            x[:, n_all:].reshape(CHIPS, -1, times, seg).transpose(0, 2, 1, 3).reshape(ff, seg)
            for x in (left, right)
        ]
        grad_down = scattered(jnp.concatenate(down, axis=1))
        left, right = scattered(left[:, :n_all]), scattered(right[:, :n_all])

    vecs = left[:, 3 * seg : 3 * seg + 128]
    grad_qkv = jnp.concatenate(
        [x[:, n * seg : (n + 1) * seg] for n in range(3) for x in (left, right)], axis=1
    )
    grad_up = jnp.concatenate([x[:, wide_q : wide_q + n_up] for x in (left, right)], axis=1)
    grad_out = jnp.concatenate([x[:, wide_q + n_up : n_all] for x in (left, right)], axis=1)
    return (
        mixed.reshape(tokens.shape),
        input_grad.astype(BF16).reshape(tokens.shape),
        vecs[:, 0],
        vecs[:, 1],
        grad_qkv,
        vecs[:, 2],
        vecs[:, 3],
        grad_out,
        vecs[:, 4],
        vecs[:, 5],
        vecs[:, 6],
        grad_up,
        vecs[:, 8:12].T.reshape(4 * rd),
        grad_down,
        vecs[:, 7],
        vecs[:, 16 : 16 + FREQS],
    )


def solution(mesh):
    rows = P(BOTH)
    mat = P(BOTH, None)
    act = P("seq", "freq", None)
    in_specs = (
        act, P("seq", "freq"), P("seq", None), act,
        rows, rows, mat, rows, rows, mat, rows, rows, rows, mat, rows, mat, rows, mat,
    )
    out_specs = (
        act, act, rows, rows, mat, rows, rows, mat, rows, rows, rows, mat, rows, mat, rows, mat,
    )
    body = functools.partial(local, n_seq=mesh.shape["seq"], n_freq=mesh.shape["freq"])
    return jax.shard_map(body, mesh=mesh, in_specs=in_specs, out_specs=out_specs, check_vma=False)
```

```python
import functools

import jax
import jax.numpy as jnp
import numpy as np
from jax import lax
from jax.experimental import pallas as pl
from jax.experimental.pallas import tpu as pltpu
from jax.sharding import PartitionSpec as P

HEADS = 12
HEAD_DIM = 64
FREQS = 12
CLIPS = 8
WIN = 128
LARGE = 160
CHIPS = 16
EPS = 1e-06
MASKED = -1e30
BOTH = ("seq", "freq")
F32 = jnp.float32
BF16 = jnp.bfloat16
VMEM_LIMIT = 60 * 1024 * 1024


def params(**kw):
    return pltpu.CompilerParams(vmem_limit_bytes=VMEM_LIMIT, **kw)


def whole():
    return pl.BlockSpec(memory_space=pltpu.VMEM)


def rows_at(parts, r, block):
    each = CHIPS // len(parts)
    return parts[r // each], pl.ds(r % each * block, block)


def smem():
    return pl.BlockSpec(memory_space=pltpu.SMEM)


def hbm():
    return pl.BlockSpec(memory_space=pl.ANY)


def once(shape):
    return pl.BlockSpec(shape, lambda *_: (0,) * len(shape), pipeline_mode=pl.Buffered(1))


def mm(a, b):
    return jnp.dot(a, b, preferred_element_type=F32)


def mm_nt(a, b):
    return lax.dot_general(a, b, (((1,), (1,)), ((), ())), preferred_element_type=F32)


def mm_tn(a, b):
    return lax.dot_general(a, b, (((0,), (0,)), ((), ())), preferred_element_type=F32)


def norm_stats(values):
    center = values - jnp.mean(values, axis=-1, keepdims=True)
    spread = jnp.mean(center * center, axis=-1, keepdims=True)
    inv = lax.rsqrt(spread + EPS)
    return center * inv, inv


def norm_back(vhat, inv, dy, gain):
    gd = dy * gain
    return inv * (
        gd
        - jnp.mean(gd, axis=-1, keepdims=True)
        - vhat * jnp.mean(gd * vhat, axis=-1, keepdims=True)
    )


def row_sum(values):
    return jnp.sum(values, axis=0, keepdims=True)


def embed(tokens, ids, n, ptab):
    count = tokens.shape[0]
    each = count // 128
    pick = lax.broadcasted_iota(jnp.int32, (16, 128), 0)
    wide = ids[:, :128].astype(F32)
    mine = jnp.concatenate(
        [
            jnp.sum(jnp.where(pick == n * each + i, wide, 0.0), axis=0, keepdims=True)
            for i in range(each)
        ],
        axis=1,
    ).astype(jnp.int32)
    row = lax.broadcasted_iota(jnp.int32, (16, count), 0)
    hot = (row == mine).astype(BF16)
    return tokens.astype(F32) + mm_tn(hot, ptab[16:32, :].astype(BF16)), hot


def qkv_kernel(
    tab, t0, t1, t2, t3, i0, i1, i2, i3, own0, own1, oth0, oth1,
    normed, keys, values, queries, hidden, weight, ptab, pm, low0, low1, sems, pm_sems
):
    step = pl.program_id(0)
    feature = weight.shape[0]
    block = feature // CHIPS
    seg = feature // 2
    core = tab[4, 0]
    per = t0.shape[0]

    def copies(cc, vectors):
        made, first = [], []
        for r in range(CHIPS):
            for half, parts in ((cc, (own0, own1)), (1 - cc, (oth0, oth1))):
                ref, src = rows_at(parts, r, block)
                dst = pl.multiple_of(tab[0 if half == cc else 1, r] * block, 16)
                for n in range(0 if vectors else 3):
                    made.append(
                        pltpu.make_async_copy(
                            ref.at[src, pl.ds(n * seg, seg)],
                            weight.at[
                                pl.ds(dst, block), pl.ds(n * feature + half * seg, seg)
                            ],
                            sems.at[len(made)],
                        )
                    )
            if vectors:
                ref, src = rows_at((own0, own1), r, block)
                first.append(
                    pltpu.make_async_copy(
                        ref.at[src, pl.ds(3 * seg, 128)],
                        pm.at[pl.ds(pl.multiple_of(tab[0, r] * block, 16), block), :],
                        pm_sems.at[len(first)],
                    )
                )
        return first if vectors else made

    def on_core(run):
        for cc in (0, 1):

            @pl.when(core == cc)
            def _():
                run(cc)

    def prepare(low):
        tile = jnp.minimum(step, pl.num_programs(0) - 2)
        for piece, (tok, ids) in enumerate(((t0, i0), (t1, i1), (t2, i2), (t3, i3))):
            value, _ = embed(tok[...], ids[...], tile, ptab)
            vhat, _ = norm_stats(value)
            line = (vhat * ptab[0:1, :] + ptab[1:2, :]).astype(BF16)
            normed[piece] = line
            low[piece * per : (piece + 1) * per, :] = line
            if piece == 0:
                hidden[...] = value

    def multiply(low):
        q = mm(low[0:per, :], weight[:, 0:feature]) + ptab[2:3, :]
        queries[...] = q.astype(BF16) * jnp.asarray(HEAD_DIM**-0.5, BF16)
        k = mm(low[...], weight[:, feature : 2 * feature]).astype(BF16)
        v = (mm(low[...], weight[:, 2 * feature :]) + ptab[3:4, :]).astype(BF16)
        for piece in range(4):
            rows = slice(piece * per, (piece + 1) * per)
            keys[piece] = k[rows]
            values[piece] = v[rows]

    @pl.when(step == 0)
    def _():
        def begin(cc):
            first = copies(cc, True)
            for one in first + copies(cc, False):
                one.start()
            for one in first:
                one.wait()

        on_core(begin)
        ptab[...] = pm[...].astype(F32).T[:32, :]
        prepare(low0)

        def finish(cc):
            for one in copies(cc, False):
                one.wait()

        on_core(finish)

    for parity, (before, now) in enumerate(((low1, low0), (low0, low1))):

        @pl.when((step > 0) & (lax.rem(step, 2) == parity))
        def _():
            multiply(before)
            prepare(now)


def qkv_call(tab, pieces, own, oth):
    feature = pieces[0].shape[1]
    group = pieces[0].shape[0] - 16
    per = 128
    steps = group // per
    tok = pl.BlockSpec((per, feature), lambda i: (jnp.minimum(i, steps - 1), 0))
    ids = pl.BlockSpec((16, feature), lambda i: (group // 16, 0))
    now = pl.BlockSpec((4, per, feature), lambda i: (0, jnp.minimum(i, steps - 1), 0))
    before = pl.BlockSpec((4, per, feature), lambda i: (0, jnp.maximum(i - 1, 0), 0))
    out = pl.pallas_call(
        qkv_kernel,
        grid=(steps + 1,),
        in_specs=[smem()] + [tok] * 4 + [ids] * 4 + [hbm()] * 4,
        out_specs=[
            now,
            before,
            before,
            pl.BlockSpec((per, feature), lambda i: (jnp.maximum(i - 1, 0), 0)),
            tok,
            once((feature, 3 * feature)),
            once((32, feature)),
        ],
        out_shape=[
            jax.ShapeDtypeStruct((4, group, feature), BF16),
            jax.ShapeDtypeStruct((4, group, feature), BF16),
            jax.ShapeDtypeStruct((4, group, feature), BF16),
            jax.ShapeDtypeStruct((group, feature), BF16),
            jax.ShapeDtypeStruct((group, feature), F32),
            jax.ShapeDtypeStruct((feature, 3 * feature), BF16),
            jax.ShapeDtypeStruct((32, feature), F32),
        ],
        scratch_shapes=[
            pltpu.VMEM((feature, 128), BF16),
            pltpu.VMEM((4 * per, feature), BF16),
            pltpu.VMEM((4 * per, feature), BF16),
            pltpu.SemaphoreType.DMA((6 * CHIPS,)),
            pltpu.SemaphoreType.DMA((CHIPS,)),
        ],
        compiler_params=params(),
        cost_estimate=pl.CostEstimate(
            flops=2 * group * feature * feature * 9, bytes_accessed=30_000_000, transcendentals=0
        ),
        name="qkv",
    )(tab, *pieces, *pieces, *own, *oth)
    return [x.reshape(4 * group, feature) for x in out[:3]] + list(out[3:])


def window(starts, g, clip, n, group, win=WIN):
    first = starts[g * 16 + clip]
    last = starts[g * 16 + clip + 1]
    lead = (first // 16) * 16 + n * win
    base = pl.multiple_of(jnp.minimum(lead, group - win), 16)
    return base, jnp.maximum(first, lead) - base, last - base


def counts(starts, clip, groups, win=WIN):
    def need(g):
        first = (starts[g * 16 + clip] // 16) * 16
        return (starts[g * 16 + clip + 1] - first + win - 1) // win

    spans = [need(g) for g in groups]
    most = spans[0]
    for s in spans[1:]:
        most = jnp.maximum(most, s)
    return most


def each_clip(starts, one, many):
    together = 4
    for start in range(0, CLIPS, together):
        clips = range(start, start + together)

        def most(win):
            steps = [counts(starts, clip, range(4), win) for clip in clips]
            return functools.reduce(jnp.maximum, steps)

        fits, fits_large = most(WIN) <= 1, most(LARGE) <= 1

        @pl.when(fits)
        def _():
            for clip in clips:
                one(clip, WIN)

        @pl.when(jnp.logical_not(fits) & fits_large)
        def _():
            for clip in clips:
                one(clip, LARGE)

        @pl.when(jnp.logical_not(fits_large))
        def _():
            @pl.loop(0, together)
            def _(i):
                clip = start + i
                many(clip, counts(starts, clip, [0]), counts(starts, clip, range(4)))


def lane_halves():
    lane = lax.broadcasted_iota(jnp.int32, (1, 128), 1)
    left = (lane < HEAD_DIM).astype(BF16)
    return left, 1 - left


def stack_heads(rows):
    left, right = lane_halves()
    return jnp.concatenate([rows * left, rows * right], axis=0)


def merge_heads(stacked):
    win = stacked.shape[0] // 2
    lane = lax.broadcasted_iota(jnp.int32, (win, 128), 1)
    return jnp.where(lane < HEAD_DIM, stacked[:win], stacked[win:])


def row_valid(lo, hi, win=WIN):
    row = lax.broadcasted_iota(jnp.int32, (win, 128), 0)
    return (row >= lo) & (row < hi)


def load_keys(starts, clip, n, group, *refs, win=WIN):
    tiles = [[] for _ in refs]
    spans = []
    for g in range(4):
        base, lo, hi = window(starts, g, clip, n, group, win)
        for t, ref in zip(tiles, refs):
            t.append(ref[pl.ds(pl.multiple_of(g * group + base, 16), win), :])
        spans.append((base, lo, hi))
    return [jnp.concatenate(t, axis=0) for t in tiles], spans


def key_bias_row(spans, win=WIN):
    lane = lax.broadcasted_iota(jnp.int32, (1, 4 * win), 1)
    valid = [
        (lane >= lo + g * win) & (lane < jnp.minimum(hi, win) + g * win)
        for g, (_, lo, hi) in enumerate(spans)
    ]
    return jnp.where(valid[0] | valid[1] | valid[2] | valid[3], 0.0, MASKED)


def key_bias_col(spans, win=WIN):
    row = lax.broadcasted_iota(jnp.int32, (win, 2 * win), 0)
    return jnp.concatenate(
        [jnp.where((row >= lo) & (row < hi), 0.0, MASKED) for _, lo, hi in spans], axis=0
    )


def attn_kernel(starts, q, k, v, *rest, group):
    out, logs = rest[-2:]

    def one(clip, win):
        base, lo, hi = window(starts, 0, clip, 0, group, win)
        stacked = stack_heads(q[pl.ds(base, win), :])
        (kt, vt), spans = load_keys(starts, clip, 0, group, k, v, win=win)
        scores = mm_nt(stacked, kt) + key_bias_row(spans, win)
        peak = jnp.max(scores, axis=1, keepdims=True)
        e = jnp.exp(scores - peak).astype(BF16)
        o = mm(e, jnp.concatenate([vt, jnp.ones((4 * win, 128), BF16)], axis=1))
        total = o[:, 128:]
        logs[0, clip : clip + 1, 0 : 2 * win] = (peak + jnp.log(total)).T[:1]
        o = o[:, :128] * (1.0 / total)
        spot = pl.ds(base, win)
        out[spot, :] = jnp.where(row_valid(lo, hi, win), merge_heads(o).astype(BF16), out[spot, :])

    def many(clip, rows, steps):
        @pl.loop(0, rows)
        def _(i):
            base, lo, hi = window(starts, 0, clip, i, group)
            stacked = stack_heads(q[pl.ds(base, WIN), :])

            def inner(j, carry):
                peak, total, acc = carry
                (kt, vt), spans = load_keys(starts, clip, j, group, k, v)
                scores = mm_nt(stacked, kt) + key_bias_row(spans)
                new = jnp.maximum(peak, jnp.max(scores, axis=1, keepdims=True))
                e = jnp.exp(scores - new)
                shrink = jnp.exp(peak - new)
                return (
                    new,
                    total * shrink + jnp.sum(e, axis=1, keepdims=True),
                    acc * shrink + mm(e.astype(BF16), vt),
                )

            start = (
                jnp.full((2 * WIN, 1), 2 * MASKED, F32),
                jnp.zeros((2 * WIN, 1), F32),
                jnp.zeros((2 * WIN, 128), F32),
            )
            _, total, acc = lax.fori_loop(0, steps, inner, start)
            o = merge_heads(acc * (1.0 / total)).astype(BF16)
            spot = pl.ds(base, WIN)
            out[spot, :] = jnp.where(row_valid(lo, hi), o, out[spot, :])

    each_clip(starts, one, many)


def attn_call(starts, queries, keys, values, part, before=()):
    group, feature = queries.shape
    pairs = feature // 384
    small = pl.BlockSpec((group, 128), lambda i: (0, i + part * pairs))
    large = pl.BlockSpec((4 * group, 128), lambda i: (0, i + part * pairs))
    logs = pl.BlockSpec((1, CLIPS, 384), lambda i: (i + part * pairs, 0, 0))
    return pl.pallas_call(
        functools.partial(attn_kernel, group=group),
        grid=(pairs,),
        in_specs=[smem(), small, large, large] + [hbm()] * len(before),
        out_specs=[small, logs],
        out_shape=[
            jax.ShapeDtypeStruct((group, feature), BF16),
            jax.ShapeDtypeStruct((feature // 128, CLIPS, 384), F32),
        ],
        input_output_aliases={4 + n: n for n in range(len(before))},
        compiler_params=params(),
        cost_estimate=pl.CostEstimate(
            flops=10_000_000_000, bytes_accessed=12_000_000, transcendentals=6_300_000
        ),
        name="attention",
    )(starts, queries, keys, values, *before)


def attn_back_kernel(starts, q, k, v, go, ctx, logs, *rest, group):
    dq, dk, dv, dk_acc, dv_acc, dq_acc = rest[-6:]
    dk_acc[...] = jnp.zeros_like(dk_acc)
    dv_acc[...] = jnp.zeros_like(dv_acc)
    dq_acc[...] = jnp.zeros_like(dq_acc)
    scale = HEAD_DIM**-0.5

    def load_query(clip, i, win=WIN):
        base, lo, hi = window(starts, 0, clip, i, group, win)
        spot = pl.ds(base, win)
        keep = jnp.where(row_valid(lo, hi, win), go[spot, :], jnp.zeros((), BF16))
        return base, stack_heads(q[spot, :]), stack_heads(keep)

    def finish(spans, base, kt, stacked, back, prob, ds, win=WIN):
        ds = ds.astype(BF16)
        dvt = mm(prob.astype(BF16), back)
        dkt = mm(ds, stacked)
        for g, (kb, _, _) in enumerate(spans):
            spot = pl.ds(pl.multiple_of(g * group + kb, 16), win)
            dk_acc[spot, :] += dkt[g * win : (g + 1) * win]
            dv_acc[spot, :] += dvt[g * win : (g + 1) * win]
        spot = pl.ds(base, win)
        dq_acc[spot, :] += merge_heads(mm_tn(ds, kt))

    def one(clip, win):
        base, stacked, back = load_query(clip, 0, win)
        (kt, vt), spans = load_keys(starts, clip, 0, group, k, v, win=win)
        prob = jnp.exp(
            mm_nt(kt, stacked)
            + key_bias_col(spans, win)
            - logs[0, clip : clip + 1, 0 : 2 * win]
        )
        gp = mm_nt(vt, back)
        spot = pl.ds(base, win)
        both = (stack_heads(ctx[spot, :]).astype(F32) * back.astype(F32)).astype(BF16)
        inner = mm_nt(jnp.ones((8, 128), BF16), both)[:1]
        finish(spans, base, kt, stacked, back, prob, prob * (gp - inner), win)

    def many(clip, rows, steps):
        @pl.loop(0, rows)
        def _(i):
            base, stacked, back = load_query(clip, i)

            def totals(j, carry):
                peak, total, inner = carry
                (kt, vt), spans = load_keys(starts, clip, j, group, k, v)
                scores = mm_nt(kt, stacked) + key_bias_col(spans)
                new = jnp.maximum(peak, jnp.max(scores, axis=0, keepdims=True))
                e = jnp.exp(scores - new)
                shrink = jnp.exp(peak - new)
                gp = mm_nt(vt, back)
                return (
                    new,
                    total * shrink + jnp.sum(e, axis=0, keepdims=True),
                    inner * shrink + jnp.sum(e * gp, axis=0, keepdims=True),
                )

            zero = jnp.zeros((1, 2 * WIN), F32)
            peak, total, inner = lax.fori_loop(
                0, steps, totals, (jnp.full((1, 2 * WIN), 2 * MASKED, F32), zero, zero)
            )
            part = 1.0 / total
            inner = inner * part

            @pl.loop(0, steps)
            def _(j):
                (kt, vt), spans = load_keys(starts, clip, j, group, k, v)
                scores = mm_nt(kt, stacked) + key_bias_col(spans)
                prob = jnp.exp(scores - peak) * part
                gp = mm_nt(vt, back)
                finish(spans, base, kt, stacked, back, prob, prob * (gp - inner))

    each_clip(starts, one, many)

    dq[...] = (dq_acc[...] * scale).astype(BF16)
    dk[...] = dk_acc[...].astype(BF16)
    dv[...] = dv_acc[...].astype(BF16)


def attn_back_call(starts, queries, keys, values, grad_context, context, logs, part, before=()):
    group, feature = queries.shape
    pairs = feature // 384
    small = pl.BlockSpec((group, 128), lambda i: (0, i + part * pairs))
    large = pl.BlockSpec((4 * group, 128), lambda i: (0, i + part * pairs))
    return pl.pallas_call(
        functools.partial(attn_back_kernel, group=group),
        grid=(pairs,),
        in_specs=[smem(), small, large, large, small, small]
        + [pl.BlockSpec((1, CLIPS, 384), lambda i: (i + part * pairs, 0, 0))]
        + [hbm()] * len(before),
        out_specs=[small, large, large],
        out_shape=[
            jax.ShapeDtypeStruct((group, feature), BF16),
            jax.ShapeDtypeStruct((4 * group, feature), BF16),
            jax.ShapeDtypeStruct((4 * group, feature), BF16),
        ],
        input_output_aliases={7 + n: n for n in range(len(before))},
        scratch_shapes=[
            pltpu.VMEM((4 * group, 128), F32),
            pltpu.VMEM((4 * group, 128), F32),
            pltpu.VMEM((group, 128), F32),
        ],
        compiler_params=params(),
        cost_estimate=pl.CostEstimate(
            flops=20_000_000_000, bytes_accessed=24_000_000, transcendentals=6_300_000
        ),
        name="attention_back",
    )(starts, queries, keys, values, grad_context, context, logs, *before)


def phi_parts(u):
    t = 1.0 / (1.0 + (0.3275911 * 0.5**0.5) * jnp.abs(u))
    e = jnp.exp(u * u * -0.5)
    poly = t * (
        0.127414796
        + t * (-0.142248368 + t * (0.7107068705 + t * (-0.7265760135 + t * 0.5307027145)))
    )
    tail = poly * e
    return jnp.where(u < 0, tail, 1.0 - tail), e * 0.3989422804014327


def middle_kernel(
    tab, ctx, hidden, ups, ptab, up_bias, u_own0, u_own1, u_oth0, u_oth1, d_own0, d_own1, d_oth0, d_oth1,
    mixed, grad_mid, grad_ctx, gu_own, gu_oth, gd_own, gd_oth, small, g_up_bias,
    w_up, w_dn, w_out, mid, sec, sec_t, acc, gsec, act, gup, t_up, t_dn, in_sems, up_sems, dn_sems,
    *, chunks
):
    j = pl.program_id(0)
    group, feature = ctx.shape
    block = feature // CHIPS
    dblock = w_dn.shape[0] // CHIPS
    seg = feature // 2
    part = w_dn.shape[0] // chunks
    per_half = chunks // 2
    core = tab[4, 0]
    tile = 256
    tiles = group // tile

    def loads(cc, part_of):
        made = []
        count = 0

        def add(src, dst, kind):
            nonlocal count
            if kind == part_of:
                made.append(pltpu.make_async_copy(src, dst, in_sems.at[count]))
            count += 1

        for r in range(CHIPS):
            for half, up, down, row in (
                (cc, (u_own0, u_own1), (d_own0, d_own1), 0),
                (1 - cc, (u_oth0, u_oth1), (d_oth0, d_oth1), 1),
            ):
                ref, src = rows_at(up, r, block)
                dref, _ = rows_at(down, r, block)
                chip = tab[row, r]
                dst = pl.ds(pl.multiple_of(chip * block, 16), block)
                add(
                    ref.at[src, pl.ds(per_half * part, seg)],
                    w_out.at[dst, pl.ds(half * seg, seg)],
                    0,
                )
                for n in range(per_half):
                    add(
                        ref.at[src, pl.ds(n * part, part)],
                        w_up.at[half * per_half + n, dst, :],
                        1,
                    )
                for n in range(dblock // block):
                    row0 = pl.multiple_of(chip * dblock + n * block, 16)
                    add(
                        dref.at[src, pl.ds(n * seg, seg)],
                        w_dn.at[pl.ds(row0, block), pl.ds(half * seg, seg)],
                        1,
                    )
        return made

    def for_core(run):
        for cc in (0, 1):

            @pl.when(core == cc)
            def _():
                run(cc)

    @pl.when(j == 0)
    def _():
        def run(cc):
            first = loads(cc, 0)
            for one in first + loads(cc, 1):
                one.start()
            for one in first:
                one.wait()

        for_core(run)
        for t in range(tiles):
            rows = slice(t * tile, (t + 1) * tile)
            value = hidden[rows, :] + mm(ctx[rows, :], w_out[...]) + ptab[4:5, :]
            mid[rows, :] = value
            vhat, _ = norm_stats(value)
            low = (vhat * ptab[5:6, :] + ptab[6:7, :]).astype(BF16)
            sec[rows, :] = low
            sec_t[:, rows] = low.T
            acc[rows, :] = value + ptab[7:8, :]
            gsec[rows, :] = jnp.zeros((tile, feature), F32)

        def rest(cc):
            for one in loads(cc, 1):
                one.wait()

        for_core(rest)

    slot = lax.rem(j, 2)

    def drain(sl):
        for r in range(CHIPS):
            pltpu.make_async_copy(
                t_up.at[sl, pl.ds(0, block), :],
                gu_own.at[pl.ds(0, block), pl.ds(0, part)],
                up_sems.at[sl, r],
            ).wait()
        for n in range(2 * (part // block)):
            pltpu.make_async_copy(
                t_dn.at[sl, pl.ds(0, block), pl.ds(0, seg)],
                gd_own.at[pl.ds(0, block), pl.ds(0, seg)],
                dn_sems.at[sl, n],
            ).wait()

    upj = w_up[j]
    dnj = w_dn[pl.ds(pl.multiple_of(j * part, 128), part), :]
    bias = up_bias[pl.ds(j, 1), :]
    gub = jnp.zeros((1, part), F32)
    cuts = [slice(t * tile, (t + 1) * tile) for t in range(tiles)]

    def products(t):
        return mm(sec[cuts[t], :], upj) + bias, mm_nt(ups[cuts[t], :], dnj)

    ahead = products(0)
    for t in range(tiles):
        u, ga = ahead
        if t + 1 < tiles:
            ahead = products(t + 1)
        rows = cuts[t]
        dist, dens = phi_parts(u)
        a = (u * dist).astype(BF16)
        g = (ga * (dist + u * dens)).astype(BF16)
        act[rows, :] = a
        gup[rows, :] = g
        gub = gub + row_sum(g.astype(F32))
        if t > 0:
            acc[cuts[t - 1], :] += mm(act[cuts[t - 1], :], dnj)
            gsec[cuts[t - 1], :] += mm_nt(gup[cuts[t - 1], :], upj)
    acc[cuts[-1], :] += mm(act[cuts[-1], :], dnj)
    gsec[cuts[-1], :] += mm_nt(gup[cuts[-1], :], upj)
    g_up_bias[pl.ds(j, 1), :] = gub

    @pl.when(j >= 2)
    def _():
        drain(slot)

    t_up[slot] = mm(sec_t[...], gup[...]).astype(BF16)
    t_dn[slot] = mm_tn(act[...], ups[...]).astype(BF16)

    def send(cc):
        col = pl.ds(pl.multiple_of(lax.rem(j, per_half) * part, 128), part)
        for is_own in (True, False):
            ref = gu_own if is_own else gu_oth

            @pl.when((j // per_half == cc) == is_own)
            def _():
                for r in range(CHIPS):
                    src = pl.ds(pl.multiple_of(tab[0 if is_own else 1, r] * block, 16), block)
                    pltpu.make_async_copy(
                        t_up.at[slot, src, :],
                        ref.at[pl.ds(r * block, block), col],
                        up_sems.at[slot, r],
                    ).start()

        n = 0
        count = part // dblock
        for half, ref, row in ((cc, gd_own, 2), (1 - cc, gd_oth, 3)):
            for i in range(count):
                place = pl.multiple_of(tab[row, j * count + i] * block, 16)
                for m in range(dblock // block):
                    pltpu.make_async_copy(
                        t_dn.at[
                            slot, pl.ds(i * dblock + m * block, block), pl.ds(half * seg, seg)
                        ],
                        ref.at[pl.ds(place, block), pl.ds(m * seg, seg)],
                        dn_sems.at[slot, n],
                    ).start()
                    n += 1

    for_core(send)

    @pl.when(j == chunks - 1)
    def _():
        s_gain = jnp.zeros((1, feature), F32)
        s_shift = jnp.zeros((1, feature), F32)
        s_out = jnp.zeros((1, feature), F32)
        s_down = jnp.zeros((1, feature), F32)
        for t in range(tiles):
            rows = slice(t * tile, (t + 1) * tile)
            mixed[rows, :] = acc[rows, :].astype(BF16)
            vhat, inv = norm_stats(mid[rows, :])
            dy = gsec[rows, :]
            wide = ups[rows, :].astype(F32)
            gm = wide + norm_back(vhat, inv, dy, ptab[5:6, :])
            grad_mid[rows, :] = gm
            low = gm.astype(BF16)
            gup[rows, :] = low
            grad_ctx[rows, :] = mm_nt(low, w_out[...]).astype(BF16)
            s_gain = s_gain + row_sum(dy * vhat)
            s_shift = s_shift + row_sum(dy)
            s_out = s_out + row_sum(gm)
            s_down = s_down + row_sum(wide)
        zero = jnp.zeros((1, feature), F32)
        small[...] = jnp.concatenate(
            [zero, zero, zero, zero, s_out, s_gain, s_shift, s_down], axis=0
        )
        drain(1 - slot)
        act[...] = mm_tn(ctx[...], gup[...]).astype(BF16)

        def run(cc):
            made = []
            for half, ref, row in ((cc, gu_own, 0), (1 - cc, gu_oth, 1)):
                for r in range(CHIPS):
                    src = pl.ds(pl.multiple_of(tab[row, r] * block, 16), block)
                    made.append(
                        pltpu.make_async_copy(
                            act.at[src, pl.ds(half * seg, seg)],
                            ref.at[pl.ds(r * block, block), pl.ds(per_half * part, seg)],
                            in_sems.at[len(made)],
                        )
                    )
            for one in made:
                one.start()
            for one in made:
                one.wait()

        for_core(run)
        drain(slot)


def middle_call(tab, ctx, hidden, ups, ptab, up_bias, up_pair, down_pair, ff):
    group, feature = hidden.shape
    chunks = ff // feature
    part = ff // chunks
    return pl.pallas_call(
        functools.partial(middle_kernel, chunks=chunks),
        grid=(chunks,),
        in_specs=[
            smem(),
            once((group, feature)),
            once((group, feature)),
            once((group, feature)),
            once((32, feature)),
            once((chunks, part)),
            *[hbm()] * 8,
        ],
        out_specs=[
            once((group, feature)),
            once((group, feature)),
            once((group, feature)),
            hbm(), hbm(), hbm(), hbm(),
            once((8, feature)),
            once((chunks, part)),
        ],
        out_shape=[
            jax.ShapeDtypeStruct((group, feature), BF16),
            jax.ShapeDtypeStruct((group, feature), F32),
            jax.ShapeDtypeStruct((group, feature), BF16),
            *[jax.ShapeDtypeStruct((feature, up_pair[0][0].shape[1]), BF16)] * 2,
            *[jax.ShapeDtypeStruct((feature, down_pair[0][0].shape[1]), BF16)] * 2,
            jax.ShapeDtypeStruct((8, feature), F32),
            jax.ShapeDtypeStruct((chunks, part), F32),
        ],
        scratch_shapes=[
            pltpu.VMEM((chunks, feature, part), BF16),
            pltpu.VMEM((ff, feature), BF16),
            pltpu.VMEM((feature, feature), BF16),
            pltpu.VMEM((group, feature), F32),
            pltpu.VMEM((group, feature), BF16),
            pltpu.VMEM((feature, group), BF16),
            pltpu.VMEM((group, feature), F32),
            pltpu.VMEM((group, feature), F32),
            pltpu.VMEM((group, part), BF16),
            pltpu.VMEM((group, part), BF16),
            pltpu.VMEM((2, feature, part), BF16),
            pltpu.VMEM((2, part, feature), BF16),
            pltpu.SemaphoreType.DMA((2 * CHIPS * (1 + chunks // 2 + ff // feature),)),
            pltpu.SemaphoreType.DMA((2, CHIPS)),
            pltpu.SemaphoreType.DMA((2, 2 * CHIPS)),
        ],
        compiler_params=params(),
        cost_estimate=pl.CostEstimate(
            flops=2 * group * feature * (3 * feature + 6 * ff),
            bytes_accessed=34_000_000,
            transcendentals=2 * group * ff,
        ),
        name="middle",
    )(tab, ctx, hidden, ups, ptab, up_bias, *sum(up_pair + down_pair, ()))


def qkv_weight_kernel(tab, normed, dq, dk, dv, own, oth, norm_t, tmp, sems, *, blocks):
    step = pl.program_id(0)
    total, feature = normed.shape
    group = dq.shape[0]
    block = feature // CHIPS
    seg = feature // 2
    core = tab[4, 0]

    def stores(cc, n):
        made = []
        for half, ref, row in ((cc, own, 0), (1 - cc, oth, 1)):
            for r in range(CHIPS):
                src = pl.ds(pl.multiple_of(tab[row, r] * block, 16), block)
                made.append(
                    pltpu.make_async_copy(
                        tmp.at[n, src, pl.ds(half * seg, seg)],
                        ref.at[pl.ds(r * block, block), pl.ds(n * seg, seg)],
                        sems.at[n, len(made)],
                    )
                )
        return made

    def on_core(run):
        for cc in (0, 1):

            @pl.when(core == cc)
            def _():
                run(cc)

    def start(n):
        def run(cc):
            for one in stores(cc, n):
                one.start()

        on_core(run)

    @pl.when(step == 0)
    def _():
        tile = 256
        for t in range(total // tile):
            rows = slice(t * tile, (t + 1) * tile)
            norm_t[:, rows] = normed[rows, :].T
        tmp[0] = mm(norm_t[:, :group], dq[...]).astype(BF16)
        start(0)

    cut = feature // blocks
    for n, ref in ((1, dk), (2, dv)):
        for i in range(blocks):

            @pl.when(step == 1 + (n - 1) * blocks + i)
            def _():
                tmp[n, :, i * cut : (i + 1) * cut] = mm(norm_t[...], ref[...]).astype(BF16)
                if i == blocks - 1:
                    start(n)

    @pl.when(step == 2 * blocks)
    def _():
        def finish(cc):
            for n in range(3):
                for one in stores(cc, n):
                    one.wait()

        on_core(finish)


def qkv_weight_call(tab, normed, dq, dk, dv):
    total, feature = normed.shape
    half = 3 * feature // 2
    blocks = 3
    cut = feature // blocks
    return pl.pallas_call(
        functools.partial(qkv_weight_kernel, blocks=blocks),
        grid=(1 + 2 * blocks,),
        in_specs=[
            smem(),
            once(normed.shape),
            once(dq.shape),
            pl.BlockSpec((total, cut), lambda i: (0, jnp.clip(i - 1, 0, blocks - 1))),
            pl.BlockSpec((total, cut), lambda i: (0, jnp.clip(i - 1 - blocks, 0, blocks - 1))),
        ],
        out_specs=[hbm(), hbm()],
        out_shape=[jax.ShapeDtypeStruct((feature, half), BF16)] * 2,
        scratch_shapes=[
            pltpu.VMEM((feature, total), BF16),
            pltpu.VMEM((3, feature, feature), BF16),
            pltpu.SemaphoreType.DMA((3, 2 * CHIPS)),
        ],
        compiler_params=params(),
        cost_estimate=pl.CostEstimate(
            flops=2 * dq.shape[0] * feature * feature * 9,
            bytes_accessed=20_000_000,
            transcendentals=0,
        ),
        name="qkv_weight",
    )(tab, normed, dq, dk, dv)


def qkv_back_kernel(*refs, group, own_rows):
    tab, refs = refs[0], refs[1:]
    n_pieces = 2 if own_rows else 1
    toks, idss, refs = refs[:n_pieces], refs[n_pieces : 2 * n_pieces], refs[2 * n_pieces :]
    dk, dv, weight, ptab, given = refs[:5]
    refs = refs[5:]
    if own_rows:
        dq, gm, out, sums, small, moved, sems = refs
    else:
        out, sums = refs
    step = pl.program_id(0)
    feature = weight.shape[0]
    steps = group // out.shape[0]

    @pl.when(step == 0)
    def _():
        sums[...] = given[...]

    def body(tok, ids, own):
        value, hot = embed(tok[...], ids[...], lax.rem(step, steps), ptab)
        vhat, inv = norm_stats(value)
        dy = mm_nt(dk[...], weight[:, feature : 2 * feature]) + mm_nt(
            dv[...], weight[:, 2 * feature :]
        )
        if own:
            dy = dy + mm_nt(dq[...], weight[:, 0:feature])
            sums[2:3, :] += row_sum(dq[...].astype(F32))
        grad = norm_back(vhat, inv, dy, ptab[0:1, :])
        out[...] = grad.astype(BF16)
        sums[0:1, :] += row_sum(dy * vhat)
        sums[1:2, :] += row_sum(dy)
        sums[3:4, :] += row_sum(dv[...].astype(F32))
        if own:
            grad = grad + gm[...]
        high = grad.astype(BF16)
        rest = (grad - high.astype(F32)).astype(BF16)
        sums[16:32, :] += mm(hot, high) + mm(hot, rest)

    if own_rows:

        @pl.when(step < steps)
        def _():
            body(toks[0], idss[0], True)

        @pl.when(step >= steps)
        def _():
            body(toks[1], idss[1], False)

    else:
        body(toks[0], idss[0], False)

    if own_rows:

        @pl.when(step == 2 * steps - 1)
        def _():
            turned = jnp.concatenate([sums[...], jnp.zeros((96, feature), F32)], axis=0).T
            moved[...] = turned.astype(BF16)
            block = feature // CHIPS
            made = []
            for side in range(2):
                for r in range(CHIPS):
                    src = pl.ds(pl.multiple_of(tab[side, r] * block, 16), block)
                    made.append(
                        pltpu.make_async_copy(
                            moved.at[src, :],
                            small.at[side, pl.ds(r * block, block), :],
                            sems.at[side, r],
                        )
                    )
            for one in made:
                one.start()
            for one in made:
                one.wait()


def qkv_back_call(tab, pair, first_piece, dk, dv, weight, ptab, given, own=()):
    feature = dk.shape[1]
    group = pair[0].shape[0] - 16
    per = 256
    steps = group // per
    skip = first_piece * steps
    count = len(pair)

    def at(piece):
        return pl.BlockSpec(
            (per, feature), lambda i: (jnp.clip(i - piece * steps, 0, steps - 1), 0)
        )

    ids = pl.BlockSpec((16, feature), lambda i: (group // 16, 0))
    tile = pl.BlockSpec((per, feature), lambda i: (i, 0))
    later = pl.BlockSpec((per, feature), lambda i: (i + skip, 0))
    first = pl.BlockSpec((per, feature), lambda i: (jnp.minimum(i, steps - 1), 0))
    return pl.pallas_call(
        functools.partial(qkv_back_kernel, group=group, own_rows=bool(own)),
        grid=(count * steps,),
        in_specs=[smem()]
        + [at(n) for n in range(count)]
        + [ids] * count
        + [later, later]
        + [once((feature, 3 * feature)), once((32, feature)), once((32, feature))]
        + [first] * len(own),
        out_specs=[tile, once((32, feature))] + [hbm()] * bool(own),
        out_shape=[
            jax.ShapeDtypeStruct((count * group, feature), BF16),
            jax.ShapeDtypeStruct((32, feature), F32),
            jax.ShapeDtypeStruct((2, feature, 128), BF16),
        ][: 2 + bool(own)],
        scratch_shapes=[pltpu.VMEM((feature, 128), BF16), pltpu.SemaphoreType.DMA((2, CHIPS))][
            : 2 * bool(own)
        ],
        compiler_params=params(),
        cost_estimate=pl.CostEstimate(
            flops=group * feature * feature * 9, bytes_accessed=15_000_000, transcendentals=0
        ),
        name="qkv_back",
    )(tab, *pair, *pair, dk, dv, weight, ptab, given, *own)


def payload_kernel(tab, *refs, rd, times):
    vecs, (up_bias, table, qkv, up, out, down, mine, other, lines) = refs[:8], refs[8:]
    feature = down.shape[1]
    seg = feature // 2
    ff = up.shape[1]
    core = tab[4, 0]
    lines[...] = jnp.zeros_like(lines)
    for n, vec in enumerate(vecs):
        lines[n : n + 1, 0:rd] = vec[...].astype(F32)
    for n in range(4):
        lines[8 + n : 9 + n, 0:rd] = up_bias[:, n * rd : (n + 1) * rd].astype(F32)

    def places(rows, first):
        row = lax.broadcasted_iota(jnp.int32, (rows, 128), 0)
        return (lax.broadcasted_iota(jnp.int32, (rows, 128), 1) == row + first).astype(BF16)

    small = mm_tn(lines[...].astype(BF16), places(16, 0))[:rd] + mm(table[...], places(FREQS, 16))
    small = small.astype(BF16)
    wide = down[...].astype(F32)

    def fill(ref, h):
        at = 0

        def put(value):
            nonlocal at
            ref[:, at : at + value.shape[1]] = value
            at += value.shape[1]

        for n in range(3):
            put(qkv[:, n * feature + h * seg : n * feature + (h + 1) * seg])
        put(small)
        put(up[:, h * (ff // 2) : (h + 1) * (ff // 2)])
        put(out[:, h * seg : (h + 1) * seg])
        for n in range(times):
            put(wide[n * rd : (n + 1) * rd, h * seg : (h + 1) * seg].astype(BF16))

    for cc in (0, 1):

        @pl.when(core == cc)
        def _():
            fill(mine, cc)
            fill(other, 1 - cc)


def payload_call(tab, vecs, up_bias, table, qkv, up, out, down):
    rd, times = qkv.shape[0], down.shape[0] // qkv.shape[0]
    half = (qkv.shape[1] + up.shape[1] + out.shape[1] + times * down.shape[1]) // 2 + 128
    return pl.pallas_call(
        functools.partial(payload_kernel, rd=rd, times=times),
        in_specs=[smem()] + [whole()] * (len(vecs) + 6),
        out_specs=[whole(), whole()],
        out_shape=[jax.ShapeDtypeStruct((rd, half), BF16)] * 2,
        scratch_shapes=[pltpu.VMEM((16, 128), F32)],
        compiler_params=params(),
        name="payload",
    )(tab, *[v.reshape(1, -1) for v in vecs], up_bias.reshape(1, -1), table, qkv, up, out, down)


def pair_kernel(tab, mine, got, for_q, for_u, for_d, *, widths):
    rd = mine.shape[0]
    n_q, n_u, times, seg = widths
    core = tab[4, 0]

    def fill(top, low):
        for ref, start, width in ((for_q, 0, n_q), (for_u, n_q, n_u)):
            cols = slice(start, start + width)
            ref[...] = jnp.concatenate(
                [top[:, cols].astype(F32), low[:, cols].astype(F32)], axis=0
            ).astype(BF16)
        for block in range(times):
            part = top if block < times // 2 else low
            start = n_q + n_u + (block % (times // 2)) * 2 * seg
            rows = [part[:, start + i * seg : start + (i + 1) * seg].astype(F32) for i in (0, 1)]
            for_d[:, block * seg : (block + 1) * seg] = jnp.concatenate(rows, axis=0).astype(BF16)

    for cc in (0, 1):

        @pl.when(core == cc)
        def _():
            fill(*((mine, got) if cc == 0 else (got, mine)))


def pair_call(tab, mine, got, widths):
    rd = mine.shape[0]
    n_q, n_u, times, seg = widths
    return pl.pallas_call(
        functools.partial(pair_kernel, widths=widths),
        in_specs=[smem(), whole(), whole()],
        out_specs=[whole()] * 3,
        out_shape=[jax.ShapeDtypeStruct((2 * rd, n), BF16) for n in (n_q, n_u, times * seg)],
        compiler_params=params(),
        name="pair",
    )(tab, mine, got)


def tail_rows_kernel(tokens, ids, out):
    group, feature = tokens.shape
    out[0:group, :] = tokens[...]
    rows = [ids[:, n * 128 : (n + 1) * 128].astype(F32) for n in range(group // 128)]
    rows = jnp.concatenate(rows + [jnp.zeros((16 - len(rows), 128), F32)], axis=0).astype(BF16)
    out[group : group + 16, :] = jnp.concatenate(
        [rows, jnp.zeros((16, feature - 128), BF16)], axis=1
    )


def tail_rows_call(tokens, ids):
    group, feature = tokens.shape
    return pl.pallas_call(
        tail_rows_kernel,
        in_specs=[whole(), whole()],
        out_specs=whole(),
        out_shape=jax.ShapeDtypeStruct((group + 16, feature), BF16),
        compiler_params=params(),
        name="tail_rows",
    )(tokens, ids)


class Hops:
    def __init__(self, n_seq, n_freq):
        self.n_seq, self.n_freq = n_seq, n_freq
        self.swaps = n_seq == 8 and n_freq == 4
        self.core = lax.axis_index("freq") % 2
        self.first = self.core == 0
        chip = lax.axis_index("seq") * 2 + lax.axis_index("freq") // 2
        if self.swaps:
            bits = ((4, 8, 2, 1), (4, 8, 1, 2))
            masks = np.zeros((2, CHIPS), np.int32)
            for c in (0, 1):
                for r in range(CHIPS):
                    for b in range(4):
                        if r >> b & 1:
                            masks[c, r] ^= bits[c][b]
            one, two = jnp.asarray(masks[0]), jnp.asarray(masks[1])
            mine = jnp.where(self.first, one, two) ^ chip
            theirs = jnp.where(self.first, two, one) ^ chip

            def places(order):
                rows = (order[:, None] == jnp.arange(CHIPS)[None, :]).astype(jnp.int32)
                return jnp.sum(rows * jnp.arange(CHIPS, dtype=jnp.int32)[:, None], axis=0)

            rows = [mine, theirs, places(mine), places(theirs)]
        else:
            rows = [jnp.arange(CHIPS, dtype=jnp.int32)] * 4
        rows = [r.astype(jnp.int32) for r in rows]
        rows += [jnp.full((CHIPS,), self.core, jnp.int32)] + [rows[0]] * 3
        self.table = jnp.stack(rows)

    def swap(self, values, move):
        pairs = []
        for s in range(self.n_seq):
            for f in range(self.n_freq):
                ds, df = move(f % 2)
                pairs.append((s * self.n_freq + f, (s ^ ds) * self.n_freq + (f ^ df)))
        return lax.ppermute(values, BOTH, pairs)

    def swap_core(self, values):
        return self.swap(values, lambda c: (0, 1))

    def swap_y(self, values):
        return self.swap(values, lambda c: (0, 2))

    def swap_z(self, values, n):
        return self.swap(values, lambda c: (2 * n, 0))

    def swap_xy(self, values, n):
        return self.swap(values, lambda c: (1, 0) if c == n else (0, 2))

    def sides(self, mine, other):
        return jnp.where(self.first, mine, other), jnp.where(self.first, other, mine)

    def own_other(self, left, right):
        return jnp.where(self.first, left, right), jnp.where(self.first, right, left)

    def gather(self, held):
        parts = yield [held] + [self.swap_z(held, n) for n in (1, 2, 3)]
        held = jnp.concatenate(parts, axis=0)
        parts = yield held, self.swap_xy(held, 0)
        held = jnp.concatenate(parts, axis=0)
        held, got, across = yield held, self.swap_xy(held, 1), self.swap_core(held)
        yield (held, got), (across, self.swap_core(got))

    def scatter(self, own, other):
        own, got = yield own, self.swap_core(other)
        add = self.add
        for n in (1, 0):
            cut = own.shape[0] // 2
            send = add(own[cut:], got[cut:])
            own = add(own[:cut], got[:cut])
            own, got = yield own, self.swap_xy(send, n)
        yield from self.last_sums((own, got))

    @staticmethod
    def add(a, b):
        return (a.astype(F32) + b.astype(F32)).astype(BF16)

    def last_sums(self, pair):
        own, got = pair
        add = self.add
        cut = own.shape[0] // 4
        sends = [add(own[n * cut : (n + 1) * cut], got[n * cut : (n + 1) * cut]) for n in (1, 2, 3)]
        own = own[:cut].astype(F32) + got[:cut].astype(F32)
        own, got = yield own, [self.swap_z(send, n) for n, send in zip((1, 2, 3), sends)]
        yield own + sum(g.astype(F32) for g in got)


class Chain:
    def __init__(self, steps, count):
        self.steps, self.left, self.at = steps, count, None

    def step(self, times=1):
        for _ in range(times):
            self.at = next(self.steps) if self.at is None else self.steps.send(self.at)
            self.left -= 1
        return self.at

    def end(self):
        return self.step(self.left)


class Still:
    def __init__(self, value):
        self.at = value

    def step(self, times=1):
        return self.at

    end = step


def after(values, *chains):
    values, held = lax.optimization_barrier((values, tuple(c.at for c in chains)))
    for c, h in zip(chains, held):
        c.at = h
    return values


def col_halves(*arrays):
    left = [a[:, : a.shape[1] // 2] for a in arrays]
    right = [a[:, a.shape[1] // 2 :] for a in arrays]
    return left, right


def side_rows(down, count):
    rows, cols = down.shape
    return down.reshape(count, rows // count, cols).transpose(1, 0, 2).reshape(rows // count, -1)


def under_rows(wide, count):
    rows, cols = wide.shape
    return wide.reshape(rows, count, cols // count).transpose(1, 0, 2).reshape(rows * count, -1)


def local(
    tokens,
    freq_ids,
    clip_ids,
    cotangent,
    ln1_gain,
    first_norm_bias,
    qkv_weight,
    q_bias,
    v_bias,
    out_weight,
    out_bias,
    ln2_gain,
    ln2_bias,
    up_weight,
    up_bias,
    down_weight,
    down_bias,
    freq_table,
    *,
    n_seq,
    n_freq,
):
    _, group, feature = tokens.shape
    rd = qkv_weight.shape[0]
    n_dev = n_seq * n_freq
    seg = feature // 2
    ff = up_weight.shape[1]
    times = ff // feature
    hops = Hops(n_seq, n_freq)
    tab = hops.table

    tok = tail_rows_call(tokens.reshape(group, feature), freq_ids.reshape(1, group))
    vectors = [ln1_gain, first_norm_bias, q_bias, v_bias, out_bias, ln2_gain, ln2_bias, down_bias]
    wide_q = 3 * seg + 128
    n_up = ff // 2
    n_uo = n_up + seg
    n_all = wide_q + n_uo
    tok_c, tok_y = hops.swap_core(tok), hops.swap_y(tok)
    if hops.swaps:
        mine, other = payload_call(
            tab, vectors, up_bias, freq_table, qkv_weight, up_weight, out_weight, down_weight
        )
        held = pair_call(tab, mine, hops.swap_core(other), (wide_q, n_uo, times, seg))
        weights, ups, downs = [Chain(hops.gather(h), 4) for h in held]
    else:

        def full(x):
            return lax.all_gather(x, BOTH, axis=0, tiled=True)

        lines = jnp.concatenate(vectors + [up_bias]).reshape(12, rd)
        small = jnp.concatenate(
            [lines, jnp.zeros((4, rd), BF16), freq_table.T, jnp.zeros((100, rd), BF16)], axis=0
        ).T
        f_qkv, f_small, f_up = full(qkv_weight), full(small), full(up_weight)
        f_out, f_down = full(out_weight), full(down_weight)
        q_full = [f_qkv[:, n * feature : (n + 1) * feature] for n in range(3)]
        down_side = f_down.reshape(CHIPS, times, -1, feature).transpose(0, 2, 1, 3)
        down_side = down_side.reshape(feature, times, 2, seg)
        sides_q, sides_u, sides_d = [], [], []
        for h in (0, 1):
            sides_q.append(jnp.concatenate(col_halves(*q_full)[h] + [f_small], axis=1))
            sides_u.append(jnp.concatenate(col_halves(f_up, f_out)[h], axis=1))
            sides_d.append(down_side[:, :, h].reshape(feature, times * seg))
        cut = feature // 2
        weights, ups, downs = [
            Still(tuple((x[:cut], x[cut:]) for x in hops.own_other(*sides)))
            for sides in (sides_q, sides_u, sides_d)
        ]

    weights.step()
    tok_c = after(tok_c, weights)
    ups.step()
    weights.step()
    tok_y = after(tok_y, weights)
    weights.step()
    tok_yc = hops.swap_core(tok_y)
    tok_c = after(tok_c, weights, ups)
    ups.step()
    downs.step()
    weights.end()
    pieces = (tok, tok_c, tok_y, tok_yc)

    place = lax.axis_index("freq")
    order = jnp.stack([place, place ^ 1, place ^ 2, place ^ 3])
    below = clip_ids.reshape(n_freq, group)[:, None, :] < jnp.arange(16, dtype=jnp.int32)[None, :, None]
    first_rows = jnp.sum(below.astype(jnp.int32), axis=2)
    pick = (order[:, None] == jnp.arange(n_freq)[None, :]).astype(jnp.int32)
    starts = jnp.sum(pick[:, :, None] * first_rows[None, :, :], axis=1).reshape(4 * 16)

    normed, keys, values, queries, hidden, w_qkv, ptab = qkv_call(tab, pieces, *weights.at)
    queries, keys, values = after((queries, keys, values), ups, downs)
    ups.step()
    downs.step()
    context = attn_call(starts, queries, keys, values, 0)
    queries, context = after((queries, context), downs)
    downs.step()
    context = attn_call(starts, queries, keys, values, 1, context)
    queries, context = after((queries, context), ups, downs)
    ups.step()
    downs.step()
    context = attn_call(starts, queries, keys, values, 2, context)
    up_rows = ptab[8:12].reshape(4, n_dev, rd).transpose(1, 0, 2).reshape(times, feature)
    upstream = cotangent.reshape(group, feature)
    context, logs = context
    mixed, grad_mid, grad_ctx, *sent, sums, g_up_bias = middle_call(
        tab, context, hidden, upstream, ptab, up_rows, ups.at, downs.at, ff
    )

    def summing(own, oth):
        return Chain(hops.scatter(own, oth), 5) if hops.swaps else Still((own, oth))

    g_u, g_d = summing(*sent[:2]), summing(*sent[2:])
    g_u.step()
    g_d.step()
    grads = attn_back_call(starts, queries, keys, values, grad_ctx, context, logs, 0)
    grads, queries = after((grads, queries), g_u, g_d)
    g_u.step()
    grads = attn_back_call(starts, queries, keys, values, grad_ctx, context, logs, 1, grads)
    grads, queries = after((grads, queries), g_u, g_d)
    g_d.step()
    grads = attn_back_call(starts, queries, keys, values, grad_ctx, context, logs, 2, grads)
    dq, dk, dv = after(grads, g_u, g_d)
    g_u.step()
    g_d.step()
    g_q = qkv_weight_call(tab, normed, dq, dk, dv)
    g_q, dk, dv = after((g_q, dk, dv), g_u, g_d)
    g_q = summing(*g_q)
    g_q.step()
    g_u.step()
    given = jnp.concatenate(
        [
            sums,
            g_up_bias.reshape(n_dev, 4, rd).transpose(1, 0, 2).reshape(4, feature),
            jnp.zeros((20, feature), F32),
        ],
        axis=0,
    )
    back_yc, given = qkv_back_call(tab, (tok_yc,), 3, dk, dv, w_qkv, ptab, given)
    far = hops.swap_core(back_yc)
    dk, dv = after((dk, dv), g_q)
    g_q.step()
    back_y, given = qkv_back_call(tab, (tok_y,), 2, dk, dv, w_qkv, ptab, given)
    far, dk, dv, back_y = after((far, dk, dv, back_y), g_u, g_d)
    g_d.step()
    far = hops.swap_y((back_y.astype(F32) + far.astype(F32)).astype(BF16))
    back, _, g_small = qkv_back_call(
        tab, (tok, tok_c), 0, dk, dv, w_qkv, ptab, given, (dq, grad_mid)
    )
    back, g_small = after((back, g_small), g_q)
    g_s = summing(g_small[0], g_small[1])
    near = hops.swap_core(back[group:])
    g_s.step(3)
    g_q.step()
    if hops.swaps:
        g_q = Chain(hops.last_sums([jnp.concatenate(p, axis=1) for p in zip(g_q.at, g_s.at)]), 2)
    else:
        g_q = Still(tuple(jnp.concatenate(p, axis=1) for p in zip(g_q.at, g_s.at)))
    g_q.step()
    far, near = after((far, near), g_q)
    input_grad = grad_mid + back[:group].astype(F32) + near.astype(F32) + far.astype(F32)
    g_q, g_u, g_d = g_q.end(), g_u.end(), g_d.end()

    if hops.swaps:

        def rows_of(k):
            down = g_d[:, k * (times // 2) * seg : (k + 1) * (times // 2) * seg]
            part = slice(k * rd, (k + 1) * rd)
            return jnp.concatenate(
                [g_q[part], g_u[part], down[:rd], down[rd:]], axis=1
            )

        mine, other = hops.own_other(rows_of(0), rows_of(1))
        got = hops.swap_core(other.astype(BF16)).astype(F32)
        left, right = hops.sides(mine, got)
        down = [
            under_rows(
                jnp.concatenate([x[:, n_all : n_all + 2 * seg], x[:, n_all + 2 * seg :]], axis=0), 2
            )
            for x in (left, right)
        ]
        grad_down = jnp.concatenate(down, axis=1)
    else:

        def scattered(x):
            return lax.psum_scatter(x, BOTH, scatter_dimension=0, tiled=True)

        left, right = [
            jnp.concatenate(parts, axis=1).astype(F32)
            for parts in zip(*[hops.sides(*g) for g in (g_q, g_u, g_d)])
        ]
        down = [
            x[:, n_all:].reshape(CHIPS, -1, times, seg).transpose(0, 2, 1, 3).reshape(ff, seg)
            for x in (left, right)
        ]
        grad_down = scattered(jnp.concatenate(down, axis=1))
        left, right = scattered(left[:, :n_all]), scattered(right[:, :n_all])

    vecs = left[:, 3 * seg : 3 * seg + 128]
    grad_qkv = jnp.concatenate(
        [x[:, n * seg : (n + 1) * seg] for n in range(3) for x in (left, right)], axis=1
    )
    grad_up = jnp.concatenate([x[:, wide_q : wide_q + n_up] for x in (left, right)], axis=1)
    grad_out = jnp.concatenate([x[:, wide_q + n_up : n_all] for x in (left, right)], axis=1)
    return (
        mixed.reshape(tokens.shape),
        input_grad.astype(BF16).reshape(tokens.shape),
        vecs[:, 0],
        vecs[:, 1],
        grad_qkv,
        vecs[:, 2],
        vecs[:, 3],
        grad_out,
        vecs[:, 4],
        vecs[:, 5],
        vecs[:, 6],
        grad_up,
        vecs[:, 8:12].T.reshape(4 * rd),
        grad_down,
        vecs[:, 7],
        vecs[:, 16 : 16 + FREQS],
    )


def solution(mesh):
    rows = P(BOTH)
    mat = P(BOTH, None)
    act = P("seq", "freq", None)
    in_specs = (
        act, P("seq", "freq"), P("seq", None), act,
        rows, rows, mat, rows, rows, mat, rows, rows, rows, mat, rows, mat, rows, mat,
    )
    out_specs = (
        act, act, rows, rows, mat, rows, rows, mat, rows, rows, rows, mat, rows, mat, rows, mat,
    )
    body = functools.partial(local, n_seq=mesh.shape["seq"], n_freq=mesh.shape["freq"])
    return jax.shard_map(body, mesh=mesh, in_specs=in_specs, out_specs=out_specs, check_vma=False)
```

```python
import functools

import jax
import jax.numpy as jnp
import numpy as np
from jax import lax
from jax.experimental import pallas as pl
from jax.experimental.pallas import tpu as pltpu
from jax.sharding import PartitionSpec as P

HEADS = 12
HEAD_DIM = 64
FREQS = 12
CLIPS = 8
WIN = 128
LARGE = 144
CHIPS = 16
EPS = 1e-06
MASKED = -1e30
BOTH = ("seq", "freq")
F32 = jnp.float32
BF16 = jnp.bfloat16
VMEM_LIMIT = 60 * 1024 * 1024


def params(**kw):
    return pltpu.CompilerParams(vmem_limit_bytes=VMEM_LIMIT, **kw)


def whole():
    return pl.BlockSpec(memory_space=pltpu.VMEM)


def rows_at(parts, r, block):
    each = CHIPS // len(parts)
    return parts[r // each], pl.ds(r % each * block, block)


def smem():
    return pl.BlockSpec(memory_space=pltpu.SMEM)


def hbm():
    return pl.BlockSpec(memory_space=pl.ANY)


def once(shape):
    return pl.BlockSpec(shape, lambda *_: (0,) * len(shape), pipeline_mode=pl.Buffered(1))


def mm(a, b):
    return jnp.dot(a, b, preferred_element_type=F32)


def mm_nt(a, b):
    return lax.dot_general(a, b, (((1,), (1,)), ((), ())), preferred_element_type=F32)


def mm_tn(a, b):
    return lax.dot_general(a, b, (((0,), (0,)), ((), ())), preferred_element_type=F32)


def norm_stats(values):
    center = values - jnp.mean(values, axis=-1, keepdims=True)
    spread = jnp.mean(center * center, axis=-1, keepdims=True)
    inv = lax.rsqrt(spread + EPS)
    return center * inv, inv


def norm_back(vhat, inv, dy, gain):
    gd = dy * gain
    return inv * (
        gd
        - jnp.mean(gd, axis=-1, keepdims=True)
        - vhat * jnp.mean(gd * vhat, axis=-1, keepdims=True)
    )


def row_sum(values):
    return jnp.sum(values, axis=0, keepdims=True)


def embed(tokens, ids, n, ptab):
    count = tokens.shape[0]
    each = count // 128
    pick = lax.broadcasted_iota(jnp.int32, (16, 128), 0)
    wide = ids[:, :128].astype(F32)
    mine = jnp.concatenate(
        [
            jnp.sum(jnp.where(pick == n * each + i, wide, 0.0), axis=0, keepdims=True)
            for i in range(each)
        ],
        axis=1,
    ).astype(jnp.int32)
    row = lax.broadcasted_iota(jnp.int32, (16, count), 0)
    hot = (row == mine).astype(BF16)
    return tokens.astype(F32) + mm_tn(hot, ptab[16:32, :].astype(BF16)), hot


def qkv_kernel(
    tab, t0, t1, t2, t3, i0, i1, i2, i3, own0, own1, oth0, oth1,
    normed, keys, values, queries, hidden, weight, ptab, pm, low0, low1, sems, pm_sems
):
    step = pl.program_id(0)
    feature = weight.shape[0]
    block = feature // CHIPS
    seg = feature // 2
    core = tab[4, 0]
    per = t0.shape[0]

    def copies(cc, vectors):
        made, first = [], []
        for r in range(CHIPS):
            for half, parts in ((cc, (own0, own1)), (1 - cc, (oth0, oth1))):
                ref, src = rows_at(parts, r, block)
                dst = pl.multiple_of(tab[0 if half == cc else 1, r] * block, 16)
                for n in range(0 if vectors else 3):
                    made.append(
                        pltpu.make_async_copy(
                            ref.at[src, pl.ds(n * seg, seg)],
                            weight.at[
                                pl.ds(dst, block), pl.ds(n * feature + half * seg, seg)
                            ],
                            sems.at[len(made)],
                        )
                    )
            if vectors:
                ref, src = rows_at((own0, own1), r, block)
                first.append(
                    pltpu.make_async_copy(
                        ref.at[src, pl.ds(3 * seg, 128)],
                        pm.at[pl.ds(pl.multiple_of(tab[0, r] * block, 16), block), :],
                        pm_sems.at[len(first)],
                    )
                )
        return first if vectors else made

    def on_core(run):
        for cc in (0, 1):

            @pl.when(core == cc)
            def _():
                run(cc)

    def prepare(low):
        tile = jnp.minimum(step, pl.num_programs(0) - 2)
        for piece, (tok, ids) in enumerate(((t0, i0), (t1, i1), (t2, i2), (t3, i3))):
            value, _ = embed(tok[...], ids[...], tile, ptab)
            vhat, _ = norm_stats(value)
            line = (vhat * ptab[0:1, :] + ptab[1:2, :]).astype(BF16)
            normed[piece] = line
            low[piece * per : (piece + 1) * per, :] = line
            if piece == 0:
                hidden[...] = value

    def multiply(low):
        q = mm(low[0:per, :], weight[:, 0:feature]) + ptab[2:3, :]
        queries[...] = q.astype(BF16) * jnp.asarray(HEAD_DIM**-0.5, BF16)
        k = mm(low[...], weight[:, feature : 2 * feature]).astype(BF16)
        v = (mm(low[...], weight[:, 2 * feature :]) + ptab[3:4, :]).astype(BF16)
        for piece in range(4):
            rows = slice(piece * per, (piece + 1) * per)
            keys[piece] = k[rows]
            values[piece] = v[rows]

    @pl.when(step == 0)
    def _():
        def begin(cc):
            first = copies(cc, True)
            for one in first + copies(cc, False):
                one.start()
            for one in first:
                one.wait()

        on_core(begin)
        ptab[...] = pm[...].astype(F32).T[:32, :]
        prepare(low0)

        def finish(cc):
            for one in copies(cc, False):
                one.wait()

        on_core(finish)

    for parity, (before, now) in enumerate(((low1, low0), (low0, low1))):

        @pl.when((step > 0) & (lax.rem(step, 2) == parity))
        def _():
            multiply(before)
            prepare(now)


def qkv_call(tab, pieces, own, oth):
    feature = pieces[0].shape[1]
    group = pieces[0].shape[0] - 16
    per = 128
    steps = group // per
    tok = pl.BlockSpec((per, feature), lambda i: (jnp.minimum(i, steps - 1), 0))
    ids = pl.BlockSpec((16, feature), lambda i: (group // 16, 0))
    now = pl.BlockSpec((4, per, feature), lambda i: (0, jnp.minimum(i, steps - 1), 0))
    before = pl.BlockSpec((4, per, feature), lambda i: (0, jnp.maximum(i - 1, 0), 0))
    out = pl.pallas_call(
        qkv_kernel,
        grid=(steps + 1,),
        in_specs=[smem()] + [tok] * 4 + [ids] * 4 + [hbm()] * 4,
        out_specs=[
            now,
            before,
            before,
            pl.BlockSpec((per, feature), lambda i: (jnp.maximum(i - 1, 0), 0)),
            tok,
            once((feature, 3 * feature)),
            once((32, feature)),
        ],
        out_shape=[
            jax.ShapeDtypeStruct((4, group, feature), BF16),
            jax.ShapeDtypeStruct((4, group, feature), BF16),
            jax.ShapeDtypeStruct((4, group, feature), BF16),
            jax.ShapeDtypeStruct((group, feature), BF16),
            jax.ShapeDtypeStruct((group, feature), F32),
            jax.ShapeDtypeStruct((feature, 3 * feature), BF16),
            jax.ShapeDtypeStruct((32, feature), F32),
        ],
        scratch_shapes=[
            pltpu.VMEM((feature, 128), BF16),
            pltpu.VMEM((4 * per, feature), BF16),
            pltpu.VMEM((4 * per, feature), BF16),
            pltpu.SemaphoreType.DMA((6 * CHIPS,)),
            pltpu.SemaphoreType.DMA((CHIPS,)),
        ],
        compiler_params=params(),
        cost_estimate=pl.CostEstimate(
            flops=2 * group * feature * feature * 9, bytes_accessed=30_000_000, transcendentals=0
        ),
        name="qkv",
    )(tab, *pieces, *pieces, *own, *oth)
    return [x.reshape(4 * group, feature) for x in out[:3]] + list(out[3:])


def window(starts, g, clip, n, group, win=WIN):
    first = starts[g * 16 + clip]
    last = starts[g * 16 + clip + 1]
    lead = (first // 16) * 16 + n * win
    base = pl.multiple_of(jnp.minimum(lead, group - win), 16)
    return base, jnp.maximum(first, lead) - base, last - base


def counts(starts, clip, groups, win=WIN):
    def need(g):
        first = (starts[g * 16 + clip] // 16) * 16
        return (starts[g * 16 + clip + 1] - first + win - 1) // win

    spans = [need(g) for g in groups]
    most = spans[0]
    for s in spans[1:]:
        most = jnp.maximum(most, s)
    return most


def each_clip(starts, one, many):
    together = 4
    for start in range(0, CLIPS, together):
        clips = range(start, start + together)

        def most(win):
            steps = [counts(starts, clip, range(4), win) for clip in clips]
            return functools.reduce(jnp.maximum, steps)

        fits, fits_large = most(WIN) <= 1, most(LARGE) <= 1

        @pl.when(fits)
        def _():
            for clip in clips:
                one(clip, WIN)

        @pl.when(jnp.logical_not(fits) & fits_large)
        def _():
            for clip in clips:
                one(clip, LARGE)

        @pl.when(jnp.logical_not(fits_large))
        def _():
            @pl.loop(0, together)
            def _(i):
                clip = start + i
                many(clip, counts(starts, clip, [0]), counts(starts, clip, range(4)))


def lane_halves():
    lane = lax.broadcasted_iota(jnp.int32, (1, 128), 1)
    left = (lane < HEAD_DIM).astype(BF16)
    return left, 1 - left


def stack_heads(rows):
    left, right = lane_halves()
    return jnp.concatenate([rows * left, rows * right], axis=0)


def merge_heads(stacked):
    win = stacked.shape[0] // 2
    lane = lax.broadcasted_iota(jnp.int32, (win, 128), 1)
    return jnp.where(lane < HEAD_DIM, stacked[:win], stacked[win:])


def row_valid(lo, hi, win=WIN):
    row = lax.broadcasted_iota(jnp.int32, (win, 128), 0)
    return (row >= lo) & (row < hi)


def load_keys(starts, clip, n, group, *refs, win=WIN):
    tiles = [[] for _ in refs]
    spans = []
    for g in range(4):
        base, lo, hi = window(starts, g, clip, n, group, win)
        for t, ref in zip(tiles, refs):
            t.append(ref[pl.ds(pl.multiple_of(g * group + base, 16), win), :])
        spans.append((base, lo, hi))
    return [jnp.concatenate(t, axis=0) for t in tiles], spans


def key_bias_row(spans, win=WIN):
    lane = lax.broadcasted_iota(jnp.int32, (1, 4 * win), 1)
    valid = [
        (lane >= lo + g * win) & (lane < jnp.minimum(hi, win) + g * win)
        for g, (_, lo, hi) in enumerate(spans)
    ]
    return jnp.where(valid[0] | valid[1] | valid[2] | valid[3], 0.0, MASKED)


def key_bias_col(spans, win=WIN):
    row = lax.broadcasted_iota(jnp.int32, (win, 2 * win), 0)
    return jnp.concatenate(
        [jnp.where((row >= lo) & (row < hi), 0.0, MASKED) for _, lo, hi in spans], axis=0
    )


def attn_kernel(starts, q, k, v, *rest, group):
    out, logs = rest[-2:]

    def one(clip, win):
        base, lo, hi = window(starts, 0, clip, 0, group, win)
        stacked = stack_heads(q[pl.ds(base, win), :])
        (kt, vt), spans = load_keys(starts, clip, 0, group, k, v, win=win)
        scores = mm_nt(stacked, kt) + key_bias_row(spans, win)
        peak = jnp.max(scores, axis=1, keepdims=True)
        e = jnp.exp(scores - peak).astype(BF16)
        o = mm(e, jnp.concatenate([vt, jnp.ones((4 * win, 128), BF16)], axis=1))
        total = o[:, 128:]
        logs[0, clip : clip + 1, 0 : 2 * win] = (peak + jnp.log(total)).T[:1]
        o = o[:, :128] * (1.0 / total)
        spot = pl.ds(base, win)
        out[spot, :] = jnp.where(row_valid(lo, hi, win), merge_heads(o).astype(BF16), out[spot, :])

    def many(clip, rows, steps):
        @pl.loop(0, rows)
        def _(i):
            base, lo, hi = window(starts, 0, clip, i, group)
            stacked = stack_heads(q[pl.ds(base, WIN), :])

            def inner(j, carry):
                peak, total, acc = carry
                (kt, vt), spans = load_keys(starts, clip, j, group, k, v)
                scores = mm_nt(stacked, kt) + key_bias_row(spans)
                new = jnp.maximum(peak, jnp.max(scores, axis=1, keepdims=True))
                e = jnp.exp(scores - new)
                shrink = jnp.exp(peak - new)
                return (
                    new,
                    total * shrink + jnp.sum(e, axis=1, keepdims=True),
                    acc * shrink + mm(e.astype(BF16), vt),
                )

            start = (
                jnp.full((2 * WIN, 1), 2 * MASKED, F32),
                jnp.zeros((2 * WIN, 1), F32),
                jnp.zeros((2 * WIN, 128), F32),
            )
            _, total, acc = lax.fori_loop(0, steps, inner, start)
            o = merge_heads(acc * (1.0 / total)).astype(BF16)
            spot = pl.ds(base, WIN)
            out[spot, :] = jnp.where(row_valid(lo, hi), o, out[spot, :])

    each_clip(starts, one, many)


def attn_call(starts, queries, keys, values, part, before=()):
    group, feature = queries.shape
    pairs = feature // 384
    small = pl.BlockSpec((group, 128), lambda i: (0, i + part * pairs))
    large = pl.BlockSpec((4 * group, 128), lambda i: (0, i + part * pairs))
    logs = pl.BlockSpec((1, CLIPS, 384), lambda i: (i + part * pairs, 0, 0))
    return pl.pallas_call(
        functools.partial(attn_kernel, group=group),
        grid=(pairs,),
        in_specs=[smem(), small, large, large] + [hbm()] * len(before),
        out_specs=[small, logs],
        out_shape=[
            jax.ShapeDtypeStruct((group, feature), BF16),
            jax.ShapeDtypeStruct((feature // 128, CLIPS, 384), F32),
        ],
        input_output_aliases={4 + n: n for n in range(len(before))},
        compiler_params=params(),
        cost_estimate=pl.CostEstimate(
            flops=10_000_000_000, bytes_accessed=12_000_000, transcendentals=6_300_000
        ),
        name="attention",
    )(starts, queries, keys, values, *before)


def attn_back_kernel(starts, q, k, v, go, ctx, logs, *rest, group):
    dq, dk, dv, dk_acc, dv_acc, dq_acc = rest[-6:]
    dk_acc[...] = jnp.zeros_like(dk_acc)
    dv_acc[...] = jnp.zeros_like(dv_acc)
    dq_acc[...] = jnp.zeros_like(dq_acc)
    scale = HEAD_DIM**-0.5

    def load_query(clip, i, win=WIN):
        base, lo, hi = window(starts, 0, clip, i, group, win)
        spot = pl.ds(base, win)
        keep = jnp.where(row_valid(lo, hi, win), go[spot, :], jnp.zeros((), BF16))
        return base, stack_heads(q[spot, :]), stack_heads(keep)

    def finish(spans, base, kt, stacked, back, prob, ds, win=WIN):
        ds = ds.astype(BF16)
        dvt = mm(prob.astype(BF16), back)
        dkt = mm(ds, stacked)
        for g, (kb, _, _) in enumerate(spans):
            spot = pl.ds(pl.multiple_of(g * group + kb, 16), win)
            dk_acc[spot, :] += dkt[g * win : (g + 1) * win]
            dv_acc[spot, :] += dvt[g * win : (g + 1) * win]
        spot = pl.ds(base, win)
        dq_acc[spot, :] += merge_heads(mm_tn(ds, kt))

    def one(clip, win):
        base, stacked, back = load_query(clip, 0, win)
        (kt, vt), spans = load_keys(starts, clip, 0, group, k, v, win=win)
        prob = jnp.exp(
            mm_nt(kt, stacked)
            + key_bias_col(spans, win)
            - logs[0, clip : clip + 1, 0 : 2 * win]
        )
        gp = mm_nt(vt, back)
        spot = pl.ds(base, win)
        both = (stack_heads(ctx[spot, :]).astype(F32) * back.astype(F32)).astype(BF16)
        inner = mm_nt(jnp.ones((8, 128), BF16), both)[:1]
        finish(spans, base, kt, stacked, back, prob, prob * (gp - inner), win)

    def many(clip, rows, steps):
        @pl.loop(0, rows)
        def _(i):
            base, stacked, back = load_query(clip, i)

            def totals(j, carry):
                peak, total, inner = carry
                (kt, vt), spans = load_keys(starts, clip, j, group, k, v)
                scores = mm_nt(kt, stacked) + key_bias_col(spans)
                new = jnp.maximum(peak, jnp.max(scores, axis=0, keepdims=True))
                e = jnp.exp(scores - new)
                shrink = jnp.exp(peak - new)
                gp = mm_nt(vt, back)
                return (
                    new,
                    total * shrink + jnp.sum(e, axis=0, keepdims=True),
                    inner * shrink + jnp.sum(e * gp, axis=0, keepdims=True),
                )

            zero = jnp.zeros((1, 2 * WIN), F32)
            peak, total, inner = lax.fori_loop(
                0, steps, totals, (jnp.full((1, 2 * WIN), 2 * MASKED, F32), zero, zero)
            )
            part = 1.0 / total
            inner = inner * part

            @pl.loop(0, steps)
            def _(j):
                (kt, vt), spans = load_keys(starts, clip, j, group, k, v)
                scores = mm_nt(kt, stacked) + key_bias_col(spans)
                prob = jnp.exp(scores - peak) * part
                gp = mm_nt(vt, back)
                finish(spans, base, kt, stacked, back, prob, prob * (gp - inner))

    each_clip(starts, one, many)

    dq[...] = (dq_acc[...] * scale).astype(BF16)
    dk[...] = dk_acc[...].astype(BF16)
    dv[...] = dv_acc[...].astype(BF16)


def attn_back_call(starts, queries, keys, values, grad_context, context, logs, part, before=()):
    group, feature = queries.shape
    pairs = feature // 384
    small = pl.BlockSpec((group, 128), lambda i: (0, i + part * pairs))
    large = pl.BlockSpec((4 * group, 128), lambda i: (0, i + part * pairs))
    return pl.pallas_call(
        functools.partial(attn_back_kernel, group=group),
        grid=(pairs,),
        in_specs=[smem(), small, large, large, small, small]
        + [pl.BlockSpec((1, CLIPS, 384), lambda i: (i + part * pairs, 0, 0))]
        + [hbm()] * len(before),
        out_specs=[small, large, large],
        out_shape=[
            jax.ShapeDtypeStruct((group, feature), BF16),
            jax.ShapeDtypeStruct((4 * group, feature), BF16),
            jax.ShapeDtypeStruct((4 * group, feature), BF16),
        ],
        input_output_aliases={7 + n: n for n in range(len(before))},
        scratch_shapes=[
            pltpu.VMEM((4 * group, 128), F32),
            pltpu.VMEM((4 * group, 128), F32),
            pltpu.VMEM((group, 128), F32),
        ],
        compiler_params=params(),
        cost_estimate=pl.CostEstimate(
            flops=20_000_000_000, bytes_accessed=24_000_000, transcendentals=6_300_000
        ),
        name="attention_back",
    )(starts, queries, keys, values, grad_context, context, logs, *before)


def phi_parts(u):
    t = 1.0 / (1.0 + (0.3275911 * 0.5**0.5) * jnp.abs(u))
    e = jnp.exp(u * u * -0.5)
    poly = t * (
        0.127414796
        + t * (-0.142248368 + t * (0.7107068705 + t * (-0.7265760135 + t * 0.5307027145)))
    )
    tail = poly * e
    return jnp.where(u < 0, tail, 1.0 - tail), e * 0.3989422804014327


def middle_kernel(
    tab, ctx, hidden, ups, ptab, up_bias, u_own0, u_own1, u_oth0, u_oth1, d_own0, d_own1, d_oth0, d_oth1,
    mixed, grad_mid, grad_ctx, gu_own, gu_oth, gd_own, gd_oth, small, g_up_bias,
    w_up, w_dn, w_out, mid, sec, sec_t, acc, gsec, act, gup, t_up, t_dn, in_sems, up_sems, dn_sems,
    *, chunks
):
    j = pl.program_id(0)
    group, feature = ctx.shape
    block = feature // CHIPS
    dblock = w_dn.shape[0] // CHIPS
    seg = feature // 2
    part = w_dn.shape[0] // chunks
    per_half = chunks // 2
    core = tab[4, 0]
    tile = 256
    tiles = group // tile

    def loads(cc, part_of):
        made = []
        count = 0

        def add(src, dst, kind):
            nonlocal count
            if kind == part_of:
                made.append(pltpu.make_async_copy(src, dst, in_sems.at[count]))
            count += 1

        for r in range(CHIPS):
            for half, up, down, row in (
                (cc, (u_own0, u_own1), (d_own0, d_own1), 0),
                (1 - cc, (u_oth0, u_oth1), (d_oth0, d_oth1), 1),
            ):
                ref, src = rows_at(up, r, block)
                dref, _ = rows_at(down, r, block)
                chip = tab[row, r]
                dst = pl.ds(pl.multiple_of(chip * block, 16), block)
                add(
                    ref.at[src, pl.ds(per_half * part, seg)],
                    w_out.at[dst, pl.ds(half * seg, seg)],
                    0,
                )
                for n in range(per_half):
                    add(
                        ref.at[src, pl.ds(n * part, part)],
                        w_up.at[half * per_half + n, dst, :],
                        1,
                    )
                for n in range(dblock // block):
                    row0 = pl.multiple_of(chip * dblock + n * block, 16)
                    add(
                        dref.at[src, pl.ds(n * seg, seg)],
                        w_dn.at[pl.ds(row0, block), pl.ds(half * seg, seg)],
                        1,
                    )
        return made

    def for_core(run):
        for cc in (0, 1):

            @pl.when(core == cc)
            def _():
                run(cc)

    @pl.when(j == 0)
    def _():
        def run(cc):
            first = loads(cc, 0)
            for one in first + loads(cc, 1):
                one.start()
            for one in first:
                one.wait()

        for_core(run)
        for t in range(tiles):
            rows = slice(t * tile, (t + 1) * tile)
            value = hidden[rows, :] + mm(ctx[rows, :], w_out[...]) + ptab[4:5, :]
            mid[rows, :] = value
            vhat, _ = norm_stats(value)
            low = (vhat * ptab[5:6, :] + ptab[6:7, :]).astype(BF16)
            sec[rows, :] = low
            sec_t[:, rows] = low.T
            acc[rows, :] = value + ptab[7:8, :]
            gsec[rows, :] = jnp.zeros((tile, feature), F32)

        def rest(cc):
            for one in loads(cc, 1):
                one.wait()

        for_core(rest)

    slot = lax.rem(j, 2)

    def drain(sl):
        for r in range(CHIPS):
            pltpu.make_async_copy(
                t_up.at[sl, pl.ds(0, block), :],
                gu_own.at[pl.ds(0, block), pl.ds(0, part)],
                up_sems.at[sl, r],
            ).wait()
        for n in range(2 * (part // block)):
            pltpu.make_async_copy(
                t_dn.at[sl, pl.ds(0, block), pl.ds(0, seg)],
                gd_own.at[pl.ds(0, block), pl.ds(0, seg)],
                dn_sems.at[sl, n],
            ).wait()

    upj = w_up[j]
    dnj = w_dn[pl.ds(pl.multiple_of(j * part, 128), part), :]
    bias = up_bias[pl.ds(j, 1), :]
    gub = jnp.zeros((1, part), F32)
    cuts = [slice(t * tile, (t + 1) * tile) for t in range(tiles)]

    def products(t):
        return mm(sec[cuts[t], :], upj) + bias, mm_nt(ups[cuts[t], :], dnj)

    ahead = products(0)
    for t in range(tiles):
        u, ga = ahead
        if t + 1 < tiles:
            ahead = products(t + 1)
        rows = cuts[t]
        dist, dens = phi_parts(u)
        a = (u * dist).astype(BF16)
        g = (ga * (dist + u * dens)).astype(BF16)
        act[rows, :] = a
        gup[rows, :] = g
        gub = gub + row_sum(g.astype(F32))
        if t > 0:
            acc[cuts[t - 1], :] += mm(act[cuts[t - 1], :], dnj)
            gsec[cuts[t - 1], :] += mm_nt(gup[cuts[t - 1], :], upj)
    acc[cuts[-1], :] += mm(act[cuts[-1], :], dnj)
    gsec[cuts[-1], :] += mm_nt(gup[cuts[-1], :], upj)
    g_up_bias[pl.ds(j, 1), :] = gub

    @pl.when(j >= 2)
    def _():
        drain(slot)

    t_up[slot] = mm(sec_t[...], gup[...]).astype(BF16)
    t_dn[slot] = mm_tn(act[...], ups[...]).astype(BF16)

    def send(cc):
        col = pl.ds(pl.multiple_of(lax.rem(j, per_half) * part, 128), part)
        for is_own in (True, False):
            ref = gu_own if is_own else gu_oth

            @pl.when((j // per_half == cc) == is_own)
            def _():
                for r in range(CHIPS):
                    src = pl.ds(pl.multiple_of(tab[0 if is_own else 1, r] * block, 16), block)
                    pltpu.make_async_copy(
                        t_up.at[slot, src, :],
                        ref.at[pl.ds(r * block, block), col],
                        up_sems.at[slot, r],
                    ).start()

        n = 0
        count = part // dblock
        for half, ref, row in ((cc, gd_own, 2), (1 - cc, gd_oth, 3)):
            for i in range(count):
                place = pl.multiple_of(tab[row, j * count + i] * block, 16)
                for m in range(dblock // block):
                    pltpu.make_async_copy(
                        t_dn.at[
                            slot, pl.ds(i * dblock + m * block, block), pl.ds(half * seg, seg)
                        ],
                        ref.at[pl.ds(place, block), pl.ds(m * seg, seg)],
                        dn_sems.at[slot, n],
                    ).start()
                    n += 1

    for_core(send)

    @pl.when(j == chunks - 1)
    def _():
        s_gain = jnp.zeros((1, feature), F32)
        s_shift = jnp.zeros((1, feature), F32)
        s_out = jnp.zeros((1, feature), F32)
        s_down = jnp.zeros((1, feature), F32)
        for t in range(tiles):
            rows = slice(t * tile, (t + 1) * tile)
            mixed[rows, :] = acc[rows, :].astype(BF16)
            vhat, inv = norm_stats(mid[rows, :])
            dy = gsec[rows, :]
            wide = ups[rows, :].astype(F32)
            gm = wide + norm_back(vhat, inv, dy, ptab[5:6, :])
            grad_mid[rows, :] = gm
            low = gm.astype(BF16)
            gup[rows, :] = low
            grad_ctx[rows, :] = mm_nt(low, w_out[...]).astype(BF16)
            s_gain = s_gain + row_sum(dy * vhat)
            s_shift = s_shift + row_sum(dy)
            s_out = s_out + row_sum(gm)
            s_down = s_down + row_sum(wide)
        zero = jnp.zeros((1, feature), F32)
        small[...] = jnp.concatenate(
            [zero, zero, zero, zero, s_out, s_gain, s_shift, s_down], axis=0
        )
        drain(1 - slot)
        act[...] = mm_tn(ctx[...], gup[...]).astype(BF16)

        def run(cc):
            made = []
            for half, ref, row in ((cc, gu_own, 0), (1 - cc, gu_oth, 1)):
                for r in range(CHIPS):
                    src = pl.ds(pl.multiple_of(tab[row, r] * block, 16), block)
                    made.append(
                        pltpu.make_async_copy(
                            act.at[src, pl.ds(half * seg, seg)],
                            ref.at[pl.ds(r * block, block), pl.ds(per_half * part, seg)],
                            in_sems.at[len(made)],
                        )
                    )
            for one in made:
                one.start()
            for one in made:
                one.wait()

        for_core(run)
        drain(slot)


def middle_call(tab, ctx, hidden, ups, ptab, up_bias, up_pair, down_pair, ff):
    group, feature = hidden.shape
    chunks = ff // feature
    part = ff // chunks
    return pl.pallas_call(
        functools.partial(middle_kernel, chunks=chunks),
        grid=(chunks,),
        in_specs=[
            smem(),
            once((group, feature)),
            once((group, feature)),
            once((group, feature)),
            once((32, feature)),
            once((chunks, part)),
            *[hbm()] * 8,
        ],
        out_specs=[
            once((group, feature)),
            once((group, feature)),
            once((group, feature)),
            hbm(), hbm(), hbm(), hbm(),
            once((8, feature)),
            once((chunks, part)),
        ],
        out_shape=[
            jax.ShapeDtypeStruct((group, feature), BF16),
            jax.ShapeDtypeStruct((group, feature), F32),
            jax.ShapeDtypeStruct((group, feature), BF16),
            *[jax.ShapeDtypeStruct((feature, up_pair[0][0].shape[1]), BF16)] * 2,
            *[jax.ShapeDtypeStruct((feature, down_pair[0][0].shape[1]), BF16)] * 2,
            jax.ShapeDtypeStruct((8, feature), F32),
            jax.ShapeDtypeStruct((chunks, part), F32),
        ],
        scratch_shapes=[
            pltpu.VMEM((chunks, feature, part), BF16),
            pltpu.VMEM((ff, feature), BF16),
            pltpu.VMEM((feature, feature), BF16),
            pltpu.VMEM((group, feature), F32),
            pltpu.VMEM((group, feature), BF16),
            pltpu.VMEM((feature, group), BF16),
            pltpu.VMEM((group, feature), F32),
            pltpu.VMEM((group, feature), F32),
            pltpu.VMEM((group, part), BF16),
            pltpu.VMEM((group, part), BF16),
            pltpu.VMEM((2, feature, part), BF16),
            pltpu.VMEM((2, part, feature), BF16),
            pltpu.SemaphoreType.DMA((2 * CHIPS * (1 + chunks // 2 + ff // feature),)),
            pltpu.SemaphoreType.DMA((2, CHIPS)),
            pltpu.SemaphoreType.DMA((2, 2 * CHIPS)),
        ],
        compiler_params=params(),
        cost_estimate=pl.CostEstimate(
            flops=2 * group * feature * (3 * feature + 6 * ff),
            bytes_accessed=34_000_000,
            transcendentals=2 * group * ff,
        ),
        name="middle",
    )(tab, ctx, hidden, ups, ptab, up_bias, *sum(up_pair + down_pair, ()))


def qkv_weight_kernel(tab, normed, dq, dk, dv, own, oth, norm_t, tmp, sems, *, blocks):
    step = pl.program_id(0)
    total, feature = normed.shape
    group = dq.shape[0]
    block = feature // CHIPS
    seg = feature // 2
    core = tab[4, 0]

    def stores(cc, n):
        made = []
        for half, ref, row in ((cc, own, 0), (1 - cc, oth, 1)):
            for r in range(CHIPS):
                src = pl.ds(pl.multiple_of(tab[row, r] * block, 16), block)
                made.append(
                    pltpu.make_async_copy(
                        tmp.at[n, src, pl.ds(half * seg, seg)],
                        ref.at[pl.ds(r * block, block), pl.ds(n * seg, seg)],
                        sems.at[n, len(made)],
                    )
                )
        return made

    def on_core(run):
        for cc in (0, 1):

            @pl.when(core == cc)
            def _():
                run(cc)

    def start(n):
        def run(cc):
            for one in stores(cc, n):
                one.start()

        on_core(run)

    @pl.when(step == 0)
    def _():
        tile = 256
        for t in range(total // tile):
            rows = slice(t * tile, (t + 1) * tile)
            norm_t[:, rows] = normed[rows, :].T
        tmp[0] = mm(norm_t[:, :group], dq[...]).astype(BF16)
        start(0)

    cut = feature // blocks
    for n, ref in ((1, dk), (2, dv)):
        for i in range(blocks):

            @pl.when(step == 1 + (n - 1) * blocks + i)
            def _():
                tmp[n, :, i * cut : (i + 1) * cut] = mm(norm_t[...], ref[...]).astype(BF16)
                if i == blocks - 1:
                    start(n)

    @pl.when(step == 2 * blocks)
    def _():
        def finish(cc):
            for n in range(3):
                for one in stores(cc, n):
                    one.wait()

        on_core(finish)


def qkv_weight_call(tab, normed, dq, dk, dv):
    total, feature = normed.shape
    half = 3 * feature // 2
    blocks = 3
    cut = feature // blocks
    return pl.pallas_call(
        functools.partial(qkv_weight_kernel, blocks=blocks),
        grid=(1 + 2 * blocks,),
        in_specs=[
            smem(),
            once(normed.shape),
            once(dq.shape),
            pl.BlockSpec((total, cut), lambda i: (0, jnp.clip(i - 1, 0, blocks - 1))),
            pl.BlockSpec((total, cut), lambda i: (0, jnp.clip(i - 1 - blocks, 0, blocks - 1))),
        ],
        out_specs=[hbm(), hbm()],
        out_shape=[jax.ShapeDtypeStruct((feature, half), BF16)] * 2,
        scratch_shapes=[
            pltpu.VMEM((feature, total), BF16),
            pltpu.VMEM((3, feature, feature), BF16),
            pltpu.SemaphoreType.DMA((3, 2 * CHIPS)),
        ],
        compiler_params=params(),
        cost_estimate=pl.CostEstimate(
            flops=2 * dq.shape[0] * feature * feature * 9,
            bytes_accessed=20_000_000,
            transcendentals=0,
        ),
        name="qkv_weight",
    )(tab, normed, dq, dk, dv)


def qkv_back_kernel(*refs, group, own_rows):
    tab, refs = refs[0], refs[1:]
    n_pieces = 2 if own_rows else 1
    toks, idss, refs = refs[:n_pieces], refs[n_pieces : 2 * n_pieces], refs[2 * n_pieces :]
    dk, dv, weight, ptab, given = refs[:5]
    refs = refs[5:]
    if own_rows:
        dq, gm, out, sums, small, moved, sems = refs
    else:
        out, sums = refs
    step = pl.program_id(0)
    feature = weight.shape[0]
    steps = group // out.shape[0]

    @pl.when(step == 0)
    def _():
        sums[...] = given[...]

    def body(tok, ids, own):
        value, hot = embed(tok[...], ids[...], lax.rem(step, steps), ptab)
        vhat, inv = norm_stats(value)
        dy = mm_nt(dk[...], weight[:, feature : 2 * feature]) + mm_nt(
            dv[...], weight[:, 2 * feature :]
        )
        if own:
            dy = dy + mm_nt(dq[...], weight[:, 0:feature])
            sums[2:3, :] += row_sum(dq[...].astype(F32))
        grad = norm_back(vhat, inv, dy, ptab[0:1, :])
        out[...] = grad.astype(BF16)
        sums[0:1, :] += row_sum(dy * vhat)
        sums[1:2, :] += row_sum(dy)
        sums[3:4, :] += row_sum(dv[...].astype(F32))
        if own:
            grad = grad + gm[...]
        high = grad.astype(BF16)
        rest = (grad - high.astype(F32)).astype(BF16)
        sums[16:32, :] += mm(hot, high) + mm(hot, rest)

    if own_rows:

        @pl.when(step < steps)
        def _():
            body(toks[0], idss[0], True)

        @pl.when(step >= steps)
        def _():
            body(toks[1], idss[1], False)

    else:
        body(toks[0], idss[0], False)

    if own_rows:

        @pl.when(step == 2 * steps - 1)
        def _():
            turned = jnp.concatenate([sums[...], jnp.zeros((96, feature), F32)], axis=0).T
            moved[...] = turned.astype(BF16)
            block = feature // CHIPS
            made = []
            for side in range(2):
                for r in range(CHIPS):
                    src = pl.ds(pl.multiple_of(tab[side, r] * block, 16), block)
                    made.append(
                        pltpu.make_async_copy(
                            moved.at[src, :],
                            small.at[side, pl.ds(r * block, block), :],
                            sems.at[side, r],
                        )
                    )
            for one in made:
                one.start()
            for one in made:
                one.wait()


def qkv_back_call(tab, pair, first_piece, dk, dv, weight, ptab, given, own=()):
    feature = dk.shape[1]
    group = pair[0].shape[0] - 16
    per = 256
    steps = group // per
    skip = first_piece * steps
    count = len(pair)

    def at(piece):
        return pl.BlockSpec(
            (per, feature), lambda i: (jnp.clip(i - piece * steps, 0, steps - 1), 0)
        )

    ids = pl.BlockSpec((16, feature), lambda i: (group // 16, 0))
    tile = pl.BlockSpec((per, feature), lambda i: (i, 0))
    later = pl.BlockSpec((per, feature), lambda i: (i + skip, 0))
    first = pl.BlockSpec((per, feature), lambda i: (jnp.minimum(i, steps - 1), 0))
    return pl.pallas_call(
        functools.partial(qkv_back_kernel, group=group, own_rows=bool(own)),
        grid=(count * steps,),
        in_specs=[smem()]
        + [at(n) for n in range(count)]
        + [ids] * count
        + [later, later]
        + [once((feature, 3 * feature)), once((32, feature)), once((32, feature))]
        + [first] * len(own),
        out_specs=[tile, once((32, feature))] + [hbm()] * bool(own),
        out_shape=[
            jax.ShapeDtypeStruct((count * group, feature), BF16),
            jax.ShapeDtypeStruct((32, feature), F32),
            jax.ShapeDtypeStruct((2, feature, 128), BF16),
        ][: 2 + bool(own)],
        scratch_shapes=[pltpu.VMEM((feature, 128), BF16), pltpu.SemaphoreType.DMA((2, CHIPS))][
            : 2 * bool(own)
        ],
        compiler_params=params(),
        cost_estimate=pl.CostEstimate(
            flops=group * feature * feature * 9, bytes_accessed=15_000_000, transcendentals=0
        ),
        name="qkv_back",
    )(tab, *pair, *pair, dk, dv, weight, ptab, given, *own)


def payload_kernel(tab, *refs, rd, times):
    vecs, (up_bias, table, qkv, up, out, down, mine, other, lines) = refs[:8], refs[8:]
    feature = down.shape[1]
    seg = feature // 2
    ff = up.shape[1]
    core = tab[4, 0]
    lines[...] = jnp.zeros_like(lines)
    for n, vec in enumerate(vecs):
        lines[n : n + 1, 0:rd] = vec[...].astype(F32)
    for n in range(4):
        lines[8 + n : 9 + n, 0:rd] = up_bias[:, n * rd : (n + 1) * rd].astype(F32)

    def places(rows, first):
        row = lax.broadcasted_iota(jnp.int32, (rows, 128), 0)
        return (lax.broadcasted_iota(jnp.int32, (rows, 128), 1) == row + first).astype(BF16)

    small = mm_tn(lines[...].astype(BF16), places(16, 0))[:rd] + mm(table[...], places(FREQS, 16))
    small = small.astype(BF16)
    wide = down[...].astype(F32)

    def fill(ref, h):
        at = 0

        def put(value):
            nonlocal at
            ref[:, at : at + value.shape[1]] = value
            at += value.shape[1]

        for n in range(3):
            put(qkv[:, n * feature + h * seg : n * feature + (h + 1) * seg])
        put(small)
        put(up[:, h * (ff // 2) : (h + 1) * (ff // 2)])
        put(out[:, h * seg : (h + 1) * seg])
        for n in range(times):
            put(wide[n * rd : (n + 1) * rd, h * seg : (h + 1) * seg].astype(BF16))

    for cc in (0, 1):

        @pl.when(core == cc)
        def _():
            fill(mine, cc)
            fill(other, 1 - cc)


def payload_call(tab, vecs, up_bias, table, qkv, up, out, down):
    rd, times = qkv.shape[0], down.shape[0] // qkv.shape[0]
    half = (qkv.shape[1] + up.shape[1] + out.shape[1] + times * down.shape[1]) // 2 + 128
    return pl.pallas_call(
        functools.partial(payload_kernel, rd=rd, times=times),
        in_specs=[smem()] + [whole()] * (len(vecs) + 6),
        out_specs=[whole(), whole()],
        out_shape=[jax.ShapeDtypeStruct((rd, half), BF16)] * 2,
        scratch_shapes=[pltpu.VMEM((16, 128), F32)],
        compiler_params=params(),
        name="payload",
    )(tab, *[v.reshape(1, -1) for v in vecs], up_bias.reshape(1, -1), table, qkv, up, out, down)


def pair_kernel(tab, mine, got, for_q, for_u, for_d, *, widths):
    rd = mine.shape[0]
    n_q, n_u, times, seg = widths
    core = tab[4, 0]

    def fill(top, low):
        for ref, start, width in ((for_q, 0, n_q), (for_u, n_q, n_u)):
            cols = slice(start, start + width)
            ref[...] = jnp.concatenate(
                [top[:, cols].astype(F32), low[:, cols].astype(F32)], axis=0
            ).astype(BF16)
        for block in range(times):
            part = top if block < times // 2 else low
            start = n_q + n_u + (block % (times // 2)) * 2 * seg
            rows = [part[:, start + i * seg : start + (i + 1) * seg].astype(F32) for i in (0, 1)]
            for_d[:, block * seg : (block + 1) * seg] = jnp.concatenate(rows, axis=0).astype(BF16)

    for cc in (0, 1):

        @pl.when(core == cc)
        def _():
            fill(*((mine, got) if cc == 0 else (got, mine)))


def pair_call(tab, mine, got, widths):
    rd = mine.shape[0]
    n_q, n_u, times, seg = widths
    return pl.pallas_call(
        functools.partial(pair_kernel, widths=widths),
        in_specs=[smem(), whole(), whole()],
        out_specs=[whole()] * 3,
        out_shape=[jax.ShapeDtypeStruct((2 * rd, n), BF16) for n in (n_q, n_u, times * seg)],
        compiler_params=params(),
        name="pair",
    )(tab, mine, got)


def tail_rows_kernel(tokens, ids, out):
    group, feature = tokens.shape
    out[0:group, :] = tokens[...]
    rows = [ids[:, n * 128 : (n + 1) * 128].astype(F32) for n in range(group // 128)]
    rows = jnp.concatenate(rows + [jnp.zeros((16 - len(rows), 128), F32)], axis=0).astype(BF16)
    out[group : group + 16, :] = jnp.concatenate(
        [rows, jnp.zeros((16, feature - 128), BF16)], axis=1
    )


def tail_rows_call(tokens, ids):
    group, feature = tokens.shape
    return pl.pallas_call(
        tail_rows_kernel,
        in_specs=[whole(), whole()],
        out_specs=whole(),
        out_shape=jax.ShapeDtypeStruct((group + 16, feature), BF16),
        compiler_params=params(),
        name="tail_rows",
    )(tokens, ids)


class Hops:
    def __init__(self, n_seq, n_freq):
        self.n_seq, self.n_freq = n_seq, n_freq
        self.swaps = n_seq == 8 and n_freq == 4
        self.core = lax.axis_index("freq") % 2
        self.first = self.core == 0
        chip = lax.axis_index("seq") * 2 + lax.axis_index("freq") // 2
        if self.swaps:
            bits = ((4, 8, 2, 1), (4, 8, 1, 2))
            masks = np.zeros((2, CHIPS), np.int32)
            for c in (0, 1):
                for r in range(CHIPS):
                    for b in range(4):
                        if r >> b & 1:
                            masks[c, r] ^= bits[c][b]
            one, two = jnp.asarray(masks[0]), jnp.asarray(masks[1])
            mine = jnp.where(self.first, one, two) ^ chip
            theirs = jnp.where(self.first, two, one) ^ chip

            def places(order):
                rows = (order[:, None] == jnp.arange(CHIPS)[None, :]).astype(jnp.int32)
                return jnp.sum(rows * jnp.arange(CHIPS, dtype=jnp.int32)[:, None], axis=0)

            rows = [mine, theirs, places(mine), places(theirs)]
        else:
            rows = [jnp.arange(CHIPS, dtype=jnp.int32)] * 4
        rows = [r.astype(jnp.int32) for r in rows]
        rows += [jnp.full((CHIPS,), self.core, jnp.int32)] + [rows[0]] * 3
        self.table = jnp.stack(rows)

    def swap(self, values, move):
        pairs = []
        for s in range(self.n_seq):
            for f in range(self.n_freq):
                ds, df = move(f % 2)
                pairs.append((s * self.n_freq + f, (s ^ ds) * self.n_freq + (f ^ df)))
        return lax.ppermute(values, BOTH, pairs)

    def swap_core(self, values):
        return self.swap(values, lambda c: (0, 1))

    def swap_y(self, values):
        return self.swap(values, lambda c: (0, 2))

    def swap_z(self, values, n):
        return self.swap(values, lambda c: (2 * n, 0))

    def swap_xy(self, values, n):
        return self.swap(values, lambda c: (1, 0) if c == n else (0, 2))

    def sides(self, mine, other):
        return jnp.where(self.first, mine, other), jnp.where(self.first, other, mine)

    def own_other(self, left, right):
        return jnp.where(self.first, left, right), jnp.where(self.first, right, left)

    def gather(self, held):
        parts = yield [held] + [self.swap_z(held, n) for n in (1, 2, 3)]
        held = jnp.concatenate(parts, axis=0)
        parts = yield held, self.swap_xy(held, 0)
        held = jnp.concatenate(parts, axis=0)
        held, got, across = yield held, self.swap_xy(held, 1), self.swap_core(held)
        yield (held, got), (across, self.swap_core(got))

    def scatter(self, own, other):
        own, got = yield own, self.swap_core(other)
        add = self.add
        for n in (1, 0):
            cut = own.shape[0] // 2
            send = add(own[cut:], got[cut:])
            own = add(own[:cut], got[:cut])
            own, got = yield own, self.swap_xy(send, n)
        yield from self.last_sums((own, got))

    @staticmethod
    def add(a, b):
        return (a.astype(F32) + b.astype(F32)).astype(BF16)

    def last_sums(self, pair):
        own, got = pair
        add = self.add
        cut = own.shape[0] // 4
        sends = [add(own[n * cut : (n + 1) * cut], got[n * cut : (n + 1) * cut]) for n in (1, 2, 3)]
        own = own[:cut].astype(F32) + got[:cut].astype(F32)
        own, got = yield own, [self.swap_z(send, n) for n, send in zip((1, 2, 3), sends)]
        yield own + sum(g.astype(F32) for g in got)


class Chain:
    def __init__(self, steps, count):
        self.steps, self.left, self.at = steps, count, None

    def step(self, times=1):
        for _ in range(times):
            self.at = next(self.steps) if self.at is None else self.steps.send(self.at)
            self.left -= 1
        return self.at

    def end(self):
        return self.step(self.left)


class Still:
    def __init__(self, value):
        self.at = value

    def step(self, times=1):
        return self.at

    end = step


def after(values, *chains):
    values, held = lax.optimization_barrier((values, tuple(c.at for c in chains)))
    for c, h in zip(chains, held):
        c.at = h
    return values


def col_halves(*arrays):
    left = [a[:, : a.shape[1] // 2] for a in arrays]
    right = [a[:, a.shape[1] // 2 :] for a in arrays]
    return left, right


def side_rows(down, count):
    rows, cols = down.shape
    return down.reshape(count, rows // count, cols).transpose(1, 0, 2).reshape(rows // count, -1)


def under_rows(wide, count):
    rows, cols = wide.shape
    return wide.reshape(rows, count, cols // count).transpose(1, 0, 2).reshape(rows * count, -1)


def local(
    tokens,
    freq_ids,
    clip_ids,
    cotangent,
    ln1_gain,
    first_norm_bias,
    qkv_weight,
    q_bias,
    v_bias,
    out_weight,
    out_bias,
    ln2_gain,
    ln2_bias,
    up_weight,
    up_bias,
    down_weight,
    down_bias,
    freq_table,
    *,
    n_seq,
    n_freq,
):
    _, group, feature = tokens.shape
    rd = qkv_weight.shape[0]
    n_dev = n_seq * n_freq
    seg = feature // 2
    ff = up_weight.shape[1]
    times = ff // feature
    hops = Hops(n_seq, n_freq)
    tab = hops.table

    tok = tail_rows_call(tokens.reshape(group, feature), freq_ids.reshape(1, group))
    vectors = [ln1_gain, first_norm_bias, q_bias, v_bias, out_bias, ln2_gain, ln2_bias, down_bias]
    wide_q = 3 * seg + 128
    n_up = ff // 2
    n_uo = n_up + seg
    n_all = wide_q + n_uo
    tok_c, tok_y = hops.swap_core(tok), hops.swap_y(tok)
    if hops.swaps:
        mine, other = payload_call(
            tab, vectors, up_bias, freq_table, qkv_weight, up_weight, out_weight, down_weight
        )
        held = pair_call(tab, mine, hops.swap_core(other), (wide_q, n_uo, times, seg))
        weights, ups, downs = [Chain(hops.gather(h), 4) for h in held]
    else:

        def full(x):
            return lax.all_gather(x, BOTH, axis=0, tiled=True)

        lines = jnp.concatenate(vectors + [up_bias]).reshape(12, rd)
        small = jnp.concatenate(
            [lines, jnp.zeros((4, rd), BF16), freq_table.T, jnp.zeros((100, rd), BF16)], axis=0
        ).T
        f_qkv, f_small, f_up = full(qkv_weight), full(small), full(up_weight)
        f_out, f_down = full(out_weight), full(down_weight)
        q_full = [f_qkv[:, n * feature : (n + 1) * feature] for n in range(3)]
        down_side = f_down.reshape(CHIPS, times, -1, feature).transpose(0, 2, 1, 3)
        down_side = down_side.reshape(feature, times, 2, seg)
        sides_q, sides_u, sides_d = [], [], []
        for h in (0, 1):
            sides_q.append(jnp.concatenate(col_halves(*q_full)[h] + [f_small], axis=1))
            sides_u.append(jnp.concatenate(col_halves(f_up, f_out)[h], axis=1))
            sides_d.append(down_side[:, :, h].reshape(feature, times * seg))
        cut = feature // 2
        weights, ups, downs = [
            Still(tuple((x[:cut], x[cut:]) for x in hops.own_other(*sides)))
            for sides in (sides_q, sides_u, sides_d)
        ]

    weights.step()
    tok_c = after(tok_c, weights)
    ups.step()
    weights.step()
    tok_y = after(tok_y, weights)
    weights.step()
    tok_yc = hops.swap_core(tok_y)
    tok_c = after(tok_c, weights, ups)
    ups.step()
    downs.step()
    weights.end()
    pieces = (tok, tok_c, tok_y, tok_yc)

    place = lax.axis_index("freq")
    order = jnp.stack([place, place ^ 1, place ^ 2, place ^ 3])
    below = clip_ids.reshape(n_freq, group)[:, None, :] < jnp.arange(16, dtype=jnp.int32)[None, :, None]
    first_rows = jnp.sum(below.astype(jnp.int32), axis=2)
    pick = (order[:, None] == jnp.arange(n_freq)[None, :]).astype(jnp.int32)
    starts = jnp.sum(pick[:, :, None] * first_rows[None, :, :], axis=1).reshape(4 * 16)

    normed, keys, values, queries, hidden, w_qkv, ptab = qkv_call(tab, pieces, *weights.at)
    queries, keys, values = after((queries, keys, values), ups, downs)
    ups.step()
    downs.step()
    context = attn_call(starts, queries, keys, values, 0)
    queries, context = after((queries, context), downs)
    downs.step()
    context = attn_call(starts, queries, keys, values, 1, context)
    queries, context = after((queries, context), ups, downs)
    ups.step()
    downs.step()
    context = attn_call(starts, queries, keys, values, 2, context)
    up_rows = ptab[8:12].reshape(4, n_dev, rd).transpose(1, 0, 2).reshape(times, feature)
    upstream = cotangent.reshape(group, feature)
    context, logs = context
    mixed, grad_mid, grad_ctx, *sent, sums, g_up_bias = middle_call(
        tab, context, hidden, upstream, ptab, up_rows, ups.at, downs.at, ff
    )

    def summing(own, oth):
        return Chain(hops.scatter(own, oth), 5) if hops.swaps else Still((own, oth))

    g_u, g_d = summing(*sent[:2]), summing(*sent[2:])
    g_u.step()
    g_d.step()
    grads = attn_back_call(starts, queries, keys, values, grad_ctx, context, logs, 0)
    grads, queries = after((grads, queries), g_u, g_d)
    g_u.step()
    grads = attn_back_call(starts, queries, keys, values, grad_ctx, context, logs, 1, grads)
    grads, queries = after((grads, queries), g_u, g_d)
    g_d.step()
    grads = attn_back_call(starts, queries, keys, values, grad_ctx, context, logs, 2, grads)
    dq, dk, dv = after(grads, g_u, g_d)
    g_u.step()
    g_d.step()
    g_q = qkv_weight_call(tab, normed, dq, dk, dv)
    g_q, dk, dv = after((g_q, dk, dv), g_u, g_d)
    g_q = summing(*g_q)
    g_q.step()
    g_u.step()
    given = jnp.concatenate(
        [
            sums,
            g_up_bias.reshape(n_dev, 4, rd).transpose(1, 0, 2).reshape(4, feature),
            jnp.zeros((20, feature), F32),
        ],
        axis=0,
    )
    back_yc, given = qkv_back_call(tab, (tok_yc,), 3, dk, dv, w_qkv, ptab, given)
    far = hops.swap_core(back_yc)
    dk, dv = after((dk, dv), g_q)
    g_q.step()
    back_y, given = qkv_back_call(tab, (tok_y,), 2, dk, dv, w_qkv, ptab, given)
    far, dk, dv, back_y = after((far, dk, dv, back_y), g_u, g_d)
    g_d.step()
    far = hops.swap_y((back_y.astype(F32) + far.astype(F32)).astype(BF16))
    back, _, g_small = qkv_back_call(
        tab, (tok, tok_c), 0, dk, dv, w_qkv, ptab, given, (dq, grad_mid)
    )
    back, g_small = after((back, g_small), g_q)
    g_s = summing(g_small[0], g_small[1])
    near = hops.swap_core(back[group:])
    g_s.step(3)
    g_q.step()
    if hops.swaps:
        g_q = Chain(hops.last_sums([jnp.concatenate(p, axis=1) for p in zip(g_q.at, g_s.at)]), 2)
    else:
        g_q = Still(tuple(jnp.concatenate(p, axis=1) for p in zip(g_q.at, g_s.at)))
    g_q.step()
    far, near = after((far, near), g_q)
    input_grad = grad_mid + back[:group].astype(F32) + near.astype(F32) + far.astype(F32)
    g_q, g_u, g_d = g_q.end(), g_u.end(), g_d.end()

    if hops.swaps:

        def rows_of(k):
            down = g_d[:, k * (times // 2) * seg : (k + 1) * (times // 2) * seg]
            part = slice(k * rd, (k + 1) * rd)
            return jnp.concatenate(
                [g_q[part], g_u[part], down[:rd], down[rd:]], axis=1
            )

        mine, other = hops.own_other(rows_of(0), rows_of(1))
        got = hops.swap_core(other.astype(BF16)).astype(F32)
        left, right = hops.sides(mine, got)
        down = [
            under_rows(
                jnp.concatenate([x[:, n_all : n_all + 2 * seg], x[:, n_all + 2 * seg :]], axis=0), 2
            )
            for x in (left, right)
        ]
        grad_down = jnp.concatenate(down, axis=1)
    else:

        def scattered(x):
            return lax.psum_scatter(x, BOTH, scatter_dimension=0, tiled=True)

        left, right = [
            jnp.concatenate(parts, axis=1).astype(F32)
            for parts in zip(*[hops.sides(*g) for g in (g_q, g_u, g_d)])
        ]
        down = [
            x[:, n_all:].reshape(CHIPS, -1, times, seg).transpose(0, 2, 1, 3).reshape(ff, seg)
            for x in (left, right)
        ]
        grad_down = scattered(jnp.concatenate(down, axis=1))
        left, right = scattered(left[:, :n_all]), scattered(right[:, :n_all])

    vecs = left[:, 3 * seg : 3 * seg + 128]
    grad_qkv = jnp.concatenate(
        [x[:, n * seg : (n + 1) * seg] for n in range(3) for x in (left, right)], axis=1
    )
    grad_up = jnp.concatenate([x[:, wide_q : wide_q + n_up] for x in (left, right)], axis=1)
    grad_out = jnp.concatenate([x[:, wide_q + n_up : n_all] for x in (left, right)], axis=1)
    return (
        mixed.reshape(tokens.shape),
        input_grad.astype(BF16).reshape(tokens.shape),
        vecs[:, 0],
        vecs[:, 1],
        grad_qkv,
        vecs[:, 2],
        vecs[:, 3],
        grad_out,
        vecs[:, 4],
        vecs[:, 5],
        vecs[:, 6],
        grad_up,
        vecs[:, 8:12].T.reshape(4 * rd),
        grad_down,
        vecs[:, 7],
        vecs[:, 16 : 16 + FREQS],
    )


def solution(mesh):
    rows = P(BOTH)
    mat = P(BOTH, None)
    act = P("seq", "freq", None)
    in_specs = (
        act, P("seq", "freq"), P("seq", None), act,
        rows, rows, mat, rows, rows, mat, rows, rows, rows, mat, rows, mat, rows, mat,
    )
    out_specs = (
        act, act, rows, rows, mat, rows, rows, mat, rows, rows, rows, mat, rows, mat, rows, mat,
    )
    body = functools.partial(local, n_seq=mesh.shape["seq"], n_freq=mesh.shape["freq"])
    return jax.shard_map(body, mesh=mesh, in_specs=in_specs, out_specs=out_specs, check_vma=False)
```
